32 devices in a mesh: dp: 16 (over z, y, core), tensor: 2 (over x).
Axes of the slice: x: 2, y: 2, z: 4, core: 2. Of those that a mesh axis runs over, the one named last changes fastest.
Arguments:
- tokens: bfloat16 [65536, 768], P('dp'), may hold values from -6 to 6
- out_grad: bfloat16 [65536, 768], P('dp'), may hold values from -6 to 6
- positions: int32 [128, 76], P('dp'), may hold values from 0 to 511, as said below
- w_query: bfloat16 [768, 768], P(None, 'tensor'), may hold values from -0.21875 to 0.21875
- b_query: float32 [768], P('tensor'), may hold values from -3 to 3
- w_key: bfloat16 [768, 768], P(None, 'tensor'), may hold values from -0.21875 to 0.21875
- w_value: bfloat16 [768, 768], P(None, 'tensor'), may hold values from -0.21875 to 0.21875
- b_value: float32 [768], P('tensor'), may hold values from -3 to 3
- w_out: bfloat16 [768, 768], P('tensor'), may hold values from -0.875 to 0.875
- b_out: float32 [768], replicated, may hold values from -3 to 3
- gain_one: float32 [768], replicated, may hold values from 0.25 to 1.75
- shift_one: float32 [768], replicated, may hold values from -3 to 3
- w_up: bfloat16 [768, 3072], P(None, 'tensor'), may hold values from -0.21875 to 0.21875
- b_up: float32 [3072], P('tensor'), may hold values from -3 to 3
- w_down: bfloat16 [3072, 768], P('tensor'), may hold values from -0.109375 to 0.109375
- b_down: float32 [768], replicated, may hold values from -3 to 3
- gain_two: float32 [768], replicated, may hold values from 0.25 to 1.75
- shift_two: float32 [768], replicated, may hold values from -3 to 3
Outputs:
- layer_out: bfloat16 [65536, 768], P('dp')
- tokens_grad: float32 [65536, 768], P('dp')
- grad_w_query: float32 [768, 768], P(None, 'tensor')
- grad_b_query: float32 [768], P('tensor')
- grad_w_key: float32 [768, 768], P(None, 'tensor')
- grad_w_value: float32 [768, 768], P(None, 'tensor')
- grad_b_value: float32 [768], P('tensor')
- grad_w_out: float32 [768, 768], P('tensor')
- grad_b_out: float32 [768], replicated
- grad_gain_one: float32 [768], replicated
- grad_shift_one: float32 [768], replicated
- grad_w_up: float32 [768, 3072], P(None, 'tensor')
- grad_b_up: float32 [3072], P('tensor')
- grad_w_down: float32 [3072, 768], P('tensor')
- grad_b_down: float32 [768], replicated
- grad_gain_two: float32 [768], replicated
- grad_shift_two: float32 [768], replicated
The draws below stay inside these ranges and needn't reach their ends.
Inputs may be any that keep to these rules, and one draw needn't show every extreme that they name: positions may repeat within a sequence, and a position counts once; a sequence has from 1 to 76 distinct positions, and some sequence has exactly 76.
All inputs are finite; a program needn't handle non-finite values.
Results may differ from the reference program's by a relative error of at most 0.024.
Values may be sent and summed in bfloat16 or wider, within the bound.
A program may use at most 256 MiB of HBM per device.

```python
import jax
import jax.numpy as jnp
from jax import lax

D = 768
HEADS = 12
HD = 64
FF = 3072
LEN = 512
SEQ_DEV = 8
PICKS = 76
SEQS = 128
TOKENS = 65536
N_DP = 16
N_TENSOR = 2


def draw_positions(key, part):
    key = jax.random.fold_in(key, 7)
    keys = jax.random.split(key, 6)
    orders = jax.vmap(lambda single: jax.random.permutation(single, LEN))(jax.random.split(keys[0], SEQS))
    candidates = orders[:, :PICKS].astype(jnp.int32)
    heavy = jax.random.randint(keys[1], (SEQS // SEQ_DEV,), 0, 2)
    heavy_rows = jnp.repeat(heavy, SEQ_DEV)
    light_count = jax.random.randint(keys[2], (SEQS,), max(1, PICKS // 4), PICKS // 2 + 1)
    heavy_count = jax.random.randint(keys[3], (SEQS,), max(1, PICKS // 2), PICKS + 1)
    counts = jnp.where(heavy_rows == 1, heavy_count, light_count)
    full_row = jax.random.randint(keys[4], (), 0, SEQS)
    counts = counts.at[full_row].set(PICKS)
    extra = jax.random.randint(keys[5], (SEQS, PICKS), 0, 1048576) % counts[:, None]
    column = jnp.arange(PICKS, dtype=jnp.int32)[None, :]
    index = jnp.where(column < counts[:, None], column, extra).astype(jnp.int32)
    return jnp.take_along_axis(candidates, index, axis=1).astype(jnp.int32)


def block_levels(rng, extent, cuts, smallest, largest):
    gain = 1.0
    for position, blocks in cuts:
        heights = jax.random.uniform(jax.random.fold_in(jax.random.fold_in(rng, 6), position), (blocks,), jnp.float32, smallest / len(cuts), largest / len(cuts))
        gain = gain * jnp.repeat(jnp.exp(heights), extent[position] // blocks).reshape((-1,) + (1,) * (len(extent) - 1 - position))
    return gain


def scatter_about(stream_key, dims, deviation, bound, cuts=(), held_as=jnp.bfloat16):
    loudness = block_levels(stream_key, dims, cuts, -0.22, 0.18) if cuts else 1.0
    entries = jax.random.normal(stream_key, dims, jnp.float32) * deviation * loudness
    return jnp.minimum(jnp.maximum(entries, -bound), bound).astype(held_as)


def setup_inputs(seed: int = 0) -> dict:
    arg_keys = jax.random.split(jax.random.key(seed), 19)
    return {
        "tokens": scatter_about(arg_keys[0], (TOKENS, D), 1.0, 6.0, ((0, 16),)),
        "out_grad": scatter_about(arg_keys[1], (TOKENS, D), 1.0, 6.0, ((0, 16),)),
        "positions": draw_positions(jax.random.fold_in(arg_keys[18], 71), 0),
        "w_query": scatter_about(arg_keys[3], (D, D), D ** -0.5, 0.21875, ((1, 2),)),
        "b_query": scatter_about(arg_keys[4], (D,), 0.5, 3.0, ((0, 2),), jnp.float32),
        "w_key": scatter_about(arg_keys[5], (D, D), D ** -0.5, 0.21875, ((1, 2),)),
        "w_value": scatter_about(arg_keys[6], (D, D), D ** -0.5, 0.21875, ((1, 2),)),
        "b_value": scatter_about(arg_keys[7], (D,), 0.5, 3.0, ((0, 2),), jnp.float32),
        "w_out": scatter_about(arg_keys[8], (D, D), (D // 16) ** -0.5, 0.875, ((0, 2),)),
        "b_out": scatter_about(arg_keys[9], (D,), 0.5, 3.0, (), jnp.float32),
        "gain_one": jnp.clip(1.0 + 0.15 * jax.random.normal(arg_keys[10], (D,), jnp.float32), 0.25, 1.75),
        "shift_one": scatter_about(arg_keys[11], (D,), 0.5, 3.0, (), jnp.float32),
        "w_up": scatter_about(arg_keys[12], (D, FF), D ** -0.5, 0.21875, ((1, 2),)),
        "b_up": scatter_about(arg_keys[13], (FF,), 0.5, 3.0, ((0, 2),), jnp.float32),
        "w_down": scatter_about(arg_keys[14], (FF, D), FF ** -0.5, 0.109375, ((0, 2),)),
        "b_down": scatter_about(arg_keys[15], (D,), 0.5, 3.0, (), jnp.float32),
        "gain_two": jnp.clip(1.0 + 0.15 * jax.random.normal(arg_keys[16], (D,), jnp.float32), 0.25, 1.75),
        "shift_two": scatter_about(arg_keys[17], (D,), 0.5, 3.0, (), jnp.float32),
    }


@jax.custom_vjp
def low(v):
    return lax.optimization_barrier(v.astype(jnp.bfloat16)).astype(jnp.float32)

@jax.custom_vjp
def low_back(v):
    return v

def low_keep(v):
    return (low(v), None)

def low_pass(kept, grad):
    return (grad,)

def back_keep(v):
    return (v, None)

def back_low(kept, grad):
    return (low(grad),)
low.defvjp(low_keep, low_pass)
low_back.defvjp(back_keep, back_low)
HIGHEST_PRECISION = lax.Precision.HIGHEST
NORM_EPSILON = 1e-12

def layer_norm(summed, gain_vector, shift_vector):
    average = lax.optimization_barrier(jnp.mean(summed, axis=-1, keepdims=True))
    centred = summed - average
    spread = lax.optimization_barrier(jnp.mean(centred * centred, axis=-1, keepdims=True))
    return centred * lax.rsqrt(spread + NORM_EPSILON) * gain_vector + shift_vector

def attend_sequence(triple):
    queries, keys_in, values_in = triple
    scores = low_back(jnp.einsum('qhd,khd->hqk', queries, keys_in, precision=HIGHEST_PRECISION) * HD ** (-0.5))
    weights = low(jax.nn.softmax(scores, axis=-1))
    return jnp.einsum('hqk,khd->qhd', weights, values_in, precision=HIGHEST_PRECISION)

def split_columns(matrix):
    return matrix.reshape(matrix.shape[0], N_TENSOR, matrix.shape[1] // N_TENSOR).transpose(1, 0, 2)

def split_rows(matrix):
    return matrix.reshape(N_TENSOR, matrix.shape[0] // N_TENSOR, matrix.shape[1])

def forward(inputs, w_query, b_query, w_key, w_value, b_value, w_out, b_out, gain_one, shift_one, w_up, b_up, w_down, b_down, gain_two, shift_two):
    row_count = inputs.shape[0]
    copies = low_back(jnp.broadcast_to(inputs, (N_TENSOR, row_count, D)))

    def project(matrix):
        return jnp.einsum('trd,tdc->rtc', copies, split_columns(matrix), precision=HIGHEST_PRECISION).reshape(row_count, D)
    queries = low(low_back(project(w_query) + b_query))
    keys_low = low(low_back(project(w_key)))
    values_low = low(low_back(project(w_value) + b_value))

    def by_heads(matrix):
        return matrix.reshape(row_count // LEN, LEN, HEADS, HD)
    attended = lax.map(jax.checkpoint(attend_sequence), (by_heads(queries), by_heads(keys_low), by_heads(values_low)))
    attended_low = low(low_back(attended.reshape(row_count, D)))
    partials = jnp.einsum('rtc,tcd->trd', attended_low.reshape(row_count, N_TENSOR, D // N_TENSOR), split_rows(w_out), precision=HIGHEST_PRECISION)
    layer_one = layer_norm(inputs + lax.optimization_barrier(jnp.sum(low(low_back(partials)), axis=0)) + b_out, gain_one, shift_one)
    spread = low_back(jnp.broadcast_to(low(layer_one), (N_TENSOR, row_count, D)))
    hidden = low_back(jnp.einsum('trd,tdf->rtf', spread, split_columns(w_up), precision=HIGHEST_PRECISION).reshape(row_count, FF) + b_up)
    active = low(jax.nn.gelu(hidden, approximate=False))
    down_parts = jnp.einsum('rtf,tfd->trd', active.reshape(row_count, N_TENSOR, FF // N_TENSOR), split_rows(w_down), precision=HIGHEST_PRECISION)
    second = layer_one + lax.optimization_barrier(jnp.sum(low(low_back(down_parts)), axis=0)) + b_down
    return layer_norm(second, gain_two, shift_two)

def reference(tokens, out_grad, positions, w_query, b_query, w_key, w_value, b_value, w_out, b_out, gain_one, shift_one, w_up, b_up, w_down, b_down, gain_two, shift_two):
    params = (w_query, b_query, w_key, w_value, b_value, w_out, b_out, gain_one, shift_one, w_up, b_up, w_down, b_down, gain_two, shift_two)
    floats = tuple((entry.astype(jnp.float32) for entry in params))
    stacked_in = tokens.astype(jnp.float32).reshape(N_DP, SEQ_DEV * LEN, D)
    stacked_grad = out_grad.astype(jnp.float32).reshape(N_DP, SEQ_DEV * LEN, D)
    stacked_picks = positions.reshape(N_DP, SEQ_DEV, PICKS)
    places = jnp.arange(LEN, dtype=jnp.int32)

    def advance(totals, pieces):
        inputs, cotangent, picked = pieces
        marked = jnp.any(picked[:, :, None] == places[None, None, :], axis=1).astype(jnp.float32)
        cotangent = cotangent * marked.reshape(-1, 1)
        result, pullback = jax.vjp(forward, inputs, *floats)
        gradients = pullback(cotangent)
        totals = tuple((running + fresh for running, fresh in zip(totals, gradients[1:])))
        return (totals, (result.astype(jnp.bfloat16), gradients[0]))
    initial = tuple((jnp.zeros_like(entry) for entry in floats))
    totals, (layer_out, tokens_grad) = lax.scan(advance, initial, (stacked_in, stacked_grad, stacked_picks))
    grad_w_query, grad_b_query, grad_w_key, grad_w_value, grad_b_value, grad_w_out, grad_b_out, grad_gain_one, grad_shift_one, grad_w_up, grad_b_up, grad_w_down, grad_b_down, grad_gain_two, grad_shift_two = totals
    return (layer_out.reshape(TOKENS, D), tokens_grad.reshape(TOKENS, D), grad_w_query, grad_b_query, grad_w_key, grad_w_value, grad_b_value, grad_w_out, grad_b_out, grad_gain_one, grad_shift_one, grad_w_up, grad_b_up, grad_w_down, grad_b_down, grad_gain_two, grad_shift_two)
```

```python
import functools
import math

import jax
import jax.numpy as jnp
from jax import lax
from jax.experimental import pallas as pl
from jax.experimental.pallas import tpu as pltpu
from jax.sharding import PartitionSpec as P

HD = 64
NORM_EPSILON = 1e-12
BF16 = jnp.bfloat16
F32 = jnp.float32
EXPONENT = HD**-0.5 * math.log2(math.e)
ROOT_HALF = 0.7071067811865476
DENSITY = 0.3989422804014327
VMEM_BYTES = 58 * 2**20


def dot(left, right):
    return jnp.dot(left, right, preferred_element_type=F32)


def dot_nt(left, right):
    return lax.dot_general(left, right, (((1,), (1,)), ((), ())), preferred_element_type=F32)


def dot_tn(left, right):
    return lax.dot_general(left, right, (((0,), (0,)), ((), ())), preferred_element_type=F32)


def norm_parts(summed):
    centred = summed - jnp.mean(summed, axis=-1, keepdims=True)
    inverse = lax.rsqrt(jnp.mean(centred * centred, axis=-1, keepdims=True) + NORM_EPSILON)
    return centred * inverse, inverse


def norm_back(upstream, normed, inverse, gain):
    scaled = upstream * gain
    return inverse * (
        scaled
        - jnp.mean(scaled, axis=-1, keepdims=True)
        - normed * jnp.mean(scaled * normed, axis=-1, keepdims=True)
    )


def row_sum(values):
    return jnp.sum(values, axis=0, keepdims=True)


def picker(slots, length):
    return jnp.where(
        slots == lax.broadcasted_iota(jnp.int32, (slots.shape[0], length), 1), 1.0, 0.0
    ).astype(BF16)


def rows_spec(rows, width):
    return pl.BlockSpec((rows, width), lambda i: (i, 0))


def whole_spec(array):
    return pl.BlockSpec(array.shape, lambda i: (0, 0), pipeline_mode=pl.Buffered(1))


def params():
    return pltpu.CompilerParams(vmem_limit_bytes=VMEM_BYTES)


def attention_body(
    tokens, w_qkv, b_query, b_value, slots, attended, keys, values, picked_q, picked_att
):
    length = tokens.shape[0]
    width = keys.shape[1]
    qkv = dot(tokens[...], w_qkv[...])
    query = (qkv[:, :width] + b_query[...]).astype(BF16)
    key = qkv[:, width : 2 * width].astype(BF16)
    value = (qkv[:, 2 * width :] + b_value[...]).astype(BF16)
    keys[...] = key
    values[...] = value
    pair = 2 * HD
    first = lax.broadcasted_iota(jnp.int32, (length, pair), 1) < HD
    zero = jnp.zeros((length, pair), BF16)
    one = jnp.ones((length, pair), BF16)
    for p in range(width // pair):
        here = slice(p * pair, (p + 1) * pair)
        k, v = key[:, here], value[:, here]
        k_two = jnp.concatenate([jnp.where(first, k, zero), jnp.where(first, zero, k)], axis=0)
        v_two = jnp.concatenate(
            [
                jnp.concatenate([jnp.where(first, v, zero), jnp.where(first, one, zero)], axis=1),
                jnp.concatenate([jnp.where(first, zero, v), jnp.where(first, zero, one)], axis=1),
            ],
            axis=0,
        )
        scores = dot_nt(query[:, here], k_two)
        left, right = scores[:, :length], scores[:, length:]
        left = jnp.exp2((left - jnp.max(left, axis=1, keepdims=True)) * EXPONENT).astype(BF16)
        right = jnp.exp2((right - jnp.max(right, axis=1, keepdims=True)) * EXPONENT).astype(BF16)
        both = dot(jnp.concatenate([left, right], axis=1), v_two)
        attended[:, here] = (both[:, :pair] / both[:, pair:]).astype(BF16)
    pick = picker(slots[...], length)
    picked_q[...] = dot(pick, query).astype(BF16)
    picked_att[...] = dot(pick, attended[...]).astype(BF16)


def attention(tokens, w_qkv, b_query, b_value, slots, sequences):
    rows, model = tokens.shape
    length = rows // sequences
    width = w_qkv.shape[1] // 3
    taken = slots.shape[0] // sequences
    shape = jax.ShapeDtypeStruct
    return pl.pallas_call(
        attention_body,
        grid=(sequences,),
        in_specs=[
            rows_spec(length, model),
            whole_spec(w_qkv),
            whole_spec(b_query),
            whole_spec(b_value),
            rows_spec(taken, 1),
        ],
        out_specs=[rows_spec(length, width)] * 3 + [rows_spec(taken, width)] * 2,
        out_shape=[shape((rows, width), BF16)] * 3 + [shape((slots.shape[0], width), BF16)] * 2,
        compiler_params=params(),
        cost_estimate=pl.CostEstimate(
            flops=int(rows * width * (6 * model + 16 * length)),
            bytes_accessed=rows * (model + 3 * width) * 2,
            transcendentals=rows * length * width // HD,
        ),
        name="attention",
    )(tokens, w_qkv, b_query, b_value, slots)


def pick_body(tokens, out_grad, slots, picked_tokens, picked_grad):
    pick = picker(slots[...], tokens.shape[0])
    picked_tokens[...] = dot(pick, tokens[...]).astype(BF16)
    picked_grad[...] = dot(pick, out_grad[...]).astype(BF16)


def pick_rows(tokens, out_grad, slots, sequences):
    rows, model = tokens.shape
    length = rows // sequences
    taken = slots.shape[0] // sequences
    return pl.pallas_call(
        pick_body,
        grid=(sequences,),
        in_specs=[rows_spec(length, model)] * 2 + [rows_spec(taken, 1)],
        out_specs=[rows_spec(taken, model)] * 2,
        out_shape=[jax.ShapeDtypeStruct((slots.shape[0], model), BF16)] * 2,
        compiler_params=params(),
        name="pick",
    )(tokens, out_grad, slots)


def gelu_share(hidden):
    return 0.5 * (1.0 + lax.erf(hidden * ROOT_HALF))


def marked_body(
    tokens,
    attended_own,
    attended_peer,
    upstream,
    w_out,
    w_up_own,
    w_up_peer,
    w_down_own,
    w_down_peer,
    b_out,
    gain_one,
    shift_one,
    b_up_own,
    b_up_peer,
    b_down,
    gain_two,
    back_one_out,
    attended_grad_own,
    attended_grad_peer,
    grad_w_up,
    grad_w_down,
    grad_w_out,
    grad_b_up,
    vectors,
    slope,
    active,
):
    width = attended_own.shape[1]
    half = w_up_own.shape[1]
    chunk = half
    attended = jnp.concatenate([attended_own[...], attended_peer[...]], axis=1)
    normed_one, inverse_one = norm_parts(
        tokens[...].astype(F32) + dot(attended, w_out[...]) + b_out[...]
    )
    layer_one = normed_one * gain_one[...] + shift_one[...]
    layer_low = layer_one.astype(BF16)
    summed = layer_one + b_down[...]
    parts = (
        (0, w_up_own, w_down_own, b_up_own),
        (half, w_up_peer, w_down_peer, b_up_peer),
    )
    for start, w_up, w_down, b_up in parts:
        for c in range(0, half, chunk):
            here = slice(c, c + chunk)
            hidden = dot(layer_low, w_up[:, here]) + b_up[:, here]
            share = gelu_share(hidden)
            act = (hidden * share).astype(BF16)
            slope[:, start + c : start + c + chunk] = (
                share + hidden * jnp.exp(-0.5 * hidden * hidden) * DENSITY
            )
            if start == 0:
                active[:, here] = act
            summed = summed + dot(act, w_down[here, :])
    normed_two, inverse_two = norm_parts(summed)
    up = upstream[...].astype(F32)
    back_two = norm_back(up, normed_two, inverse_two, gain_two[...])
    back_low = back_two.astype(BF16)
    layer_grad = back_two
    for start, w_up, w_down, b_up in parts:
        for c in range(0, half, chunk):
            here = slice(c, c + chunk)
            hidden_grad = (
                dot_nt(back_low, w_down[here, :]) * slope[:, start + c : start + c + chunk]
            ).astype(BF16)
            layer_grad = layer_grad + dot_nt(hidden_grad, w_up[:, here])
            if start == 0:
                grad_b_up[:, here] = row_sum(hidden_grad.astype(F32))
                grad_w_up[:, here] = dot_tn(layer_low, hidden_grad).astype(BF16)
                grad_w_down[here, :] = dot_tn(active[:, here], back_low).astype(BF16)
    back_one = norm_back(layer_grad, normed_one, inverse_one, gain_one[...])
    back_one_low = back_one.astype(BF16)
    back_one_out[...] = back_one
    grad_w_out[...] = dot_tn(attended_own[...], back_one_low).astype(BF16)
    attended_grad = dot_nt(back_one_low, w_out[...]).astype(BF16)
    attended_grad_own[...] = attended_grad[:, :width]
    attended_grad_peer[...] = attended_grad[:, width:]
    vectors[...] = jnp.concatenate(
        [
            row_sum(back_one),
            row_sum(layer_grad * normed_one),
            row_sum(layer_grad),
            row_sum(back_two),
            row_sum(up * normed_two),
            row_sum(up),
            jnp.zeros((2, up.shape[1]), F32),
        ],
        axis=0,
    )


def marked_rows(*args):
    tokens, attended_own = args[0], args[1]
    rows, model = tokens.shape
    width = attended_own.shape[1]
    half = args[5].shape[1]
    shape = jax.ShapeDtypeStruct
    return pl.pallas_call(
        marked_body,
        out_shape=[
            shape((rows, model), F32),
            shape((rows, width), BF16),
            shape((rows, width), BF16),
            shape((model, half), BF16),
            shape((half, model), BF16),
            shape((width, model), BF16),
            shape((1, half), F32),
            shape((8, model), F32),
        ],
        scratch_shapes=[pltpu.VMEM((rows, 2 * half), F32), pltpu.VMEM((rows, half), BF16)],
        compiler_params=params(),
        cost_estimate=pl.CostEstimate(
            flops=int(rows * model * (2 * half * 10 + 2 * width * 5)),
            bytes_accessed=6 * model * half * 2,
            transcendentals=rows * half * 4,
        ),
        name="marked",
    )(*args)


def backward_body(
    tokens,
    keys_own,
    keys_peer,
    values_own,
    values_peer,
    query_own,
    query_peer,
    grad_own,
    grad_peer,
    back_one,
    slots,
    picked_tokens,
    w_query,
    w_key_value,
    tokens_grad,
    grad_w_query,
    grad_w_key_value,
    grad_b_query,
    grad_b_value,
    query_grads,
    sums,
):
    step = pl.program_id(0)
    last = pl.num_programs(0) - 1
    length = tokens.shape[0]
    width = keys_own.shape[1]
    taken = slots.shape[0]
    factor = HD**-0.5
    pair = 2 * HD
    first = lax.broadcasted_iota(jnp.int32, (taken, pair), 1) < HD
    zero = jnp.zeros((taken, pair), BF16)

    def stacked(block):
        return jnp.concatenate(
            [jnp.where(first, block, zero), jnp.where(first, zero, block)], axis=0
        )

    d_query, d_key, d_value = [], [], []
    for keys, values, query, grad in (
        (keys_own, values_own, query_own, grad_own),
        (keys_peer, values_peer, query_peer, grad_peer),
    ):
        for p in range(width // pair):
            here = slice(p * pair, (p + 1) * pair)
            k, v = keys[:, here], values[:, here]
            q, g = stacked(query[:, here]), stacked(grad[:, here])
            scores = dot_nt(q, k)
            grown = jnp.exp2((scores - jnp.max(scores, axis=1, keepdims=True)) * EXPONENT)
            weights = grown / jnp.sum(grown, axis=1, keepdims=True)
            weights_grad = dot_nt(g, v)
            inner = jnp.sum(weights * weights_grad, axis=1, keepdims=True)
            scores_grad = (weights * (weights_grad - inner)).astype(BF16)
            d_value.append(dot_tn(weights.astype(BF16), g).astype(BF16))
            d_key.append((dot_tn(scores_grad, q) * factor).astype(BF16))
            split = dot(scores_grad, k) * factor
            d_query.append(jnp.where(first, split[:taken], split[taken:]).astype(BF16))
    half = len(d_key) // 2
    own = jnp.concatenate(d_key[:half] + d_value[:half], axis=1)
    mixed = jnp.concatenate([own] + d_key[half:] + d_value[half:], axis=1)
    query_part = jnp.concatenate(d_query, axis=1)
    query_own_part = query_part[:, :width]
    extra = back_one[...] + dot_nt(query_part, w_query[...])
    high = extra.astype(BF16)
    low = (extra - high.astype(F32)).astype(BF16)
    pick = picker(slots[...], length)
    tokens_grad[...] = dot_nt(mixed, w_key_value[...]) + dot_tn(
        jnp.concatenate([pick, pick], axis=0), jnp.concatenate([high, low], axis=0)
    )
    query_grads[pl.ds(pl.multiple_of(step * taken, taken), taken), :] = query_own_part
    update = dot_tn(tokens[...], own)
    query_sum = row_sum(query_own_part.astype(F32))
    value_sum = row_sum(own[:, width:].astype(F32))

    @pl.when(step == 0)
    def _():
        sums[...] = update
        grad_b_query[...] = query_sum
        grad_b_value[...] = value_sum

    @pl.when(step > 0)
    def _():
        sums[...] += update
        grad_b_query[...] += query_sum
        grad_b_value[...] += value_sum

    @pl.when(step == last)
    def _():
        grad_w_key_value[...] = sums[...].astype(BF16)
        grad_w_query[...] = dot_tn(picked_tokens[...], query_grads[...]).astype(BF16)


def attention_back(
    tokens, keys, values, query, grad, back_one, slots, picked_tokens, w_query, w_key_value, sequences
):
    rows, model = tokens.shape
    length = rows // sequences
    width = keys[0].shape[1]
    taken = slots.shape[0] // sequences
    shape = jax.ShapeDtypeStruct
    return pl.pallas_call(
        backward_body,
        grid=(sequences,),
        in_specs=[rows_spec(length, model)]
        + [rows_spec(length, width)] * 4
        + [rows_spec(taken, width)] * 4
        + [rows_spec(taken, model), rows_spec(taken, 1)]
        + [whole_spec(picked_tokens), whole_spec(w_query), whole_spec(w_key_value)],
        out_specs=[
            rows_spec(length, model),
            pl.BlockSpec((model, width), lambda i: (0, 0)),
            pl.BlockSpec((model, 2 * width), lambda i: (0, 0)),
            pl.BlockSpec((1, width), lambda i: (0, 0)),
            pl.BlockSpec((1, width), lambda i: (0, 0)),
        ],
        out_shape=[
            shape((rows, model), F32),
            shape((model, width), BF16),
            shape((model, 2 * width), BF16),
            shape((1, width), F32),
            shape((1, width), F32),
        ],
        scratch_shapes=[
            pltpu.VMEM((slots.shape[0], width), BF16),
            pltpu.VMEM((model, 2 * width), F32),
        ],
        compiler_params=params(),
        cost_estimate=pl.CostEstimate(
            flops=int(rows * model * 6 * 2 * width),
            bytes_accessed=rows * model * 14,
            transcendentals=0,
        ),
        name="attention_back",
    )(
        tokens,
        keys[0],
        keys[1],
        values[0],
        values[1],
        query[0],
        query[1],
        grad[0],
        grad[1],
        back_one,
        slots,
        picked_tokens,
        w_query,
        w_key_value,
    )


def dense_body(
    tokens,
    attended_own,
    attended_peer,
    w_out,
    w_up_own,
    w_up_peer,
    w_down_own,
    w_down_peer,
    b_out,
    gain_one,
    shift_one,
    b_up_own,
    b_up_peer,
    b_down,
    gain_two,
    shift_two,
    layer_out,
):
    attended = jnp.concatenate([attended_own[...], attended_peer[...]], axis=1)
    normed, _ = norm_parts(tokens[...].astype(F32) + dot(attended, w_out[...]) + b_out[...])
    layer_one = normed * gain_one[...] + shift_one[...]
    layer_low = layer_one.astype(BF16)
    summed = layer_one + b_down[...]
    for w_up, w_down, b_up in (
        (w_up_own, w_down_own, b_up_own),
        (w_up_peer, w_down_peer, b_up_peer),
    ):
        hidden = dot(layer_low, w_up[...]) + b_up[...]
        summed = summed + dot((hidden * gelu_share(hidden)).astype(BF16), w_down[...])
    normed, _ = norm_parts(summed)
    layer_out[...] = (normed * gain_two[...] + shift_two[...]).astype(BF16)


def dense_rows(*args):
    tokens, attended_own = args[0], args[1]
    rows, model = tokens.shape
    width = attended_own.shape[1]
    half = args[4].shape[1]
    block = 512
    return pl.pallas_call(
        dense_body,
        grid=(rows // block,),
        in_specs=[rows_spec(block, model), rows_spec(block, width), rows_spec(block, width)]
        + [whole_spec(array) for array in args[3:]],
        out_specs=rows_spec(block, model),
        out_shape=jax.ShapeDtypeStruct((rows, model), BF16),
        compiler_params=params(),
        cost_estimate=pl.CostEstimate(
            flops=int(rows * model * (8 * half + 4 * width)),
            bytes_accessed=rows * model * 6,
            transcendentals=rows * half * 2,
        ),
        name="dense",
    )(*args)


def on_device(
    tokens,
    out_grad,
    positions,
    w_query,
    b_query,
    w_key,
    w_value,
    b_value,
    w_out,
    b_out,
    gain_one,
    shift_one,
    w_up,
    b_up,
    w_down,
    b_down,
    gain_two,
    shift_two,
):
    sequences, picks = positions.shape
    model = tokens.shape[1]
    width = w_query.shape[1]
    half = w_up.shape[1]

    def peer(array):
        return lax.ppermute(array, "tensor", [(0, 1), (1, 0)])

    def row(vector):
        return vector.reshape(1, -1)

    earlier = jnp.tril(jnp.ones((picks, picks), jnp.bool_), -1)
    repeated = jnp.any((positions[:, :, None] == positions[:, None, :]) & earlier, axis=2)
    taken = -(-picks // 16) * 16
    slots = jnp.pad(
        jnp.where(repeated, -1, positions), ((0, 0), (0, taken - picks)), constant_values=-1
    ).reshape(-1, 1)

    qkv_own = jnp.concatenate([w_query, w_key, w_value], axis=1)
    qkv_peer = peer(qkv_own)
    biases_own = jnp.concatenate([b_query, b_value, b_up])
    biases_peer = peer(biases_own)
    out_peer = peer(w_out)
    up_peer = peer(w_up)
    down_peer = peer(w_down)
    b_up_peer = row(biases_peer[2 * width :])

    att_own, key_own, value_own, pick_q_own, pick_att_own = attention(
        tokens, qkv_own, row(b_query), row(b_value), slots, sequences
    )
    att_peer, key_peer, value_peer, pick_q_peer, pick_att_peer = attention(
        tokens,
        qkv_peer,
        row(biases_peer[:width]),
        row(biases_peer[width : 2 * width]),
        slots,
        sequences,
    )
    picked_tokens, picked_grad = pick_rows(tokens, out_grad, slots, sequences)
    out_all = jnp.concatenate([w_out, out_peer], axis=0)
    shared = (
        out_all,
        w_up,
        up_peer,
        w_down,
        down_peer,
        row(b_out),
        row(gain_one),
        row(shift_one),
        row(b_up),
        b_up_peer,
        row(b_down),
        row(gain_two),
    )
    (
        back_one,
        att_grad_own,
        att_grad_peer,
        grad_w_up,
        grad_w_down,
        grad_w_out,
        grad_b_up,
        vectors,
    ) = marked_rows(picked_tokens, pick_att_own, pick_att_peer, picked_grad, *shared)
    w_query_all = jnp.concatenate([w_query, qkv_peer[:, :width]], axis=1)
    w_key_value = jnp.concatenate([w_key, w_value, qkv_peer[:, width:]], axis=1)
    tokens_grad, grad_w_query, grad_w_key_value, grad_b_query, grad_b_value = attention_back(
        tokens,
        (key_own, key_peer),
        (value_own, value_peer),
        (pick_q_own, pick_q_peer),
        (att_grad_own, att_grad_peer),
        back_one,
        slots,
        picked_tokens,
        w_query_all,
        w_key_value,
        sequences,
    )
    layer_out = dense_rows(tokens, att_own, att_peer, *shared, row(shift_two))

    grad_w_up, grad_w_down, grad_w_out, grad_w_query, grad_w_key_value = lax.psum(
        (grad_w_up, grad_w_down, grad_w_out, grad_w_query, grad_w_key_value), "dp"
    )
    vectors, grad_b_up, grad_b_query, grad_b_value = lax.psum(
        (vectors, grad_b_up, grad_b_query, grad_b_value), "dp"
    )
    return (
        layer_out,
        tokens_grad,
        grad_w_query.astype(F32),
        grad_b_query[0],
        grad_w_key_value[:, :width].astype(F32),
        grad_w_key_value[:, width:].astype(F32),
        grad_b_value[0],
        grad_w_out.astype(F32),
        vectors[0],
        vectors[1],
        vectors[2],
        grad_w_up.astype(F32),
        grad_b_up[0],
        grad_w_down.astype(F32),
        vectors[3],
        vectors[4],
        vectors[5],
    )


def solution(mesh):
    across = P("dp", None)
    columns, rows, split, copied = P(None, "tensor"), P("tensor", None), P("tensor"), P()
    in_specs = (
        across,
        across,
        across,
        columns,
        split,
        columns,
        columns,
        split,
        rows,
        copied,
        copied,
        copied,
        columns,
        split,
        rows,
        copied,
        copied,
        copied,
    )
    out_specs = (
        across,
        across,
        columns,
        split,
        columns,
        columns,
        split,
        rows,
        copied,
        copied,
        copied,
        columns,
        split,
        rows,
        copied,
        copied,
        copied,
    )
    return jax.shard_map(
        on_device, mesh=mesh, in_specs=in_specs, out_specs=out_specs, check_vma=False
    )
```

```python
import functools
import math

import jax
import jax.numpy as jnp
from jax import lax
from jax.experimental import pallas as pl
from jax.experimental.pallas import tpu as pltpu
from jax.sharding import PartitionSpec as P

HD = 64
NORM_EPSILON = 1e-12
BF16 = jnp.bfloat16
F32 = jnp.float32
EXPONENT = HD**-0.5 * math.log2(math.e)
ROOT_HALF = 0.7071067811865476
DENSITY = 0.3989422804014327
VMEM_BYTES = 58 * 2**20


def dot(left, right):
    return jnp.dot(left, right, preferred_element_type=F32)


def dot_nt(left, right):
    return lax.dot_general(left, right, (((1,), (1,)), ((), ())), preferred_element_type=F32)


def dot_tn(left, right):
    return lax.dot_general(left, right, (((0,), (0,)), ((), ())), preferred_element_type=F32)


def norm_parts(summed):
    centred = summed - jnp.mean(summed, axis=-1, keepdims=True)
    inverse = lax.rsqrt(jnp.mean(centred * centred, axis=-1, keepdims=True) + NORM_EPSILON)
    return centred * inverse, inverse


def norm_back(upstream, normed, inverse, gain):
    scaled = upstream * gain
    return inverse * (
        scaled
        - jnp.mean(scaled, axis=-1, keepdims=True)
        - normed * jnp.mean(scaled * normed, axis=-1, keepdims=True)
    )


def row_sum(values):
    return jnp.sum(values, axis=0, keepdims=True)


def rows_spec(rows, width):
    return pl.BlockSpec((rows, width), lambda i: (i, 0))


def whole_spec(array):
    return pl.BlockSpec(array.shape, lambda i: (0, 0), pipeline_mode=pl.Buffered(1))


def params():
    return pltpu.CompilerParams(vmem_limit_bytes=VMEM_BYTES)


def flipped(index, span):
    return index + span - 2 * span * ((index // span) % 2)


def attention_body(
    tokens,
    out_grad,
    positions,
    w_query,
    w_key,
    w_value,
    w_out,
    w_up,
    w_down,
    b_query,
    b_value,
    b_up,
    attended,
    keys,
    values,
    picked_q,
    picked_att,
    picked_tokens,
    picked_grad,
    picks,
    qkv_all,
    out_all,
    up_peer,
    down_peer,
    b_up_peer,
    qkv,
    biases,
    kept_picks,
    local_sems,
    send_sems,
    recv_sems,
    bias_sems,
):
    step = pl.program_id(0)
    sequences = pl.num_programs(0) // 2
    turn = step // sequences
    length = tokens.shape[0]
    width = keys.shape[1]
    dp = lax.axis_index("dp")
    across = {"tensor": 1 - lax.axis_index("tensor")}
    beside = {"dp": flipped(dp, 2)}
    close = {"dp": flipped(dp, 1)}
    mine = dp % 4

    arrays = (
        (qkv.at[0], qkv.at[1]),
        (w_out, out_all.at[pl.ds(width, width)]),
        (w_up, up_peer),
        (w_down, down_peer),
    )

    def rows_of(ref, piece):
        count = ref.shape[0] // 4
        return ref.at[pl.ds(pl.multiple_of(piece * count, count), count)]

    def hop(index, kind):
        source, target = arrays[index]
        piece = (mine, mine, mine, flipped(mine, 2))[kind]
        device = (across, beside, close, close)[kind]
        return pltpu.make_async_remote_copy(
            src_ref=rows_of(source if kind == 0 else target, piece),
            dst_ref=rows_of(target, piece),
            send_sem=send_sems.at[index, kind],
            recv_sem=recv_sems.at[index, kind],
            device_id=device,
            device_id_type=pl.DeviceIdType.MESH,
        )

    def arrival(index, kind):
        _, target = arrays[index]
        piece = (mine, flipped(mine, 2), flipped(mine, 1), flipped(flipped(mine, 2), 1))[kind]
        device = (across, beside, close, close)[kind]
        here = rows_of(target, piece)
        return pltpu.make_async_remote_copy(
            src_ref=here,
            dst_ref=here,
            send_sem=send_sems.at[index, kind],
            recv_sem=recv_sems.at[index, kind],
            device_id=device,
            device_id_type=pl.DeviceIdType.MESH,
        )

    bias_pairs = (
        (biases.at[0], biases.at[1]),
        (biases.at[2], biases.at[3]),
        (b_up, b_up_peer),
    )

    def bias_copy(index):
        source, target = bias_pairs[index]
        return pltpu.make_async_remote_copy(
            src_ref=source,
            dst_ref=target,
            send_sem=bias_sems.at[0, index],
            recv_sem=bias_sems.at[1, index],
            device_id=across,
            device_id_type=pl.DeviceIdType.MESH,
        )

    loads = (
        pltpu.make_async_copy(w_query, qkv.at[0, :, pl.ds(0, width)], local_sems.at[0]),
        pltpu.make_async_copy(w_key, qkv.at[0, :, pl.ds(width, width)], local_sems.at[1]),
        pltpu.make_async_copy(w_value, qkv.at[0, :, pl.ds(2 * width, width)], local_sems.at[2]),
        pltpu.make_async_copy(b_query, biases.at[0], local_sems.at[3]),
        pltpu.make_async_copy(b_value, biases.at[2], local_sems.at[4]),
    )
    keep_out = pltpu.make_async_copy(w_out, out_all.at[pl.ds(0, width)], local_sems.at[5])
    keep_qkv = pltpu.make_async_copy(qkv, qkv_all, local_sems.at[6])

    @pl.when(step == 0)
    def _():
        for load in loads:
            load.start()
        keep_out.start()
        barrier = pltpu.get_barrier_semaphore()
        for device in (across, beside, close):
            pl.semaphore_signal(
                barrier, inc=1, device_id=device, device_id_type=pl.DeviceIdType.MESH
            )
        for load in loads:
            load.wait()
        pl.semaphore_wait(barrier, 3)
        hop(0, 0).start()
        for index in range(3):
            bias_copy(index).start()

    @pl.when(step == 3)
    def _():
        arrival(0, 0).wait_recv()
        hop(0, 1).start()
        hop(0, 2).start()
        hop(1, 0).start()
        hop(2, 0).start()

    @pl.when(step == sequences - 2)
    def _():
        arrival(0, 1).wait_recv()
        hop(0, 3).start()

    @pl.when(step == sequences - 1)
    def _():
        for index in (1, 2):
            arrival(index, 0).wait_recv()
            hop(index, 1).start()
            hop(index, 2).start()
        hop(3, 0).start()

    @pl.when(step == sequences)
    def _():
        arrival(0, 2).wait_recv()
        arrival(0, 3).wait_recv()
        bias_copy(0).wait_recv()
        bias_copy(1).wait_recv()
        keep_qkv.start()

    @pl.when(step == sequences + 3)
    def _():
        arrival(3, 0).wait_recv()
        hop(3, 1).start()
        hop(3, 2).start()

    @pl.when(step == sequences + 4)
    def _():
        for index in (1, 2):
            arrival(index, 1).wait_recv()
            hop(index, 3).start()

    tokens_here = tokens[...]
    projected = dot(tokens_here, qkv[turn])
    query = (projected[:, :width] + biases[turn]).astype(BF16)
    key = projected[:, width : 2 * width].astype(BF16)
    value = (projected[:, 2 * width :] + biases[2 + turn]).astype(BF16)
    keys[...] = key
    values[...] = value
    pair = 2 * HD
    first = lax.broadcasted_iota(jnp.int32, (length, pair), 1) < HD
    zero = jnp.zeros((length, pair), BF16)
    one = jnp.ones((length, pair), BF16)
    for p in range(width // pair):
        here = slice(p * pair, (p + 1) * pair)
        k, v = key[:, here], value[:, here]
        k_two = jnp.concatenate([jnp.where(first, k, zero), jnp.where(first, zero, k)], axis=0)
        v_two = jnp.concatenate(
            [
                jnp.concatenate([jnp.where(first, v, zero), jnp.where(first, one, zero)], axis=1),
                jnp.concatenate([jnp.where(first, zero, v), jnp.where(first, zero, one)], axis=1),
            ],
            axis=0,
        )
        scores = dot_nt(query[:, here], k_two)
        left, right = scores[:, :length], scores[:, length:]
        left = jnp.exp2((left - jnp.max(left, axis=1, keepdims=True)) * EXPONENT).astype(BF16)
        right = jnp.exp2((right - jnp.max(right, axis=1, keepdims=True)) * EXPONENT).astype(BF16)
        both = dot(jnp.concatenate([left, right], axis=1), v_two)
        attended[:, here] = (both[:, :pair] / both[:, pair:]).astype(BF16)

    taken = picks.shape[0]
    sequence = step % sequences

    @pl.when(turn == 0)
    def _():
        spread = jnp.broadcast_to(
            positions[pl.ds(sequence, 1), :], (length, positions.shape[1])
        )
        column = lax.broadcasted_iota(jnp.int32, spread.shape, 1).astype(F32)
        hit = spread == lax.broadcasted_iota(jnp.int32, spread.shape, 0)
        earliest = jnp.min(jnp.where(hit, column, 1e6), axis=1, keepdims=True)
        fresh = jnp.where(column == earliest, 1.0, 0.0).T[:taken].astype(BF16)
        picks[...] = fresh
        kept_picks[sequence] = fresh
        picked_tokens[...] = dot(fresh, tokens_here).astype(BF16)
        picked_grad[...] = dot(fresh, out_grad[...]).astype(BF16)

    pick = kept_picks[sequence]
    picked_q[...] = dot(pick, query).astype(BF16)
    picked_att[...] = dot(pick, attended[...]).astype(BF16)

    @pl.when(step == 2 * sequences - 1)
    def _():
        arrival(3, 1).wait_recv()
        hop(3, 3).start()
        for index in (1, 2, 3):
            arrival(index, 2).wait_recv()
            arrival(index, 3).wait_recv()
        bias_copy(2).wait_recv()
        for index in range(4):
            for kind in range(4):
                hop(index, kind).wait_send()
        for index in range(3):
            bias_copy(index).wait_send()
        keep_out.wait()
        keep_qkv.wait()


def attention(
    tokens, out_grad, positions, w_query, w_key, w_value, w_out, w_up, w_down, b_query, b_value, b_up, taken
):
    rows, model = tokens.shape
    sequences = positions.shape[0]
    length = rows // sequences
    width = w_query.shape[1]
    shape = jax.ShapeDtypeStruct
    slots = sequences * taken

    def both(count, columns):
        return pl.BlockSpec((count, columns), lambda s: (s % sequences, s // sequences))

    def once(count, columns):
        return pl.BlockSpec((count, columns), lambda s: (jnp.minimum(s, sequences - 1), 0))

    def again(count, columns):
        return pl.BlockSpec((count, columns), lambda s: (s % sequences, 0))

    anywhere = pl.BlockSpec(memory_space=pl.ANY)
    return pl.pallas_call(
        attention_body,
        grid=(2 * sequences,),
        in_specs=[
            again(length, model),
            once(length, model),
            pl.BlockSpec(positions.shape, lambda s: (0, 0)),
        ]
        + [anywhere] * 9,
        out_specs=[
            both(length, width),
            both(length, width),
            both(length, width),
            both(taken, width),
            both(taken, width),
            once(taken, model),
            once(taken, model),
            once(taken, length),
        ]
        + [anywhere] * 5,
        out_shape=[
            shape((rows, 2 * width), BF16),
            shape((rows, 2 * width), BF16),
            shape((rows, 2 * width), BF16),
            shape((slots, 2 * width), BF16),
            shape((slots, 2 * width), BF16),
            shape((slots, model), BF16),
            shape((slots, model), BF16),
            shape((slots, length), BF16),
            shape((2, model, 3 * width), BF16),
            shape((2 * width, model), BF16),
            shape(w_up.shape, BF16),
            shape(w_down.shape, BF16),
            shape(b_up.shape, F32),
        ],
        scratch_shapes=[
            pltpu.VMEM((2, model, 3 * width), BF16),
            pltpu.VMEM((4, 1, width), F32),
            pltpu.VMEM((sequences, taken, length), BF16),
            pltpu.SemaphoreType.DMA((7,)),
            pltpu.SemaphoreType.DMA((4, 4)),
            pltpu.SemaphoreType.DMA((4, 4)),
            pltpu.SemaphoreType.DMA((2, 3)),
        ],
        compiler_params=pltpu.CompilerParams(
            vmem_limit_bytes=VMEM_BYTES, collective_id=0, has_side_effects=True
        ),
        cost_estimate=pl.CostEstimate(
            flops=int(2 * rows * width * (6 * model + 16 * length)),
            bytes_accessed=rows * model * 12,
            transcendentals=rows * length * width // HD,
        ),
        name="attention",
    )(tokens, out_grad, positions, w_query, w_key, w_value, w_out, w_up, w_down, b_query, b_value, b_up)


def gelu_share(hidden):
    return 0.5 * (1.0 + lax.erf(hidden * ROOT_HALF))


def marked_body(
    tokens,
    attended,
    upstream,
    w_out,
    w_up_own,
    w_up_peer,
    w_down_own,
    w_down_peer,
    b_out,
    gain_one,
    shift_one,
    b_up_own,
    b_up_peer,
    b_down,
    gain_two,
    back_one_out,
    attended_grad,
    grad_w_up,
    grad_w_down,
    grad_w_out,
    grad_b_up,
    vectors,
    slope,
    active,
):
    width = attended.shape[1] // 2
    half = w_up_own.shape[1]
    chunk = half
    normed_one, inverse_one = norm_parts(
        tokens[...].astype(F32) + dot(attended[...], w_out[...]) + b_out[...]
    )
    layer_one = normed_one * gain_one[...] + shift_one[...]
    layer_low = layer_one.astype(BF16)
    summed = layer_one + b_down[...]
    parts = (
        (0, w_up_own, w_down_own, b_up_own),
        (half, w_up_peer, w_down_peer, b_up_peer),
    )
    for start, w_up, w_down, b_up in parts:
        for c in range(0, half, chunk):
            here = slice(c, c + chunk)
            hidden = dot(layer_low, w_up[:, here]) + b_up[:, here]
            share = gelu_share(hidden)
            act = (hidden * share).astype(BF16)
            slope[:, start + c : start + c + chunk] = (
                share + hidden * jnp.exp(-0.5 * hidden * hidden) * DENSITY
            )
            if start == 0:
                active[:, here] = act
            summed = summed + dot(act, w_down[here, :])
    normed_two, inverse_two = norm_parts(summed)
    up = upstream[...].astype(F32)
    back_two = norm_back(up, normed_two, inverse_two, gain_two[...])
    back_low = back_two.astype(BF16)
    layer_grad = back_two
    for start, w_up, w_down, b_up in parts:
        for c in range(0, half, chunk):
            here = slice(c, c + chunk)
            hidden_grad = (
                dot_nt(back_low, w_down[here, :]) * slope[:, start + c : start + c + chunk]
            ).astype(BF16)
            layer_grad = layer_grad + dot_nt(hidden_grad, w_up[:, here])
            if start == 0:
                grad_b_up[:, here] = row_sum(hidden_grad.astype(F32))
                grad_w_up[:, here] = dot_tn(layer_low, hidden_grad).astype(BF16)
                grad_w_down[here, :] = dot_tn(active[:, here], back_low).astype(BF16)
    back_one = norm_back(layer_grad, normed_one, inverse_one, gain_one[...])
    back_one_low = back_one.astype(BF16)
    back_one_out[...] = back_one
    grad_w_out[...] = dot_tn(attended[:, :width], back_one_low).astype(BF16)
    attended_grad[...] = dot_nt(back_one_low, w_out[...]).astype(BF16)
    vectors[...] = jnp.concatenate(
        [
            row_sum(back_one),
            row_sum(layer_grad * normed_one),
            row_sum(layer_grad),
            row_sum(back_two),
            row_sum(up * normed_two),
            row_sum(up),
            jnp.zeros((2, up.shape[1]), F32),
        ],
        axis=0,
    )


def marked_rows(*args):
    tokens, attended = args[0], args[1]
    rows, model = tokens.shape
    width = attended.shape[1] // 2
    half = args[4].shape[1]
    shape = jax.ShapeDtypeStruct
    return pl.pallas_call(
        marked_body,
        out_shape=[
            shape((rows, model), F32),
            shape((rows, 2 * width), BF16),
            shape((model, half), BF16),
            shape((half, model), BF16),
            shape((width, model), BF16),
            shape((1, half), F32),
            shape((8, model), F32),
        ],
        scratch_shapes=[pltpu.VMEM((rows, 2 * half), F32), pltpu.VMEM((rows, half), BF16)],
        compiler_params=params(),
        cost_estimate=pl.CostEstimate(
            flops=int(rows * model * (2 * half * 10 + 2 * width * 5)),
            bytes_accessed=6 * model * half * 2,
            transcendentals=rows * half * 4,
        ),
        name="marked",
    )(*args)


def backward_body(
    tokens,
    keys,
    values,
    queries,
    grads,
    back_one,
    picks,
    picked_tokens,
    qkv_all,
    tokens_grad,
    grad_w_query,
    grad_w_key_value,
    grad_b_query,
    grad_b_value,
    query_grads,
    sums,
):
    step = pl.program_id(0)
    last = pl.num_programs(0) - 1
    width = keys.shape[1] // 2
    taken = picks.shape[0]
    factor = HD**-0.5
    pair = 2 * HD

    @pl.when(step == 0)
    def _():
        sums[...] = jnp.zeros_like(sums)
        grad_b_query[...] = jnp.zeros_like(grad_b_query)
        grad_b_value[...] = jnp.zeros_like(grad_b_value)

    first = lax.broadcasted_iota(jnp.int32, (taken, pair), 1) < HD
    zero = jnp.zeros((taken, pair), BF16)

    def stacked(block):
        return jnp.concatenate(
            [jnp.where(first, block, zero), jnp.where(first, zero, block)], axis=0
        )

    d_query, d_key, d_value = [], [], []
    for half in range(2):
        starts = [half * width + p * pair for p in range(width // pair)]
        pieces = [
            (
                keys[:, c : c + pair],
                values[:, c : c + pair],
                stacked(queries[:, c : c + pair]),
                stacked(grads[:, c : c + pair]),
            )
            for c in starts
        ]
        scores = [dot_nt(k, q) for k, v, q, g in pieces]
        weights_grads = [dot_nt(v, g) for k, v, q, g in pieces]
        weights_low, scores_grads = [], []
        for score, weights_grad in zip(scores, weights_grads):
            grown = jnp.exp2((score - jnp.max(score, axis=0, keepdims=True)) * EXPONENT)
            weights = grown * (1.0 / jnp.sum(grown, axis=0, keepdims=True))
            inner = jnp.sum(weights * weights_grad, axis=0, keepdims=True)
            weights_low.append(weights.astype(BF16))
            scores_grads.append((weights * (weights_grad - inner)).astype(BF16))
        for weights, scores_grad, (k, v, q, g) in zip(weights_low, scores_grads, pieces):
            d_value.append(dot(weights, g).astype(BF16))
            d_key.append((dot(scores_grad, q) * factor).astype(BF16))
            split = dot_tn(scores_grad, k) * factor
            d_query.append(jnp.where(first, split[:taken], split[taken:]).astype(BF16))
    half = len(d_key) // 2
    own = jnp.concatenate(d_key[:half] + d_value[:half], axis=1)
    peer = jnp.concatenate(d_key[half:] + d_value[half:], axis=1)
    query_own = jnp.concatenate(d_query[:half], axis=1)
    query_peer = jnp.concatenate(d_query[half:], axis=1)
    extra = (
        back_one[...]
        + dot_nt(query_own, qkv_all[0, :, :width])
        + dot_nt(query_peer, qkv_all[1, :, :width])
    )
    high = extra.astype(BF16)
    low = (extra - high.astype(F32)).astype(BF16)
    pick = picks[...]
    tokens_grad[...] = (
        dot_nt(own, qkv_all[0, :, width:])
        + dot_nt(peer, qkv_all[1, :, width:])
        + dot_tn(jnp.concatenate([pick, pick], axis=0), jnp.concatenate([high, low], axis=0))
    )
    query_grads[pl.ds(pl.multiple_of(step * taken, taken), taken), :] = query_own
    sums[...] += dot_tn(tokens[...], own)
    grad_b_query[...] += row_sum(query_own.astype(F32))
    grad_b_value[...] += row_sum(own[:, width:].astype(F32))

    @pl.when(step == last)
    def _():
        grad_w_key_value[...] = sums[...].astype(BF16)
        grad_w_query[...] = dot_tn(picked_tokens[...], query_grads[...]).astype(BF16)


def attention_back(
    tokens, keys, values, queries, grads, back_one, picks, picked_tokens, qkv_all, sequences
):
    rows, model = tokens.shape
    length = rows // sequences
    width = keys.shape[1] // 2
    taken = picks.shape[0] // sequences
    shape = jax.ShapeDtypeStruct
    return pl.pallas_call(
        backward_body,
        grid=(sequences,),
        in_specs=[rows_spec(length, model)]
        + [rows_spec(length, 2 * width)] * 2
        + [rows_spec(taken, 2 * width)] * 2
        + [rows_spec(taken, model), rows_spec(taken, length)]
        + [
            whole_spec(picked_tokens),
            pl.BlockSpec(qkv_all.shape, lambda i: (0, 0, 0), pipeline_mode=pl.Buffered(1)),
        ],
        out_specs=[
            rows_spec(length, model),
            pl.BlockSpec((model, width), lambda i: (0, 0)),
            pl.BlockSpec((model, 2 * width), lambda i: (0, 0)),
            pl.BlockSpec((1, width), lambda i: (0, 0)),
            pl.BlockSpec((1, width), lambda i: (0, 0)),
        ],
        out_shape=[
            shape((rows, model), F32),
            shape((model, width), BF16),
            shape((model, 2 * width), BF16),
            shape((1, width), F32),
            shape((1, width), F32),
        ],
        scratch_shapes=[
            pltpu.VMEM((picks.shape[0], width), BF16),
            pltpu.VMEM((model, 2 * width), F32),
        ],
        compiler_params=params(),
        cost_estimate=pl.CostEstimate(
            flops=int(rows * model * 6 * 2 * width),
            bytes_accessed=rows * model * 14,
            transcendentals=0,
        ),
        name="attention_back",
    )(tokens, keys, values, queries, grads, back_one, picks, picked_tokens, qkv_all)


def dense_body(
    tokens,
    attended,
    w_out,
    w_up_own,
    w_up_peer,
    w_down_own,
    w_down_peer,
    b_out,
    gain_one,
    shift_one,
    b_up_own,
    b_up_peer,
    b_down,
    gain_two,
    shift_two,
    layer_out,
):
    normed, _ = norm_parts(tokens[...].astype(F32) + dot(attended[...], w_out[...]) + b_out[...])
    layer_one = normed * gain_one[...] + shift_one[...]
    layer_low = layer_one.astype(BF16)
    summed = layer_one + b_down[...]
    for w_up, w_down, b_up in (
        (w_up_own, w_down_own, b_up_own),
        (w_up_peer, w_down_peer, b_up_peer),
    ):
        hidden = dot(layer_low, w_up[...]) + b_up[...]
        summed = summed + dot((hidden * gelu_share(hidden)).astype(BF16), w_down[...])
    normed, _ = norm_parts(summed)
    layer_out[...] = (normed * gain_two[...] + shift_two[...]).astype(BF16)


def dense_rows(*args):
    tokens, attended = args[0], args[1]
    rows, model = tokens.shape
    width = attended.shape[1] // 2
    half = args[3].shape[1]
    block = 512
    return pl.pallas_call(
        dense_body,
        grid=(rows // block,),
        in_specs=[rows_spec(block, model), rows_spec(block, 2 * width)]
        + [whole_spec(array) for array in args[2:]],
        out_specs=rows_spec(block, model),
        out_shape=jax.ShapeDtypeStruct((rows, model), BF16),
        compiler_params=params(),
        cost_estimate=pl.CostEstimate(
            flops=int(rows * model * (8 * half + 4 * width)),
            bytes_accessed=rows * model * 6,
            transcendentals=rows * half * 2,
        ),
        name="dense",
    )(*args)


def on_device(
    tokens,
    out_grad,
    positions,
    w_query,
    b_query,
    w_key,
    w_value,
    b_value,
    w_out,
    b_out,
    gain_one,
    shift_one,
    w_up,
    b_up,
    w_down,
    b_down,
    gain_two,
    shift_two,
):
    sequences, count = positions.shape
    width = w_query.shape[1]
    taken = -(-count // 16) * 16

    def row(vector):
        return vector.reshape(1, -1)

    slots = jnp.pad(positions, ((0, 0), (0, -count % 128)), constant_values=-1)
    (
        attended,
        keys,
        values,
        picked_q,
        picked_att,
        picked_tokens,
        picked_grad,
        picks,
        qkv_all,
        out_all,
        up_peer,
        down_peer,
        b_up_peer,
    ) = attention(
        tokens,
        out_grad,
        slots,
        w_query,
        w_key,
        w_value,
        w_out,
        w_up,
        w_down,
        row(b_query),
        row(b_value),
        row(b_up),
        taken,
    )
    shared = (
        out_all,
        w_up,
        up_peer,
        w_down,
        down_peer,
        row(b_out),
        row(gain_one),
        row(shift_one),
        row(b_up),
        b_up_peer,
        row(b_down),
        row(gain_two),
    )
    back_one, att_grad, grad_w_up, grad_w_down, grad_w_out, grad_b_up, vectors = marked_rows(
        picked_tokens, picked_att, picked_grad, *shared
    )
    tokens_grad, grad_w_query, grad_w_key_value, grad_b_query, grad_b_value = attention_back(
        tokens, keys, values, picked_q, att_grad, back_one, picks, picked_tokens, qkv_all, sequences
    )
    layer_out = dense_rows(tokens, attended, *shared, row(shift_two))

    grad_w_up, grad_w_down, grad_w_out, grad_w_query, grad_w_key_value = lax.psum(
        (grad_w_up, grad_w_down, grad_w_out, grad_w_query, grad_w_key_value), "dp"
    )
    vectors, grad_b_up, grad_b_query, grad_b_value = lax.psum(
        (vectors, grad_b_up, grad_b_query, grad_b_value), "dp"
    )
    return (
        layer_out,
        tokens_grad,
        grad_w_query.astype(F32),
        grad_b_query[0],
        grad_w_key_value[:, :width].astype(F32),
        grad_w_key_value[:, width:].astype(F32),
        grad_b_value[0],
        grad_w_out.astype(F32),
        vectors[0],
        vectors[1],
        vectors[2],
        grad_w_up.astype(F32),
        grad_b_up[0],
        grad_w_down.astype(F32),
        vectors[3],
        vectors[4],
        vectors[5],
    )


def solution(mesh):
    across = P("dp", None)
    columns, rows, split, copied = P(None, "tensor"), P("tensor", None), P("tensor"), P()
    in_specs = (
        across,
        across,
        across,
        columns,
        split,
        columns,
        columns,
        split,
        rows,
        copied,
        copied,
        copied,
        columns,
        split,
        rows,
        copied,
        copied,
        copied,
    )
    out_specs = (
        across,
        across,
        columns,
        split,
        columns,
        columns,
        split,
        rows,
        copied,
        copied,
        copied,
        columns,
        split,
        rows,
        copied,
        copied,
        copied,
    )
    return jax.shard_map(
        on_device, mesh=mesh, in_specs=in_specs, out_specs=out_specs, check_vma=False
    )
```

```python
import functools
import math

import jax
import jax.numpy as jnp
from jax import lax
from jax.experimental import pallas as pl
from jax.experimental.pallas import tpu as pltpu
from jax.sharding import PartitionSpec as P

HD = 64
NORM_EPSILON = 1e-12
BF16 = jnp.bfloat16
F32 = jnp.float32
EXPONENT = HD**-0.5 * math.log2(math.e)
ROOT_HALF = 0.7071067811865476
DENSITY = 0.3989422804014327
VMEM_BYTES = 58 * 2**20


def dot(left, right):
    return jnp.dot(left, right, preferred_element_type=F32)


def dot_nt(left, right):
    return lax.dot_general(left, right, (((1,), (1,)), ((), ())), preferred_element_type=F32)


def dot_tn(left, right):
    return lax.dot_general(left, right, (((0,), (0,)), ((), ())), preferred_element_type=F32)


def norm_parts(summed):
    centred = summed - jnp.mean(summed, axis=-1, keepdims=True)
    inverse = lax.rsqrt(jnp.mean(centred * centred, axis=-1, keepdims=True) + NORM_EPSILON)
    return centred * inverse, inverse


def norm_back(upstream, normed, inverse, gain):
    scaled = upstream * gain
    return inverse * (
        scaled
        - jnp.mean(scaled, axis=-1, keepdims=True)
        - normed * jnp.mean(scaled * normed, axis=-1, keepdims=True)
    )


def vector(packed, width, half, model, name):
    order = ("b_out", "gain_one", "shift_one", "b_down", "gain_two", "shift_two")
    base = 2 * width
    if name == "b_up":
        return packed[:, base : base + half]
    start = base + half + order.index(name) * model
    return packed[:, start : start + model]


def row_sum(values):
    return jnp.sum(values, axis=0, keepdims=True)


def rows_spec(rows, width):
    return pl.BlockSpec((rows, width), lambda i: (i, 0))


def whole_spec(array):
    return pl.BlockSpec(array.shape, lambda i: (0, 0), pipeline_mode=pl.Buffered(1))


def params():
    return pltpu.CompilerParams(vmem_limit_bytes=VMEM_BYTES)


def flipped(index, span):
    return index + span - 2 * span * ((index // span) % 2)


def attention_body(
    tokens,
    out_grad,
    positions,
    w_query,
    w_key,
    w_value,
    w_out,
    w_up,
    w_down,
    packed,
    attended,
    keys,
    values,
    picked_q,
    picked_att,
    picked_tokens,
    picked_grad,
    picks,
    qkv_all,
    out_all,
    up_peer,
    down_peer,
    b_up_peer,
    qkv,
    biases,
    kept_picks,
    places,
    local_sems,
    send_sems,
    recv_sems,
    bias_sems,
):
    step = pl.program_id(0)
    sequences = pl.num_programs(0) // 2
    turn = step // sequences
    length = tokens.shape[0]
    width = keys.shape[1]
    dp = lax.axis_index("dp")
    across = {"tensor": 1 - lax.axis_index("tensor")}
    beside = {"dp": flipped(dp, 2)}
    close = {"dp": flipped(dp, 1)}
    mine = dp % 4

    arrays = (
        (qkv.at[0], qkv.at[1]),
        (w_out, out_all.at[pl.ds(width, width)]),
        (w_up, up_peer),
        (w_down, down_peer),
    )

    def rows_of(ref, piece):
        count = ref.shape[0] // 4
        return ref.at[pl.ds(pl.multiple_of(piece * count, count), count)]

    def hop(index, kind):
        source, target = arrays[index]
        piece = (mine, mine, mine, flipped(mine, 2))[kind]
        device = (across, beside, close, close)[kind]
        return pltpu.make_async_remote_copy(
            src_ref=rows_of(source if kind == 0 else target, piece),
            dst_ref=rows_of(target, piece),
            send_sem=send_sems.at[index, kind],
            recv_sem=recv_sems.at[index, kind],
            device_id=device,
            device_id_type=pl.DeviceIdType.MESH,
        )

    def arrival(index, kind):
        _, target = arrays[index]
        piece = (mine, flipped(mine, 2), flipped(mine, 1), flipped(flipped(mine, 2), 1))[kind]
        device = (across, beside, close, close)[kind]
        here = rows_of(target, piece)
        return pltpu.make_async_remote_copy(
            src_ref=here,
            dst_ref=here,
            send_sem=send_sems.at[index, kind],
            recv_sem=recv_sems.at[index, kind],
            device_id=device,
            device_id_type=pl.DeviceIdType.MESH,
        )

    bias_pairs = (
        (biases.at[0], biases.at[1]),
        (biases.at[2], biases.at[3]),
        (packed.at[:, pl.ds(2 * width, b_up_peer.shape[1])], b_up_peer),
    )

    def bias_copy(index):
        source, target = bias_pairs[index]
        return pltpu.make_async_remote_copy(
            src_ref=source,
            dst_ref=target,
            send_sem=bias_sems.at[0, index],
            recv_sem=bias_sems.at[1, index],
            device_id=across,
            device_id_type=pl.DeviceIdType.MESH,
        )

    loads = (
        pltpu.make_async_copy(w_query, qkv.at[0, :, pl.ds(0, width)], local_sems.at[0]),
        pltpu.make_async_copy(w_key, qkv.at[0, :, pl.ds(width, width)], local_sems.at[1]),
        pltpu.make_async_copy(w_value, qkv.at[0, :, pl.ds(2 * width, width)], local_sems.at[2]),
        pltpu.make_async_copy(packed.at[:, pl.ds(0, width)], biases.at[0], local_sems.at[3]),
        pltpu.make_async_copy(packed.at[:, pl.ds(width, width)], biases.at[2], local_sems.at[4]),
    )
    keep_out = pltpu.make_async_copy(w_out, out_all.at[pl.ds(0, width)], local_sems.at[5])
    keep_qkv = pltpu.make_async_copy(qkv, qkv_all, local_sems.at[6])

    @pl.when(step == 0)
    def _():
        for load in loads:
            load.start()
        keep_out.start()
        places[...] = jnp.full(places.shape, -1, jnp.int32)
        places[:, : positions.shape[1]] = positions[...]
        barrier = pltpu.get_barrier_semaphore()
        for device in (across, beside, close):
            pl.semaphore_signal(
                barrier, inc=1, device_id=device, device_id_type=pl.DeviceIdType.MESH
            )
        for load in loads:
            load.wait()
        pl.semaphore_wait(barrier, 3)
        hop(0, 0).start()
        for index in range(3):
            bias_copy(index).start()

    @pl.when(step == 3)
    def _():
        arrival(0, 0).wait_recv()
        hop(0, 1).start()
        hop(0, 2).start()
        hop(1, 0).start()
        hop(2, 0).start()

    @pl.when(step == sequences - 2)
    def _():
        arrival(0, 1).wait_recv()
        hop(0, 3).start()

    @pl.when(step == sequences - 1)
    def _():
        for index in (1, 2):
            arrival(index, 0).wait_recv()
            hop(index, 1).start()
            hop(index, 2).start()
        hop(3, 0).start()

    @pl.when(step == sequences)
    def _():
        arrival(0, 2).wait_recv()
        arrival(0, 3).wait_recv()
        bias_copy(0).wait_recv()
        bias_copy(1).wait_recv()
        keep_qkv.start()

    @pl.when(step == sequences + 3)
    def _():
        arrival(3, 0).wait_recv()
        hop(3, 1).start()
        hop(3, 2).start()

    @pl.when(step == sequences + 4)
    def _():
        for index in (1, 2):
            arrival(index, 1).wait_recv()
            hop(index, 3).start()

    tokens_here = tokens[...]
    projected = dot(tokens_here, qkv[turn])
    query = (projected[:, :width] + biases[turn]).astype(BF16)
    key = projected[:, width : 2 * width].astype(BF16)
    value = (projected[:, 2 * width :] + biases[2 + turn]).astype(BF16)
    keys[...] = key
    values[...] = value
    pair = 2 * HD
    first = lax.broadcasted_iota(jnp.int32, (length, pair), 1) < HD
    zero = jnp.zeros((length, pair), BF16)
    one = jnp.ones((length, pair), BF16)
    for p in range(width // pair):
        here = slice(p * pair, (p + 1) * pair)
        k, v = key[:, here], value[:, here]
        k_two = jnp.concatenate([jnp.where(first, k, zero), jnp.where(first, zero, k)], axis=0)
        v_two = jnp.concatenate(
            [
                jnp.concatenate([jnp.where(first, v, zero), jnp.where(first, one, zero)], axis=1),
                jnp.concatenate([jnp.where(first, zero, v), jnp.where(first, zero, one)], axis=1),
            ],
            axis=0,
        )
        scores = dot_nt(query[:, here], k_two)
        left, right = scores[:, :length], scores[:, length:]
        left = jnp.exp2((left - jnp.max(left, axis=1, keepdims=True)) * EXPONENT).astype(BF16)
        right = jnp.exp2((right - jnp.max(right, axis=1, keepdims=True)) * EXPONENT).astype(BF16)
        both = dot(jnp.concatenate([left, right], axis=1), v_two)
        attended[:, here] = (both[:, :pair] / both[:, pair:]).astype(BF16)

    taken = picks.shape[0]
    sequence = step % sequences

    @pl.when(turn == 0)
    def _():
        spread = jnp.broadcast_to(places[pl.ds(sequence, 1), :], (length, places.shape[1]))
        column = lax.broadcasted_iota(jnp.int32, spread.shape, 1).astype(F32)
        hit = spread == lax.broadcasted_iota(jnp.int32, spread.shape, 0)
        earliest = jnp.min(jnp.where(hit, column, 1e6), axis=1, keepdims=True)
        fresh = jnp.where(column == earliest, 1.0, 0.0).T[:taken].astype(BF16)
        picks[...] = fresh
        kept_picks[sequence] = fresh
        picked_tokens[...] = dot(fresh, tokens_here).astype(BF16)
        picked_grad[...] = dot(fresh, out_grad[...]).astype(BF16)

    pick = kept_picks[sequence]
    picked_q[...] = dot(pick, query).astype(BF16)
    picked_att[...] = dot(pick, attended[...]).astype(BF16)

    @pl.when(step == 2 * sequences - 1)
    def _():
        arrival(3, 1).wait_recv()
        hop(3, 3).start()
        for index in (1, 2, 3):
            arrival(index, 2).wait_recv()
            arrival(index, 3).wait_recv()
        bias_copy(2).wait_recv()
        for index in range(4):
            for kind in range(4):
                hop(index, kind).wait_send()
        for index in range(3):
            bias_copy(index).wait_send()
        keep_out.wait()
        keep_qkv.wait()


def attention(
    tokens, out_grad, positions, w_query, w_key, w_value, w_out, w_up, w_down, packed, taken
):
    rows, model = tokens.shape
    sequences = positions.shape[0]
    length = rows // sequences
    width = w_query.shape[1]
    shape = jax.ShapeDtypeStruct
    slots = sequences * taken

    def both(count, columns):
        return pl.BlockSpec((count, columns), lambda s: (s % sequences, s // sequences))

    def once(count, columns):
        return pl.BlockSpec((count, columns), lambda s: (jnp.minimum(s, sequences - 1), 0))

    def again(count, columns):
        return pl.BlockSpec((count, columns), lambda s: (s % sequences, 0))

    anywhere = pl.BlockSpec(memory_space=pl.ANY)
    return pl.pallas_call(
        attention_body,
        grid=(2 * sequences,),
        in_specs=[
            again(length, model),
            once(length, model),
            pl.BlockSpec(positions.shape, lambda s: (0, 0)),
        ]
        + [anywhere] * 7,
        out_specs=[
            both(length, width),
            both(length, width),
            both(length, width),
            both(taken, width),
            both(taken, width),
            once(taken, model),
            once(taken, model),
            once(taken, length),
        ]
        + [anywhere] * 5,
        out_shape=[
            shape((rows, 2 * width), BF16),
            shape((rows, 2 * width), BF16),
            shape((rows, 2 * width), BF16),
            shape((slots, 2 * width), BF16),
            shape((slots, 2 * width), BF16),
            shape((slots, model), BF16),
            shape((slots, model), BF16),
            shape((slots, length), BF16),
            shape((2, model, 3 * width), BF16),
            shape((2 * width, model), BF16),
            shape(w_up.shape, BF16),
            shape(w_down.shape, BF16),
            shape((1, w_up.shape[1]), F32),
        ],
        scratch_shapes=[
            pltpu.VMEM((2, model, 3 * width), BF16),
            pltpu.VMEM((4, 1, width), F32),
            pltpu.VMEM((sequences, taken, length), BF16),
            pltpu.VMEM((sequences, -(-positions.shape[1] // 128) * 128), jnp.int32),
            pltpu.SemaphoreType.DMA((7,)),
            pltpu.SemaphoreType.DMA((4, 4)),
            pltpu.SemaphoreType.DMA((4, 4)),
            pltpu.SemaphoreType.DMA((2, 3)),
        ],
        compiler_params=pltpu.CompilerParams(
            vmem_limit_bytes=VMEM_BYTES, collective_id=0, has_side_effects=True
        ),
        cost_estimate=pl.CostEstimate(
            flops=int(2 * rows * width * (6 * model + 16 * length)),
            bytes_accessed=rows * model * 12,
            transcendentals=rows * length * width // HD,
        ),
        name="attention",
    )(tokens, out_grad, positions, w_query, w_key, w_value, w_out, w_up, w_down, packed)


def gelu_share(hidden):
    return 0.5 * (1.0 + lax.erf(hidden * ROOT_HALF))


def marked_body(
    tokens,
    attended,
    upstream,
    w_out,
    w_up_own,
    w_up_peer,
    w_down_own,
    w_down_peer,
    b_up_peer,
    packed,
    back_one_out,
    attended_grad,
    grad_ff,
    grad_w_out,
    vectors,
    slope,
    active,
):
    width = attended.shape[1] // 2
    half = w_up_own.shape[1]
    model = tokens.shape[1]
    named = functools.partial(vector, packed, width, half, model)
    normed_one, inverse_one = norm_parts(
        tokens[...].astype(F32) + dot(attended[...], w_out[...]) + named("b_out")
    )
    layer_one = normed_one * named("gain_one") + named("shift_one")
    layer_low = layer_one.astype(BF16)
    summed = layer_one + named("b_down")
    parts = ((0, w_up_own, w_down_own, named("b_up")), (1, w_up_peer, w_down_peer, b_up_peer[...]))
    for part, w_up, w_down, b_up in parts:
        hidden = dot(layer_low, w_up[...]) + b_up
        share = gelu_share(hidden)
        act = (hidden * share).astype(BF16)
        slope[part] = share + hidden * jnp.exp(-0.5 * hidden * hidden) * DENSITY
        if part == 0:
            active[...] = act
        summed = summed + dot(act, w_down[...])
    normed_two, inverse_two = norm_parts(summed)
    up = upstream[...].astype(F32)
    back_two = norm_back(up, normed_two, inverse_two, named("gain_two"))
    back_low = back_two.astype(BF16)
    layer_grad = back_two
    for part, w_up, w_down, b_up in parts:
        hidden_grad = (dot_nt(back_low, w_down[...]) * slope[part]).astype(BF16)
        layer_grad = layer_grad + dot_nt(hidden_grad, w_up[...])
        if part == 0:
            grad_b_up = row_sum(hidden_grad.astype(F32))
            for c in range(0, half, model):
                grad_ff[c : c + model, :] = dot_tn(layer_low, hidden_grad[:, c : c + model]).astype(
                    BF16
                )
            grad_ff[half : 2 * half, :] = dot_tn(active[...], back_low).astype(BF16)
    back_one = norm_back(layer_grad, normed_one, inverse_one, named("gain_one"))
    back_one_low = back_one.astype(BF16)
    back_one_out[...] = back_one
    grad_w_out[...] = dot_tn(attended[:, :width], back_one_low).astype(BF16)
    attended_grad[...] = dot_nt(back_one_low, w_out[...]).astype(BF16)
    vectors[...] = jnp.concatenate(
        [
            row_sum(back_one),
            row_sum(layer_grad * normed_one),
            row_sum(layer_grad),
            row_sum(back_two),
            row_sum(up * normed_two),
            row_sum(up),
        ]
        + [grad_b_up[:, c : c + model] for c in range(0, half, model)],
        axis=0,
    )


def marked_rows(*args):
    tokens, attended = args[0], args[1]
    rows, model = tokens.shape
    width = attended.shape[1] // 2
    half = args[4].shape[1]
    shape = jax.ShapeDtypeStruct
    return pl.pallas_call(
        marked_body,
        out_shape=[
            shape((rows, model), F32),
            shape((rows, 2 * width), BF16),
            shape((2 * half, model), BF16),
            shape((width, model), BF16),
            shape((6 + half // model, model), F32),
        ],
        scratch_shapes=[pltpu.VMEM((2, rows, half), F32), pltpu.VMEM((rows, half), BF16)],
        compiler_params=params(),
        cost_estimate=pl.CostEstimate(
            flops=int(rows * model * (2 * half * 10 + 2 * width * 5)),
            bytes_accessed=6 * model * half * 2,
            transcendentals=rows * half * 4,
        ),
        name="marked",
    )(*args)


class Ring:
    def __init__(self, chips, share, model):
        self.chips, self.count, self.columns = chips, share // chips, model // 2
        self.share = share
        dp = lax.axis_index("dp")
        self.core, chip = dp % 2, dp // 2
        self.place = self.at(chip)
        self.mate = {"dp": flipped(dp, 1)}
        self.up = {"dp": self.device(self.place + 1)}
        self.down = {"dp": self.device(self.place + chips - 1)}

    def at(self, chip):
        high, low = chip // 2, chip % 2
        return (1 - low) * high + low * (self.chips - 1 - high)

    def device(self, place):
        place = place % self.chips
        back = place // (self.chips // 2)
        chip = (1 - back) * 2 * place + back * (2 * (self.chips - 1 - place) + 1)
        return 2 * chip + self.core

    def neighbours(self):
        return self.up, self.down, self.mate

    def onward(self, way):
        return (self.up, self.down)[way]

    def segment(self, way, step):
        sign = 1 - 2 * way
        return (self.place - sign * step + 2 * self.chips) % self.chips

    def rows(self, segment):
        return pl.ds(pl.multiple_of(segment * self.count, 16), self.count)

    def final_rows(self, segment, core):
        return pl.ds(pl.multiple_of(core * self.share + segment * self.count, 16), self.count)

    def lanes(self, way):
        return pl.ds(way * self.columns, self.columns)


def remote(source, target, send, receive, device):
    return pltpu.make_async_remote_copy(
        src_ref=source,
        dst_ref=target,
        send_sem=send,
        recv_sem=receive,
        device_id=device,
        device_id_type=pl.DeviceIdType.MESH,
    )


def greet(devices):
    barrier = pltpu.get_barrier_semaphore()
    for device in devices:
        pl.semaphore_signal(barrier, inc=1, device_id=device, device_id_type=pl.DeviceIdType.MESH)
    pl.semaphore_wait(barrier, len(devices))


class Reduce:
    def __init__(self, ring, source, total, other, slots, core_sems, sems):
        self.ring, self.source, self.total, self.other = ring, source, total, other
        self.slots, self.core_sems, self.sems = slots, core_sems, sems

    def _core(self):
        ring = self.ring
        give = pl.ds(pl.multiple_of((1 - ring.core) * ring.share, 16), ring.share)
        keep = pl.ds(pl.multiple_of(ring.core * ring.share, 16), ring.share)
        return (
            remote(
                self.source.at[give],
                self.other,
                self.core_sems.at[0],
                self.core_sems.at[1],
                ring.mate,
            ),
            pltpu.make_async_copy(self.source.at[keep], self.total, self.core_sems.at[2]),
        )

    def begin(self):
        given, kept = self._core()
        given.start()
        kept.start()

    def join(self):
        given, kept = self._core()
        kept.wait()
        given.wait()
        self.total[...] += self.other[...]

    def _copy(self, way, step):
        ring = self.ring
        return remote(
            self.total.at[ring.rows(ring.segment(way, step)), ring.lanes(way)],
            self.slots.at[way, step],
            self.sems.at[0, way, step],
            self.sems.at[1, way, step],
            ring.onward(way),
        )

    def event(self, step):
        ring = self.ring

        @pl.when(step > 0)
        def _():
            for way in range(2):
                self._copy(way, step - 1).wait()
                here = ring.rows(ring.segment(way, step))
                self.total[here, ring.lanes(way)] += self.slots[way, step - 1]

        @pl.when(step < ring.chips - 1)
        def _():
            for way in range(2):
                self._copy(way, step).start()

    def done_segment(self, way):
        return self.ring.segment(way, self.ring.chips - 1)


class Gather:
    def __init__(self, ring, firsts, out, local_sems, sems, mate_sems):
        self.ring, self.firsts, self.out = ring, firsts, out
        self.local_sems, self.sems, self.mate_sems = local_sems, sems, mate_sems

    def _segment(self, way, step):
        sign = 1 - 2 * way
        return (self.ring.place + sign - sign * step + 2 * self.ring.chips) % self.ring.chips

    def _there(self, way, step, core):
        ring = self.ring
        return self.out.at[ring.final_rows(self._segment(way, step), core), ring.lanes(way)]

    def _keep(self, way):
        return pltpu.make_async_copy(
            self.firsts[way], self._there(way, 0, self.ring.core), self.local_sems.at[way]
        )

    def _send(self, way, step, first):
        there = self._there(way, step, self.ring.core)
        source = self.firsts[way] if first else there
        return remote(
            source, there, self.sems.at[0, way, step], self.sems.at[1, way, step], self.ring.onward(way)
        )

    def _arrive(self, way, step):
        there = self._there(way, step + 1, self.ring.core)
        return remote(
            there, there, self.sems.at[0, way, step], self.sems.at[1, way, step], self.ring.onward(way)
        )

    def _mate(self, way, step, first):
        there = self._there(way, step, self.ring.core)
        source = self.firsts[way] if first else there
        return remote(
            source,
            there,
            self.mate_sems.at[0, way, step],
            self.mate_sems.at[1, way, step],
            self.ring.mate,
        )

    def _from_mate(self, way, step):
        there = self._there(way, step, 1 - self.ring.core)
        return remote(
            there,
            there,
            self.mate_sems.at[0, way, step],
            self.mate_sems.at[1, way, step],
            self.ring.mate,
        )

    def begin(self):
        for way in range(2):
            self._keep(way).start()
            self._send(way, 0, True).start()
            self._mate(way, 0, True).start()

    def event(self, step):
        for way in range(2):
            self._arrive(way, step - 1).wait_recv()

        @pl.when(step < self.ring.chips - 1)
        def _():
            for way in range(2):
                self._send(way, step, False).start()

        for way in range(2):
            self._mate(way, step, False).start()

    def finish(self):
        for way in range(2):
            self._keep(way).wait()
            self._send(way, 0, True).wait_send()
            self._mate(way, 0, True).wait_send()
            self._from_mate(way, 0).wait_recv()

        def rest(step, carry):
            for way in range(2):

                @pl.when(step < self.ring.chips - 1)
                def _():
                    self._send(way, step, False).wait_send()

                self._mate(way, step, False).wait_send()
                self._from_mate(way, step).wait_recv()
            return carry

        lax.fori_loop(1, self.ring.chips, rest, 0)


def backward_body(
    chips,
    tokens,
    keys,
    values,
    queries,
    grads,
    back_one,
    picked_tokens,
    qkv_all,
    grad_w_out,
    vectors_in,
    grad_ff,
    d_own,
    d_peer,
    extra_out,
    grads_rest,
    vectors,
    reduced,
    query_grads,
    sums,
    total,
    other,
    slots,
    core_sems,
    ring_sems,
):
    step = pl.program_id(0)
    last = pl.num_programs(0) - 1
    model = tokens.shape[1]
    width = keys.shape[1] // 2
    taken = queries.shape[0]
    factor = HD**-0.5
    pair = 2 * HD
    ring = Ring(chips, total.shape[0], model)
    reduction = Reduce(ring, grad_ff, total, other, slots, core_sems, ring_sems)

    @pl.when(step == 0)
    def _():
        sums[...] = jnp.zeros_like(sums)
        vectors[...] = jnp.zeros_like(vectors)
        greet(ring.neighbours())
        reduction.begin()

    @pl.when(step == 1)
    def _():
        reduction.join()

    @pl.when(step > 0)
    def _():
        reduction.event(step - 1)

    first = lax.broadcasted_iota(jnp.int32, (taken, pair), 1) < HD
    zero = jnp.zeros((taken, pair), BF16)

    def stacked(block):
        return jnp.concatenate(
            [jnp.where(first, block, zero), jnp.where(first, zero, block)], axis=0
        )

    d_query, d_key, d_value = [], [], []
    for half in range(2):
        starts = [half * width + p * pair for p in range(width // pair)]
        pieces = [
            (
                keys[:, c : c + pair],
                values[:, c : c + pair],
                stacked(queries[:, c : c + pair]),
                stacked(grads[:, c : c + pair]),
            )
            for c in starts
        ]
        scores = [dot_nt(k, q) for k, v, q, g in pieces]
        weights_grads = [dot_nt(v, g) for k, v, q, g in pieces]
        weights_low, scores_grads = [], []
        for score, weights_grad in zip(scores, weights_grads):
            grown = jnp.exp2((score - jnp.max(score, axis=0, keepdims=True)) * EXPONENT)
            weights = grown * (1.0 / jnp.sum(grown, axis=0, keepdims=True))
            inner = jnp.sum(weights * weights_grad, axis=0, keepdims=True)
            weights_low.append(weights.astype(BF16))
            scores_grads.append((weights * (weights_grad - inner)).astype(BF16))
        for weights, scores_grad, (k, v, q, g) in zip(weights_low, scores_grads, pieces):
            d_value.append(dot(weights, g).astype(BF16))
            d_key.append((dot(scores_grad, q) * factor).astype(BF16))
            split = dot_tn(scores_grad, k) * factor
            d_query.append(jnp.where(first, split[:taken], split[taken:]).astype(BF16))
    half = len(d_key) // 2
    own = jnp.concatenate(d_key[:half] + d_value[:half], axis=1)
    d_own[...] = own
    d_peer[...] = jnp.concatenate(d_key[half:] + d_value[half:], axis=1)
    query_own = jnp.concatenate(d_query[:half], axis=1)
    query_peer = jnp.concatenate(d_query[half:], axis=1)
    extra_out[...] = (
        back_one[...]
        + dot_nt(query_own, qkv_all[0, :, :width])
        + dot_nt(query_peer, qkv_all[1, :, :width])
    )
    query_grads[pl.ds(pl.multiple_of(step * taken, taken), taken), :] = query_own
    sums[...] += dot_tn(tokens[...], own)
    vectors[8:9, :width] += row_sum(query_own.astype(F32))
    vectors[8:9, width:] += row_sum(own[:, width:].astype(F32))

    @pl.when(step == last)
    def _():
        grads_rest[:model, :] = sums[...].astype(BF16)
        query_total = dot_tn(picked_tokens[...], query_grads[...]).astype(BF16)
        for c in range(2):
            grads_rest[model : model + width, c * width : (c + 1) * width] = query_total[
                c * width : (c + 1) * width
            ]
        grads_rest[model + width : model + 2 * width, :] = grad_w_out[...]
        vectors[:8, :] = vectors_in[...]

        def rest(event, carry):
            reduction.event(event)
            return carry

        lax.fori_loop(last, chips, rest, 0)
        for way in range(2):
            reduced[way] = total[ring.rows(reduction.done_segment(way)), ring.lanes(way)]


def attention_back(
    tokens,
    keys,
    values,
    queries,
    grads,
    back_one,
    picked_tokens,
    qkv_all,
    grad_w_out,
    vectors,
    grad_ff,
    sequences,
    chips,
):
    rows, model = tokens.shape
    length = rows // sequences
    width = keys.shape[1] // 2
    slots = queries.shape[0]
    taken = slots // sequences
    share = grad_ff.shape[0] // 2
    rest_rows = padded_rows(model + 2 * width, chips)
    shape = jax.ShapeDtypeStruct

    def fixed(array_shape):
        return pl.BlockSpec(array_shape, lambda i: (0,) * len(array_shape))

    piece = (2, share // chips, model // 2)
    return pl.pallas_call(
        functools.partial(backward_body, chips),
        grid=(sequences,),
        in_specs=[rows_spec(length, model)]
        + [rows_spec(length, 2 * width)] * 2
        + [rows_spec(taken, 2 * width)] * 2
        + [rows_spec(taken, model)]
        + [
            whole_spec(picked_tokens),
            pl.BlockSpec(qkv_all.shape, lambda i: (0, 0, 0), pipeline_mode=pl.Buffered(1)),
            whole_spec(grad_w_out),
            whole_spec(vectors),
            pl.BlockSpec(memory_space=pl.ANY),
        ],
        out_specs=[
            rows_spec(length, 2 * width),
            rows_spec(length, 2 * width),
            rows_spec(taken, model),
            fixed((rest_rows, model)),
            fixed((16, model)),
            fixed(piece),
        ],
        out_shape=[
            shape((rows, 2 * width), BF16),
            shape((rows, 2 * width), BF16),
            shape((slots, model), F32),
            shape((rest_rows, model), BF16),
            shape((16, model), F32),
            shape(piece, BF16),
        ],
        scratch_shapes=[
            pltpu.VMEM((slots, width), BF16),
            pltpu.VMEM((model, 2 * width), F32),
            pltpu.VMEM((share, model), BF16),
            pltpu.VMEM((share, model), BF16),
            pltpu.VMEM((2, chips - 1) + piece[1:], BF16),
            pltpu.SemaphoreType.DMA((3,)),
            pltpu.SemaphoreType.DMA((2, 2, chips - 1)),
        ],
        compiler_params=pltpu.CompilerParams(
            vmem_limit_bytes=VMEM_BYTES, collective_id=1, has_side_effects=True
        ),
        cost_estimate=pl.CostEstimate(
            flops=int(rows * model * 4 * 2 * width),
            bytes_accessed=rows * model * 14,
            transcendentals=0,
        ),
        name="attention_back",
    )(
        tokens,
        keys,
        values,
        queries,
        grads,
        back_one,
        picked_tokens,
        qkv_all,
        grad_w_out,
        vectors,
        grad_ff,
    )


def padded_rows(rows, chips):
    return -(-rows // (32 * chips)) * 32 * chips


def finish_body(
    d_own,
    d_peer,
    extra,
    picks,
    qkv_all,
    layer_in,
    up_left,
    up_right,
    down,
    key_value,
    query,
    out,
    tokens_grad,
    layer_out,
    grad_w_up,
    grad_w_down,
    grad_w_key,
    grad_w_value,
    grad_w_query,
    grad_w_out,
):
    width = grad_w_key.shape[1]
    model = tokens_grad.shape[1]
    wide = extra[...]
    high = wide.astype(BF16)
    low = (wide - high.astype(F32)).astype(BF16)
    pick = picks[...]
    tokens_grad[...] = (
        dot_nt(d_own[...], qkv_all[0, :, width:])
        + dot_nt(d_peer[...], qkv_all[1, :, width:])
        + dot_tn(jnp.concatenate([pick, pick], axis=0), jnp.concatenate([high, low], axis=0))
    )
    layer_out[...] = layer_in[...]
    grad_w_up[:, :model] = up_left[...].astype(F32)
    grad_w_up[:, model:] = up_right[...].astype(F32)
    grad_w_down[...] = down[...].astype(F32)
    grad_w_key[...] = key_value[:, :width].astype(F32)
    grad_w_value[...] = key_value[:, width:].astype(F32)
    grad_w_query[...] = query[...].astype(F32)
    grad_w_out[...] = out[...].astype(F32)


def finish(d_own, d_peer, extra, picks, qkv_all, layer, sums_ff, sums_rest, half, sequences):
    rows, model = d_own.shape
    length = rows // sequences
    width = model // 2
    taken = picks.shape[0] // sequences
    assert half == 2 * model and width % sequences == 0 and sequences % 2 == 0
    part = model // sequences
    shape = jax.ShapeDtypeStruct

    def block(count, columns, start, column=None):
        offset = start // count
        return pl.BlockSpec((count, columns), lambda i: (offset + i, 0))

    turns = sequences // 2
    return pl.pallas_call(
        finish_body,
        grid=(sequences,),
        in_specs=[
            rows_spec(length, model),
            rows_spec(length, model),
            rows_spec(taken, model),
            rows_spec(taken, length),
            pl.BlockSpec(qkv_all.shape, lambda i: (0, 0, 0), pipeline_mode=pl.Buffered(1)),
            rows_spec(length, model),
            block(part, model, 0),
            block(part, model, model),
            block(2 * part, model, half),
            block(part, model, 0),
            pl.BlockSpec((part, width), lambda i: (model // part + i % turns, i // turns)),
            block(width // sequences, model, model + width),
        ],
        out_specs=[
            rows_spec(length, model),
            rows_spec(length, model),
            rows_spec(part, half),
            rows_spec(2 * part, model),
            rows_spec(part, width),
            rows_spec(part, width),
            rows_spec(part, width),
            rows_spec(width // sequences, model),
        ],
        out_shape=[
            shape((rows, model), F32),
            shape((rows, model), BF16),
            shape((model, half), F32),
            shape((half, model), F32),
            shape((model, width), F32),
            shape((model, width), F32),
            shape((model, width), F32),
            shape((width, model), F32),
        ],
        compiler_params=params(),
        cost_estimate=pl.CostEstimate(
            flops=int(rows * model * 4 * 2 * width),
            bytes_accessed=rows * model * 16,
            transcendentals=0,
        ),
        name="finish",
    )(
        d_own,
        d_peer,
        extra,
        picks,
        qkv_all,
        layer,
        sums_ff,
        sums_ff,
        sums_ff,
        sums_rest,
        sums_rest,
        sums_rest,
    )


def dense_body(
    chips,
    levels,
    tokens,
    attended,
    w_out,
    w_up_own,
    w_up_peer,
    w_down_own,
    w_down_peer,
    b_up_peer,
    packed,
    reduced,
    grads_rest,
    vectors_in,
    layer_out,
    sums_ff,
    sums_rest,
    vectors,
    total,
    other,
    slots,
    last_pieces,
    exchanged,
    gained,
    core_sems,
    ring_sems,
    keep_sems,
    ff_sems,
    ff_mate_sems,
    rest_sems,
    rest_mate_sems,
    vector_sems,
):
    step = pl.program_id(0)
    steps = pl.num_programs(0)
    width = attended.shape[1] // 2
    half = w_up_own.shape[1]
    model = tokens.shape[1]
    dp = lax.axis_index("dp")
    ring = Ring(chips, total.shape[0], model)
    ff_ring = Ring(chips, sums_ff.shape[0] // 2, model)
    reduction = Reduce(ring, grads_rest, total, other, slots, core_sems, ring_sems)
    gather_ff = Gather(
        ff_ring,
        [reduced.at[way] for way in range(2)],
        sums_ff,
        keep_sems.at[0],
        ff_sems,
        ff_mate_sems,
    )
    gather_rest = Gather(
        ring,
        [last_pieces.at[way] for way in range(2)],
        sums_rest,
        keep_sems.at[1],
        rest_sems,
        rest_mate_sems,
    )

    def exchange(level):
        return remote(
            exchanged.at[level],
            gained.at[level],
            vector_sems.at[0, level],
            vector_sems.at[1, level],
            {"dp": flipped(dp, 2**level)},
        )

    def vector_event(level):
        if level > 0:
            exchange(level - 1).wait()
            exchanged[level] = exchanged[level - 1] + gained[level - 1]
        if level < levels:
            exchange(level).start()
        else:
            vectors[...] = exchanged[level]

    def rest_event(event):
        @pl.when(event < chips)
        def _():
            reduction.event(event)

        @pl.when(event == chips - 1)
        def _():
            for way in range(2):
                last_pieces[way] = total[ring.rows(reduction.done_segment(way)), ring.lanes(way)]
            gather_rest.begin()

        @pl.when(event > chips - 1)
        def _():
            gather_rest.event(event - (chips - 1))

    @pl.when(step == 0)
    def _():
        greet(ring.neighbours() + tuple({"dp": flipped(dp, 2**level)} for level in range(1, levels)))
        reduction.begin()
        gather_ff.begin()
        exchanged[0] = vectors_in[...]
        vector_event(0)

    @pl.when(step > 0)
    def _():
        @pl.when(step < chips)
        def _():
            gather_ff.event(step)

        rest_event(2 * step - 1)

    for level in range(1, levels + 1):

        @pl.when(step == jnp.minimum(level, steps - 1))
        def _():
            vector_event(level)

    named = functools.partial(vector, packed, width, half, model)
    normed, _ = norm_parts(tokens[...].astype(F32) + dot(attended[...], w_out[...]) + named("b_out"))
    layer_one = normed * named("gain_one") + named("shift_one")
    layer_low = layer_one.astype(BF16)
    summed = layer_one + named("b_down")
    hidden = dot(layer_low, w_up_own[...]) + named("b_up")
    summed = summed + dot((hidden * gelu_share(hidden)).astype(BF16), w_down_own[...])

    @pl.when(step == 0)
    def _():
        reduction.join()

    rest_event(2 * step)
    hidden = dot(layer_low, w_up_peer[...]) + b_up_peer[...]
    summed = summed + dot((hidden * gelu_share(hidden)).astype(BF16), w_down_peer[...])
    normed, _ = norm_parts(summed)
    layer_out[...] = (normed * named("gain_two") + named("shift_two")).astype(BF16)

    @pl.when(step == steps - 1)
    def _():
        def more_ff(event, carry):
            gather_ff.event(event)
            return carry

        def more_rest(event, carry):
            rest_event(event)
            return carry

        lax.fori_loop(steps, chips, more_ff, 0)
        lax.fori_loop(2 * steps - 1, 2 * chips - 1, more_rest, 0)
        gather_ff.finish()
        gather_rest.finish()


def dense_rows(
    tokens,
    attended,
    w_out,
    w_up_own,
    w_up_peer,
    w_down_own,
    w_down_peer,
    b_up_peer,
    packed,
    reduced,
    grads_rest,
    vectors,
    sequences,
    chips,
):
    rows, model = tokens.shape
    half = w_up_own.shape[1]
    block = rows // sequences
    levels = (2 * chips).bit_length() - 1
    assert 2**levels == 2 * chips
    share = grads_rest.shape[0] // 2
    piece = (share // chips, model // 2)
    shape = jax.ShapeDtypeStruct
    anywhere = pl.BlockSpec(memory_space=pl.ANY)
    arrays = (w_out, w_up_own, w_up_peer, w_down_own, w_down_peer, b_up_peer, packed)
    dma = pltpu.SemaphoreType.DMA
    return pl.pallas_call(
        functools.partial(dense_body, chips, levels),
        grid=(sequences,),
        in_specs=[rows_spec(block, model)] * 2
        + [whole_spec(array) for array in arrays]
        + [anywhere, anywhere, whole_spec(vectors)],
        out_specs=[
            rows_spec(block, model),
            anywhere,
            anywhere,
            pl.BlockSpec(vectors.shape, lambda i: (0, 0)),
        ],
        out_shape=[
            shape((rows, model), BF16),
            shape((2 * half, model), BF16),
            shape(grads_rest.shape, BF16),
            shape(vectors.shape, F32),
        ],
        scratch_shapes=[
            pltpu.VMEM((share, model), BF16),
            pltpu.VMEM((share, model), BF16),
            pltpu.VMEM((2, chips - 1) + piece, BF16),
            pltpu.VMEM((2,) + piece, BF16),
            pltpu.VMEM((levels + 1,) + vectors.shape, F32),
            pltpu.VMEM((levels,) + vectors.shape, F32),
            dma((3,)),
            dma((2, 2, chips - 1)),
            dma((2, 2)),
            dma((2, 2, chips - 1)),
            dma((2, 2, chips)),
            dma((2, 2, chips - 1)),
            dma((2, 2, chips)),
            dma((2, levels)),
        ],
        compiler_params=pltpu.CompilerParams(
            vmem_limit_bytes=VMEM_BYTES, collective_id=2, has_side_effects=True
        ),
        cost_estimate=pl.CostEstimate(
            flops=int(rows * model * (8 * half + 2 * model)),
            bytes_accessed=rows * model * 6,
            transcendentals=rows * half * 2,
        ),
        name="dense",
    )(tokens, attended, *arrays, reduced, grads_rest, vectors)


def on_device(
    chips,
    tokens,
    out_grad,
    positions,
    w_query,
    b_query,
    w_key,
    w_value,
    b_value,
    w_out,
    b_out,
    gain_one,
    shift_one,
    w_up,
    b_up,
    w_down,
    b_down,
    gain_two,
    shift_two,
):
    sequences, count = positions.shape
    half = w_up.shape[1]
    taken = -(-count // 16) * 16
    packed = jnp.concatenate(
        [b_query, b_value, b_up, b_out, gain_one, shift_one, b_down, gain_two, shift_two]
    ).reshape(1, -1)
    (
        attended,
        keys,
        values,
        picked_q,
        picked_att,
        picked_tokens,
        picked_grad,
        picks,
        qkv_all,
        out_all,
        up_peer,
        down_peer,
        b_up_peer,
    ) = attention(
        tokens, out_grad, positions, w_query, w_key, w_value, w_out, w_up, w_down, packed, taken
    )
    shared = (out_all, w_up, up_peer, w_down, down_peer, b_up_peer, packed)
    back_one, att_grad, grad_ff, grad_w_out, vectors = marked_rows(
        picked_tokens, picked_att, picked_grad, *shared
    )
    d_own, d_peer, extra, grads_rest, vectors, reduced = attention_back(
        tokens,
        keys,
        values,
        picked_q,
        att_grad,
        back_one,
        picked_tokens,
        qkv_all,
        grad_w_out,
        vectors,
        grad_ff,
        sequences,
        chips,
    )
    layer, sums_ff, sums_rest, vectors = dense_rows(
        tokens, attended, *shared, reduced, grads_rest, vectors, sequences, chips
    )
    (
        tokens_grad,
        layer_out,
        grad_w_up,
        grad_w_down,
        grad_w_key,
        grad_w_value,
        grad_w_query,
        grad_w_out,
    ) = finish(d_own, d_peer, extra, picks, qkv_all, layer, sums_ff, sums_rest, half, sequences)
    width = w_query.shape[1]
    return (
        layer_out,
        tokens_grad,
        grad_w_query,
        vectors[8, :width],
        grad_w_key,
        grad_w_value,
        vectors[8, width:],
        grad_w_out,
        vectors[0],
        vectors[1],
        vectors[2],
        grad_w_up,
        vectors[6:8].reshape(-1),
        grad_w_down,
        vectors[3],
        vectors[4],
        vectors[5],
    )


def solution(mesh):
    across = P("dp", None)
    columns, rows, split, copied = P(None, "tensor"), P("tensor", None), P("tensor"), P()
    in_specs = (
        across,
        across,
        across,
        columns,
        split,
        columns,
        columns,
        split,
        rows,
        copied,
        copied,
        copied,
        columns,
        split,
        rows,
        copied,
        copied,
        copied,
    )
    out_specs = (
        across,
        across,
        columns,
        split,
        columns,
        columns,
        split,
        rows,
        copied,
        copied,
        copied,
        columns,
        split,
        rows,
        copied,
        copied,
        copied,
    )
    return jax.shard_map(
        functools.partial(on_device, mesh.shape["dp"] // 2), mesh=mesh, in_specs=in_specs, out_specs=out_specs, check_vma=False
    )
```

```python
import functools
import math

import jax
import jax.numpy as jnp
from jax import lax
from jax.experimental import pallas as pl
from jax.experimental.pallas import tpu as pltpu
from jax.sharding import PartitionSpec as P

HD = 64
NORM_EPSILON = 1e-12
BF16 = jnp.bfloat16
F32 = jnp.float32
EXPONENT = HD**-0.5 * math.log2(math.e)
ROOT_HALF = 0.7071067811865476
DENSITY = 0.3989422804014327
VMEM_BYTES = 58 * 2**20
FF_WAYS = 4
LOCAL = 2


def dot(left, right):
    return jnp.dot(left, right, preferred_element_type=F32)


def dot_nt(left, right):
    return lax.dot_general(left, right, (((1,), (1,)), ((), ())), preferred_element_type=F32)


def dot_tn(left, right):
    return lax.dot_general(left, right, (((0,), (0,)), ((), ())), preferred_element_type=F32)


def norm_parts(summed):
    centred = summed - jnp.mean(summed, axis=-1, keepdims=True)
    inverse = lax.rsqrt(jnp.mean(centred * centred, axis=-1, keepdims=True) + NORM_EPSILON)
    return centred * inverse, inverse


def norm_back(upstream, normed, inverse, gain):
    scaled = upstream * gain
    return inverse * (
        scaled
        - jnp.mean(scaled, axis=-1, keepdims=True)
        - normed * jnp.mean(scaled * normed, axis=-1, keepdims=True)
    )


def row(vector):
    return vector[...].reshape(1, -1)


def row_sum(values):
    return jnp.sum(values, axis=0, keepdims=True)


def rows_spec(rows, width):
    return pl.BlockSpec((rows, width), lambda i: (i, 0))


def vector_spec(array):
    return pl.BlockSpec(array.shape, lambda i: (0,))


def whole_spec(array):
    return pl.BlockSpec(array.shape, lambda i: (0, 0), pipeline_mode=pl.Buffered(1))


def params():
    return pltpu.CompilerParams(vmem_limit_bytes=VMEM_BYTES)


def flipped(index, span):
    return index + span - 2 * span * ((index // span) % 2)


def remote(source, target, send, receive, device):
    return pltpu.make_async_remote_copy(
        src_ref=source,
        dst_ref=target,
        send_sem=send,
        recv_sem=receive,
        device_id=device,
        device_id_type=pl.DeviceIdType.MESH,
    )


def greet(devices):
    barrier = pltpu.get_barrier_semaphore()
    for device in devices:
        pl.semaphore_signal(barrier, inc=1, device_id=device, device_id_type=pl.DeviceIdType.MESH)
    pl.semaphore_wait(barrier, len(devices))


PIECES = 8


class Fetch:
    def __init__(self, source, target, send_sems, recv_sems, first, second):
        self.source, self.target = source, target
        self.send_sems, self.recv_sems = send_sems, recv_sems
        self.dp = lax.axis_index("dp")
        self.hops = ((0, 0), (first, 0), (second, 0), (second, first)) + tuple(
            (1, flips) for flips in (0, first, second, first + second)
        )

    def _copy(self, source, piece, hop):
        count = self.target.shape[0] // PIECES
        rows = pl.ds(pl.multiple_of(piece * count, 16), count)
        if hop:
            device = {"dp": flipped(self.dp, self.hops[hop][0])}
        else:
            device = {"tensor": 1 - lax.axis_index("tensor")}
        return remote(
            source.at[rows], self.target.at[rows], self.send_sems.at[hop], self.recv_sems.at[hop], device
        )

    def _piece(self, flips):
        piece = self.dp % PIECES
        for span in (4, 2, 1):
            if flips & span:
                piece = flipped(piece, span)
        return piece

    def out(self, hop):
        return self._copy(
            self.target if hop else self.source, self._piece(self.hops[hop][1]), hop
        )

    def into(self, hop):
        return self._copy(self.target, self._piece(self.hops[hop][0] | self.hops[hop][1]), hop)

    def move(self, what):
        if what == "x":
            self.out(0).start()
        if what == "z":
            self.into(0).wait_recv()
            for hop in (1, 2, 4):
                self.out(hop).start()
        if what == "y":
            self.into(1).wait_recv()
            for hop in (3, 5):
                self.out(hop).start()
        if what == "c":
            self.into(2).wait_recv()
            self.into(3).wait_recv()
            for hop in (6, 7):
                self.out(hop).start()
        if what == "end":
            for hop in (4, 5, 6, 7):
                self.into(hop).wait_recv()


def attention_body(
    tokens,
    out_grad,
    positions,
    w_query,
    w_key,
    w_value,
    w_out,
    w_up,
    w_down,
    b_query,
    b_value,
    b_up,
    attended,
    attended_local,
    keys,
    values,
    picked_q,
    picked_tokens,
    picked_grad,
    picks,
    picked_att,
    qkv_all,
    out_all,
    up_peer,
    down_peer,
    b_up_peer,
    qkv,
    biases,
    up_biases,
    kept_tokens,
    kept_picks,
    kept_att,
    kept_local,
    places,
    local_sems,
    send_sems,
    recv_sems,
    bias_sems,
    att_sems,
):
    step = pl.program_id(0)
    sequences = pl.num_programs(0) // 2
    sequence = step % sequences
    turn = step // sequences
    length = tokens.shape[0]
    width = keys.shape[1]
    model = tokens.shape[1]
    taken = picks.shape[0]
    dp = lax.axis_index("dp")
    across = {"tensor": 1 - lax.axis_index("tensor")}

    def halves(source, target):
        rows = target.shape[0] // 2
        return [(source.at[pl.ds(i * rows, rows)], target.at[pl.ds(i * rows, rows)]) for i in range(2)]

    pairs = (
        [(w_out, out_all.at[pl.ds(width, width)])]
        + halves(qkv.at[0], qkv.at[1])
        + halves(w_up, up_peer)
        + halves(w_down, down_peer)
    )
    fetches = [
        Fetch(source, target, send_sems.at[i], recv_sems.at[i], *((4, 2), (2, 4))[i % 2])
        for i, (source, target) in enumerate(pairs)
    ]
    bias_copies = [
        remote(source, target, bias_sems.at[0, i], bias_sems.at[1, i], across)
        for i, (source, target) in enumerate(
            (
                (biases.at[0], biases.at[1]),
                (biases.at[2], biases.at[3]),
                (up_biases, b_up_peer),
            )
        )
    ]

    far = pl.ds(LOCAL * taken, (sequences - LOCAL) * taken)
    att_copy = remote(
        kept_att.at[far],
        picked_att.at[far, pl.ds(width, width)],
        att_sems.at[0],
        att_sems.at[1],
        across,
    )

    loads = [
        pltpu.make_async_copy(weight, qkv.at[0, :, pl.ds(i * width, width)], local_sems.at[i])
        for i, weight in enumerate((w_query, w_key, w_value))
    ]
    keep_out = pltpu.make_async_copy(w_out, out_all.at[pl.ds(0, width)], local_sems.at[3])
    keep_qkv = pltpu.make_async_copy(qkv, qkv_all, local_sems.at[4])
    keep_att = pltpu.make_async_copy(kept_att, picked_att.at[:, pl.ds(0, width)], local_sems.at[5])
    keep_local = pltpu.make_async_copy(
        kept_local, picked_att.at[pl.ds(0, LOCAL * taken), pl.ds(width, width)], local_sems.at[6]
    )

    @pl.when(step == 0)
    def _():
        for load in loads:
            load.start()
        keep_out.start()
        places[...] = jnp.full(places.shape, -1, jnp.int32)
        places[:, : positions.shape[1]] = positions[...]
        biases[0] = row(b_query)
        biases[2] = row(b_value)
        up_biases[...] = row(b_up)
        greet((across,) + tuple({"dp": flipped(dp, span)} for span in (1, 2, 4)))
        fetches[0].move("x")
        for load in loads:
            load.wait()
        fetches[1].move("x")
        fetches[2].move("x")
        for copy in bias_copies:
            copy.start()

    moves = {
        1: [(3, "x")],
        2: [(0, "z"), (1, "z")],
        3: [(2, "z"), (4, "x")],
        4: [(3, "z"), (0, "y"), (1, "y"), (5, "x")],
        5: [(4, "z"), (2, "y"), (6, "x")],
        6: [(3, "y"), (0, "c"), (1, "c")],
        7: [(5, "z"), (6, "z"), (4, "y"), (2, "c")],
        8: [(1, "end"), (2, "end")],
        9: [(5, "y"), (6, "y"), (3, "c")],
        10: [(4, "c"), (5, "c")],
        14: [(6, "c")],
    }
    for when, made in moves.items():

        @pl.when(step == when)
        def _():
            for index, what in made:
                fetches[index].move(what)

    @pl.when(step == sequences)
    def _():
        bias_copies[0].wait_recv()
        bias_copies[1].wait_recv()
        keep_qkv.start()
        keep_att.start()
        att_copy.start()

    def attend(query, key, value, outcome):
        pair = 2 * HD
        first = lax.broadcasted_iota(jnp.int32, (length, pair), 1) < HD
        zero = jnp.zeros((length, pair), BF16)
        one = jnp.ones((length, pair), BF16)
        for p in range(width // pair):
            here = slice(p * pair, (p + 1) * pair)
            k, v = key[:, here], value[:, here]
            k_two = jnp.concatenate([jnp.where(first, k, zero), jnp.where(first, zero, k)], axis=0)
            v_two = jnp.concatenate(
                [
                    jnp.concatenate(
                        [jnp.where(first, v, zero), jnp.where(first, one, zero)], axis=1
                    ),
                    jnp.concatenate(
                        [jnp.where(first, zero, v), jnp.where(first, zero, one)], axis=1
                    ),
                ],
                axis=0,
            )
            scores = dot_nt(query[:, here], k_two)
            left, right = scores[:, :length], scores[:, length:]
            left = jnp.exp2((left - jnp.max(left, axis=1, keepdims=True)) * EXPONENT).astype(BF16)
            right = jnp.exp2((right - jnp.max(right, axis=1, keepdims=True)) * EXPONENT).astype(
                BF16
            )
            both = dot(jnp.concatenate([left, right], axis=1), v_two)
            outcome[:, here] = (both[:, :pair] / both[:, pair:]).astype(BF16)

    rows = pl.ds(pl.multiple_of(sequence * taken, 16), taken)

    @pl.when(turn == 0)
    def _():
        tokens_here = tokens[...]
        projected = dot(tokens_here, qkv[0])
        query = (projected[:, :width] + biases[0]).astype(BF16)
        key = projected[:, width : 2 * width].astype(BF16)
        value = (projected[:, 2 * width :] + biases[2]).astype(BF16)
        keys[...] = key
        values[...] = value
        attend(query, key, value, attended)

        spread = jnp.broadcast_to(places[pl.ds(sequence, 1), :], (length, places.shape[1]))
        column = lax.broadcasted_iota(jnp.int32, spread.shape, 1).astype(F32)
        hit = spread == lax.broadcasted_iota(jnp.int32, spread.shape, 0)
        earliest = jnp.min(jnp.where(hit, column, 1e6), axis=1, keepdims=True)
        pick = jnp.where(column == earliest, 1.0, 0.0).T[:taken].astype(BF16)
        picks[...] = pick
        tokens_low = dot(pick, tokens_here).astype(BF16)
        picked_tokens[...] = tokens_low
        picked_grad[...] = dot(pick, out_grad[...]).astype(BF16)
        picked_q[...] = dot(pick, query).astype(BF16)
        kept_tokens[rows, :] = tokens_low
        kept_picks[rows, :] = pick
        kept_att[rows, :] = dot(pick, attended[...]).astype(BF16)

    @pl.when((turn == 1) & (sequence < LOCAL))
    def _():
        projected = dot(tokens[...], qkv[1])
        query = (projected[:, :width] + biases[1]).astype(BF16)
        key = projected[:, width : 2 * width].astype(BF16)
        value = (projected[:, 2 * width :] + biases[3]).astype(BF16)
        keys[...] = key
        values[...] = value
        attend(query, key, value, attended_local)
        pick = kept_picks[rows, :]
        picked_q[...] = dot(pick, query).astype(BF16)
        kept_local[pl.ds(pl.multiple_of(sequence % LOCAL * taken, 16), taken), :] = dot(
            pick, attended_local[...]
        ).astype(BF16)

    @pl.when((turn == 1) & (sequence >= LOCAL))
    def _():
        projected = dot(tokens[...], qkv[1, :, width:])
        keys[...] = projected[:, :width].astype(BF16)
        values[...] = (projected[:, width:] + biases[3]).astype(BF16)
        picked_q[...] = (dot(kept_tokens[rows, :], qkv[1, :, :width]) + biases[1]).astype(BF16)

    @pl.when(step == 2 * sequences - 1)
    def _():
        keep_local.start()
        for index in (0, 3, 4, 5, 6):
            fetches[index].move("end")
        bias_copies[2].wait_recv()
        for fetch in fetches:
            for hop in range(PIECES):
                fetch.out(hop).wait_send()
        for copy in bias_copies:
            copy.wait_send()
        att_copy.wait()
        keep_out.wait()
        keep_qkv.wait()
        keep_att.wait()
        keep_local.wait()


def attention(
    tokens, out_grad, positions, w_query, w_key, w_value, w_out, w_up, w_down, b_query, b_value, b_up, taken
):
    rows, model = tokens.shape
    sequences = positions.shape[0]
    length = rows // sequences
    width = w_query.shape[1]
    shape = jax.ShapeDtypeStruct
    slots = sequences * taken

    def both(count, columns):
        return pl.BlockSpec((count, columns), lambda s: (s % sequences, s // sequences))

    def once(count, columns):
        return pl.BlockSpec((count, columns), lambda s: (jnp.minimum(s, sequences - 1), 0))

    def again(count, columns):
        return pl.BlockSpec((count, columns), lambda s: (s % sequences, 0))

    anywhere = pl.BlockSpec(memory_space=pl.ANY)
    dma = pltpu.SemaphoreType.DMA
    return pl.pallas_call(
        attention_body,
        grid=(2 * sequences,),
        in_specs=[
            again(length, model),
            once(length, model),
            pl.BlockSpec(positions.shape, lambda s: (0, 0)),
        ]
        + [anywhere] * 6
        + [vector_spec(array) for array in (b_query, b_value, b_up)],
        out_specs=[
            once(length, width),
            pl.BlockSpec((length, width), lambda s: (jnp.clip(s - sequences, 0, LOCAL - 1), 0)),
            both(length, width),
            both(length, width),
            both(taken, width),
            once(taken, model),
            once(taken, model),
            once(taken, length),
        ]
        + [anywhere] * 6,
        out_shape=[
            shape((rows, width), BF16),
            shape((LOCAL * length, width), BF16),
            shape((rows, 2 * width), BF16),
            shape((rows, 2 * width), BF16),
            shape((slots, 2 * width), BF16),
            shape((slots, model), BF16),
            shape((slots, model), BF16),
            shape((slots, length), BF16),
            shape((slots, 2 * width), BF16),
            shape((2, model, 3 * width), BF16),
            shape((2 * width, model), BF16),
            shape(w_up.shape, BF16),
            shape(w_down.shape, BF16),
            shape((1, w_up.shape[1]), F32),
        ],
        scratch_shapes=[
            pltpu.VMEM((2, model, 3 * width), BF16),
            pltpu.VMEM((4, 1, width), F32),
            pltpu.VMEM((1, w_up.shape[1]), F32),
            pltpu.VMEM((slots, model), BF16),
            pltpu.VMEM((slots, length), BF16),
            pltpu.VMEM((slots, width), BF16),
            pltpu.VMEM((LOCAL * taken, width), BF16),
            pltpu.VMEM((sequences, -(-positions.shape[1] // 128) * 128), jnp.int32),
            dma((7,)),
            dma((7, PIECES)),
            dma((7, PIECES)),
            dma((2, 3)),
            dma((2,)),
        ],
        compiler_params=pltpu.CompilerParams(
            vmem_limit_bytes=VMEM_BYTES, collective_id=0, has_side_effects=True
        ),
        cost_estimate=pl.CostEstimate(
            flops=int(rows * width * (10 * model + 16 * length)),
            bytes_accessed=rows * model * 12,
            transcendentals=rows * length * width // HD,
        ),
        name="attention",
    )(tokens, out_grad, positions, w_query, w_key, w_value, w_out, w_up, w_down, b_query, b_value, b_up)


def gelu_share(hidden):
    return 0.5 * (1.0 + lax.erf(hidden * ROOT_HALF))


def marked_body(
    late,
    tokens,
    picked_att,
    upstream,
    w_out,
    w_up_own_hbm,
    w_up_peer_hbm,
    w_down_own_hbm,
    w_down_peer_hbm,
    b_up_peer,
    b_up,
    b_out,
    gain_one,
    shift_one,
    b_down,
    gain_two,
    attended,
    back_one_out,
    attended_grad,
    grad_ff_hbm,
    grad_w_out,
    vectors,
    attended_peer,
    w_up,
    w_down,
    grad_ff,
    slope,
    active,
    load_sems,
    store_sems,
    att_sems,
):
    model = tokens.shape[1]
    width = model // 2
    half = w_up.shape[2]
    loads = [
        pltpu.make_async_copy(source, target, load_sems.at[i])
        for i, (source, target) in enumerate(
            (
                (w_up_own_hbm, w_up.at[0]),
                (w_down_own_hbm, w_down.at[0]),
                (w_up_peer_hbm, w_up.at[1]),
                (w_down_peer_hbm, w_down.at[1]),
            )
        )
    ]
    for load in loads:
        load.start()
    across = {"tensor": 1 - lax.axis_index("tensor")}
    greet((across,))
    share = remote(
        attended.at[pl.ds(attended.shape[0] - attended_peer.shape[0] - late, attended_peer.shape[0])],
        attended_peer,
        att_sems.at[0],
        att_sems.at[1],
        across,
    )
    share.start()

    count = tokens.shape[0] // 2
    split = (slice(0, count), slice(count, 2 * count))
    ones = [
        norm_parts(
            tokens[r, :].astype(F32) + dot(picked_att[r, :], w_out[...]) + row(b_out)
        )
        for r in split
    ]
    layers = [normed * row(gain_one) + row(shift_one) for normed, _ in ones]
    lows = [layer.astype(BF16) for layer in layers]
    sums = [layer + row(b_down) for layer in layers]
    for part in range(2):
        loads[2 * part].wait()
        bias = b_up_peer[...] if part else row(b_up)
        for i, r in enumerate(split):
            hidden = dot(lows[i], w_up[part]) + bias
            gate = gelu_share(hidden)
            act = (hidden * gate).astype(BF16)
            slope[part, r, :] = gate + hidden * jnp.exp(-0.5 * hidden * hidden) * DENSITY
            if part == 0:
                active[r, :] = act
            if i == 0:
                loads[2 * part + 1].wait()
            sums[i] = sums[i] + dot(act, w_down[part])
    twos = [norm_parts(summed) for summed in sums]
    ups = [upstream[r, :].astype(F32) for r in split]
    backs = [
        norm_back(up, normed, inverse, row(gain_two)) for up, (normed, inverse) in zip(ups, twos)
    ]
    back_lows = [back.astype(BF16) for back in backs]
    layer_low = jnp.concatenate(lows, axis=0)
    back_low = jnp.concatenate(back_lows, axis=0)
    layer_grads = list(backs)
    stores = [
        pltpu.make_async_copy(
            grad_ff.at[pl.ds(i * half, half)], grad_ff_hbm.at[pl.ds(i * half, half)], store_sems.at[i]
        )
        for i in range(2)
    ]
    grad_ff[half : 2 * half, :] = dot_tn(active[...], back_low).astype(BF16)
    stores[1].start()
    for part in range(2):
        hidden_grads = []
        for i, r in enumerate(split):
            hidden_grad = (dot_nt(back_lows[i], w_down[part]) * slope[part, r, :]).astype(BF16)
            layer_grads[i] = layer_grads[i] + dot_nt(hidden_grad, w_up[part])
            hidden_grads.append(hidden_grad)
        if part == 0:
            hidden_grad = jnp.concatenate(hidden_grads, axis=0)
            grad_b_up = row_sum(hidden_grad.astype(F32))
            for c in range(0, half, model):
                grad_ff[c : c + model, :] = dot_tn(layer_low, hidden_grad[:, c : c + model]).astype(
                    BF16
                )
            stores[0].start()
    back_ones = [
        norm_back(grad, normed, inverse, row(gain_one))
        for grad, (normed, inverse) in zip(layer_grads, ones)
    ]
    back_one_low = jnp.concatenate([back.astype(BF16) for back in back_ones], axis=0)
    for r, back in zip(split, back_ones):
        back_one_out[r, :] = back
    grad_w_out[...] = dot_tn(picked_att[:, :width], back_one_low).astype(BF16)
    attended_grad[...] = dot_nt(back_one_low, w_out[...]).astype(BF16)

    def total(pieces):
        return row_sum(pieces[0]) + row_sum(pieces[1])

    vectors[...] = jnp.concatenate(
        [
            total(back_ones),
            total([grad * normed for grad, (normed, _) in zip(layer_grads, ones)]),
            total(layer_grads),
            total(backs),
            total([up * normed for up, (normed, _) in zip(ups, twos)]),
            total(ups),
        ]
        + [grad_b_up[:, c : c + model] for c in range(0, half, model)],
        axis=0,
    )
    for store in stores:
        store.wait()
    share.wait()


def marked_rows(
    picked_tokens,
    picked_att,
    picked_grad,
    out_all,
    w_up,
    up_peer,
    w_down,
    down_peer,
    b_up_peer,
    vectors,
    attended,
    early,
    late,
    chips,
):
    rows, model = picked_tokens.shape
    width = model // 2
    half = w_up.shape[1]
    shape = jax.ShapeDtypeStruct
    inside = pl.BlockSpec(memory_space=pltpu.VMEM)
    anywhere = pl.BlockSpec(memory_space=pl.ANY)
    dma = pltpu.SemaphoreType.DMA
    return pl.pallas_call(
        functools.partial(marked_body, late),
        in_specs=[inside] * 4 + [anywhere] * 4 + [inside] * (1 + len(vectors)) + [anywhere],
        out_specs=[inside, inside, anywhere, inside, inside, anywhere],
        out_shape=[
            shape((rows, model), F32),
            shape((rows, 2 * width), BF16),
            shape((padded_rows(2 * half, chips, FF_WAYS), model), BF16),
            shape((width, model), BF16),
            shape((6 + half // model, model), F32),
            shape((early, width), BF16),
        ],
        scratch_shapes=[
            pltpu.VMEM((2, model, half), BF16),
            pltpu.VMEM((2, half, model), BF16),
            pltpu.VMEM((2 * half, model), BF16),
            pltpu.VMEM((2, rows, half), F32),
            pltpu.VMEM((rows, half), BF16),
            dma((4,)),
            dma((2,)),
            dma((2,)),
        ],
        compiler_params=pltpu.CompilerParams(
            vmem_limit_bytes=VMEM_BYTES, collective_id=3, has_side_effects=True
        ),
        cost_estimate=pl.CostEstimate(
            flops=int(rows * model * (2 * half * 10 + 2 * width * 5)),
            bytes_accessed=6 * model * half * 2,
            transcendentals=rows * half * 4,
        ),
        name="marked",
    )(
        picked_tokens,
        picked_att,
        picked_grad,
        out_all,
        w_up,
        up_peer,
        w_down,
        down_peer,
        b_up_peer,
        *vectors,
        attended,
    )


class Ring:
    def __init__(self, chips, share, ways):
        self.chips, self.ways, self.count = chips, ways, share // (ways * chips)
        self.share = share
        dp = lax.axis_index("dp")
        self.core, chip = dp % 2, dp // 2
        self.place = self.at(chip)
        self.mate = {"dp": flipped(dp, 1)}
        self.up = {"dp": self.device(self.place + 1)}
        self.down = {"dp": self.device(self.place + chips - 1)}

    def at(self, chip):
        high, low = chip // 2, chip % 2
        return (1 - low) * high + low * (self.chips - 1 - high)

    def device(self, place):
        place = place % self.chips
        back = place // (self.chips // 2)
        chip = (1 - back) * 2 * place + back * (2 * (self.chips - 1 - place) + 1)
        return 2 * chip + self.core

    def neighbours(self):
        return self.up, self.down, self.mate

    def onward(self, way):
        return (self.up, self.down)[way % 2]

    def segment(self, way, step):
        sign = 1 - 2 * (way % 2)
        return (self.place - sign * step + 2 * self.chips) % self.chips

    def rows(self, way, segment):
        return pl.ds(pl.multiple_of((way * self.chips + segment) * self.count, 16), self.count)

    def final_rows(self, way, segment, core):
        start = core * self.share + (way * self.chips + segment) * self.count
        return pl.ds(pl.multiple_of(start, 16), self.count)


class Reduce:
    def __init__(self, ring, source, total, other, slots, core_sems, sems):
        self.ring, self.source, self.total, self.other = ring, source, total, other
        self.slots, self.core_sems, self.sems = slots, core_sems, sems

    def _core(self):
        ring = self.ring
        give = pl.ds(pl.multiple_of((1 - ring.core) * ring.share, 16), ring.share)
        keep = pl.ds(pl.multiple_of(ring.core * ring.share, 16), ring.share)
        return (
            remote(
                self.source.at[give],
                self.other,
                self.core_sems.at[0],
                self.core_sems.at[1],
                ring.mate,
            ),
            pltpu.make_async_copy(self.source.at[keep], self.total, self.core_sems.at[2]),
        )

    def begin(self):
        given, kept = self._core()
        given.start()
        kept.start()

    def join(self):
        given, kept = self._core()
        kept.wait()
        given.wait()
        self.total[...] += self.other[...]

    def _copy(self, way, step):
        ring = self.ring
        return remote(
            self.total.at[ring.rows(way, ring.segment(way, step))],
            self.slots.at[way, step],
            self.sems.at[0, way, step],
            self.sems.at[1, way, step],
            ring.onward(way),
        )

    def event(self, step, ways):
        ring = self.ring

        @pl.when(step > 0)
        def _():
            for way in ways:
                self._copy(way, step - 1).wait()
                here = ring.rows(way, ring.segment(way, step))
                self.total[here, :] += self.slots[way, step - 1]

        @pl.when(step < ring.chips - 1)
        def _():
            for way in ways:
                self._copy(way, step).start()

    def done_segment(self, way):
        return self.ring.segment(way, self.ring.chips - 1)


class Gather:
    def __init__(self, ring, firsts, held, out, store_sems, sems, mate_sems):
        self.ring, self.firsts, self.held, self.out = ring, firsts, held, out
        self.store_sems, self.sems, self.mate_sems = store_sems, sems, mate_sems

    def _rows(self, way, step, core):
        ring, sign = self.ring, 1 - 2 * (way % 2)
        segment = (ring.place + sign - sign * step + 2 * ring.chips) % ring.chips
        return ring.final_rows(way, segment, core)

    def _store(self, way, step, core, which):
        rows = self._rows(way, step, core)
        return pltpu.make_async_copy(
            self.held.at[rows], self.out.at[rows], self.store_sems.at[which, way, step]
        )

    def _own(self, way, step):
        return self._store(way, step, self.ring.core, 0)

    def _mates(self, way, step):
        return self._store(way, step, 1 - self.ring.core, 1)

    def _send(self, way, step):
        here = self.held.at[self._rows(way, step, self.ring.core)]
        return remote(
            here, here, self.sems.at[0, way, step], self.sems.at[1, way, step], self.ring.onward(way)
        )

    def _arrive(self, way, step):
        here = self.held.at[self._rows(way, step + 1, self.ring.core)]
        return remote(
            here, here, self.sems.at[0, way, step], self.sems.at[1, way, step], self.ring.onward(way)
        )

    def _mate(self, way, step, core):
        here = self.held.at[self._rows(way, step, core)]
        return remote(
            here,
            here,
            self.mate_sems.at[0, way, step],
            self.mate_sems.at[1, way, step],
            self.ring.mate,
        )

    def _pass_on(self, step, ways):
        for way in ways:

            @pl.when(step < self.ring.chips - 1)
            def _():
                self._send(way, step).start()

            self._mate(way, step, self.ring.core).start()
            self._own(way, step).start()

    def begin(self, ways):
        for way in ways:
            self.held[self._rows(way, 0, self.ring.core), :] = self.firsts[way]
        self._pass_on(0, ways)

    def event(self, step, ways):
        for way in ways:
            self._arrive(way, step - 1).wait_recv()
        self._pass_on(step, ways)
        for way in ways:
            self._mate(way, step - 1, 1 - self.ring.core).wait_recv()
            self._mates(way, step - 1).start()

    def finish(self):
        last = self.ring.chips - 1
        ways = range(self.ring.ways)
        for way in ways:
            self._mate(way, last, 1 - self.ring.core).wait_recv()
            self._mates(way, last).start()

        def rest(step, carry):
            for way in ways:

                @pl.when(step < last)
                def _():
                    self._send(way, step).wait_send()

                self._mate(way, step, self.ring.core).wait_send()
                self._own(way, step).wait()
                self._mates(way, step).wait()
            return carry

        lax.fori_loop(0, self.ring.chips, rest, 0)


def backward_body(
    chips,
    tokens,
    keys,
    values,
    queries,
    grads,
    back_one,
    picked_tokens,
    qkv_all,
    grad_w_out,
    vectors_in,
    grad_ff,
    attended,
    d_own,
    d_peer,
    extra_out,
    grads_rest,
    vectors,
    reduced,
    attended_peer,
    query_grads,
    sums,
    total,
    other,
    slots,
    core_sems,
    ring_sems,
    att_sems,
):
    step = pl.program_id(0)
    last = pl.num_programs(0) - 1
    model = tokens.shape[1]
    width = keys.shape[1] // 2
    taken = queries.shape[0]
    factor = HD**-0.5
    pair = 2 * HD
    ring = Ring(chips, total.shape[0], FF_WAYS)
    reduction = Reduce(ring, grad_ff, total, other, slots, core_sems, ring_sems)
    across = {"tensor": 1 - lax.axis_index("tensor")}
    shared_rows = attended_peer.shape[0]
    share = remote(
        attended.at[pl.ds(attended.shape[0] - shared_rows, shared_rows)],
        attended_peer,
        att_sems.at[0],
        att_sems.at[1],
        across,
    )

    @pl.when(step == 0)
    def _():
        sums[...] = jnp.zeros_like(sums)
        vectors[...] = jnp.zeros_like(vectors)
        greet(ring.neighbours() + (across,))
        reduction.begin()
        share.start()

    @pl.when(step == 1)
    def _():
        reduction.join()

    @pl.when(step > 0)
    def _():
        reduction.event(step - 1, (0, 1))

    first = lax.broadcasted_iota(jnp.int32, (taken, pair), 1) < HD
    zero = jnp.zeros((taken, pair), BF16)

    def stacked(block):
        return jnp.concatenate(
            [jnp.where(first, block, zero), jnp.where(first, zero, block)], axis=0
        )

    d_query, d_key, d_value = [], [], []
    for half in range(2):
        if half == 1:

            @pl.when(step > 0)
            def _():
                reduction.event(step - 1, (2, 3))

        starts = [half * width + p * pair for p in range(width // pair)]
        pieces = [
            (
                keys[:, c : c + pair],
                values[:, c : c + pair],
                stacked(queries[:, c : c + pair]),
                stacked(grads[:, c : c + pair]),
            )
            for c in starts
        ]
        scores = [dot_nt(k, q) for k, v, q, g in pieces]
        weights_grads = [dot_nt(v, g) for k, v, q, g in pieces]
        weights_low, scores_grads = [], []
        for score, weights_grad in zip(scores, weights_grads):
            grown = jnp.exp2((score - jnp.max(score, axis=0, keepdims=True)) * EXPONENT)
            weights = grown * (1.0 / jnp.sum(grown, axis=0, keepdims=True))
            inner = jnp.sum(weights * weights_grad, axis=0, keepdims=True)
            weights_low.append(weights.astype(BF16))
            scores_grads.append((weights * (weights_grad - inner)).astype(BF16))
        for weights, scores_grad, (k, v, q, g) in zip(weights_low, scores_grads, pieces):
            d_value.append(dot(weights, g).astype(BF16))
            d_key.append((dot(scores_grad, q) * factor).astype(BF16))
            split = dot_tn(scores_grad, k) * factor
            d_query.append(jnp.where(first, split[:taken], split[taken:]).astype(BF16))
    half = len(d_key) // 2
    own = jnp.concatenate(d_key[:half] + d_value[:half], axis=1)
    d_own[...] = own
    d_peer[...] = jnp.concatenate(d_key[half:] + d_value[half:], axis=1)
    query_own = jnp.concatenate(d_query[:half], axis=1)
    query_peer = jnp.concatenate(d_query[half:], axis=1)
    extra_out[...] = (
        back_one[...]
        + dot_nt(query_own, qkv_all[0, :, :width])
        + dot_nt(query_peer, qkv_all[1, :, :width])
    )
    query_grads[pl.ds(pl.multiple_of(step * taken, taken), taken), :] = query_own
    sums[...] += dot_tn(tokens[...], own)
    vectors[8:9, :width] += row_sum(query_own.astype(F32))
    vectors[8:9, width:] += row_sum(own[:, width:].astype(F32))

    @pl.when(step == last)
    def _():
        grads_rest[:model, :] = sums[...].astype(BF16)
        query_total = dot_tn(picked_tokens[...], query_grads[...]).astype(BF16)
        for c in range(2):
            grads_rest[model : model + width, c * width : (c + 1) * width] = query_total[
                c * width : (c + 1) * width
            ]
        grads_rest[model + width : model + 2 * width, :] = grad_w_out[...]
        vectors[:8, :] = vectors_in[...]

        def rest(event, carry):
            reduction.event(event, range(FF_WAYS))
            return carry

        lax.fori_loop(last, chips, rest, 0)
        for way in range(FF_WAYS):
            reduced[way] = total[ring.rows(way, reduction.done_segment(way)), :]
        share.wait()


def attention_back(
    tokens,
    keys,
    values,
    queries,
    grads,
    back_one,
    picked_tokens,
    qkv_all,
    grad_w_out,
    vectors,
    grad_ff,
    attended,
    late,
    sequences,
    chips,
):
    rows, model = tokens.shape
    length = rows // sequences
    width = keys.shape[1] // 2
    slots = queries.shape[0]
    taken = slots // sequences
    share = grad_ff.shape[0] // 2
    rest_rows = padded_rows(model + 2 * width, chips, 2)
    shape = jax.ShapeDtypeStruct

    def fixed(array_shape):
        return pl.BlockSpec(array_shape, lambda i: (0,) * len(array_shape))

    piece = (FF_WAYS, share // (FF_WAYS * chips), model)
    return pl.pallas_call(
        functools.partial(backward_body, chips),
        grid=(sequences,),
        in_specs=[rows_spec(length, model)]
        + [rows_spec(length, 2 * width)] * 2
        + [rows_spec(taken, 2 * width)] * 2
        + [rows_spec(taken, model)]
        + [
            whole_spec(picked_tokens),
            pl.BlockSpec(qkv_all.shape, lambda i: (0, 0, 0), pipeline_mode=pl.Buffered(1)),
            whole_spec(grad_w_out),
            whole_spec(vectors),
            pl.BlockSpec(memory_space=pl.ANY),
            pl.BlockSpec(memory_space=pl.ANY),
        ],
        out_specs=[
            rows_spec(length, 2 * width),
            rows_spec(length, 2 * width),
            rows_spec(taken, model),
            fixed((rest_rows, model)),
            fixed((16, model)),
            fixed(piece),
            pl.BlockSpec(memory_space=pl.ANY),
        ],
        out_shape=[
            shape((rows, 2 * width), BF16),
            shape((rows, 2 * width), BF16),
            shape((slots, model), F32),
            shape((rest_rows, model), BF16),
            shape((16, model), F32),
            shape(piece, BF16),
            shape((late, width), BF16),
        ],
        scratch_shapes=[
            pltpu.VMEM((slots, width), BF16),
            pltpu.VMEM((model, 2 * width), F32),
            pltpu.VMEM((share, model), BF16),
            pltpu.VMEM((share, model), BF16),
            pltpu.VMEM((FF_WAYS, chips - 1) + piece[1:], BF16),
            pltpu.SemaphoreType.DMA((3,)),
            pltpu.SemaphoreType.DMA((2, FF_WAYS, chips - 1)),
            pltpu.SemaphoreType.DMA((2,)),
        ],
        compiler_params=pltpu.CompilerParams(
            vmem_limit_bytes=VMEM_BYTES, collective_id=1, has_side_effects=True
        ),
        cost_estimate=pl.CostEstimate(
            flops=int(rows * model * 4 * 2 * width),
            bytes_accessed=rows * model * 14,
            transcendentals=0,
        ),
        name="attention_back",
    )(
        tokens,
        keys,
        values,
        queries,
        grads,
        back_one,
        picked_tokens,
        qkv_all,
        grad_w_out,
        vectors,
        grad_ff,
        attended,
    )


def padded_rows(rows, chips, ways):
    unit = 32 * ways * chips
    return -(-rows // unit) * unit


def finish_body(
    d_own,
    d_peer,
    extra,
    picks,
    qkv_all,
    layer_in,
    up_left,
    up_right,
    down,
    key_value,
    query,
    out,
    vectors,
    tokens_grad,
    layer_out,
    grad_w_up,
    grad_w_down,
    grad_w_key,
    grad_w_value,
    grad_w_query,
    grad_w_out,
    grad_b_out,
    grad_gain_one,
    grad_shift_one,
    grad_b_down,
    grad_gain_two,
    grad_shift_two,
    grad_b_up,
    grad_b_query,
    grad_b_value,
):
    @pl.when(pl.program_id(0) == 0)
    def _():
        singles = (
            grad_b_out,
            grad_gain_one,
            grad_shift_one,
            grad_b_down,
            grad_gain_two,
            grad_shift_two,
        )
        for i, single in enumerate(singles):
            single[...] = vectors[i : i + 1, :].reshape(-1)
        grad_b_up[...] = jnp.concatenate([vectors[6:7, :], vectors[7:8, :]], axis=1).reshape(-1)
        grad_b_query[...] = vectors[8:9, : grad_b_query.shape[0]].reshape(-1)
        grad_b_value[...] = vectors[8:9, grad_b_query.shape[0] :].reshape(-1)

    width = grad_w_key.shape[1]
    model = tokens_grad.shape[1]
    wide = extra[...]
    high = wide.astype(BF16)
    low = (wide - high.astype(F32)).astype(BF16)
    pick = picks[...]
    tokens_grad[...] = (
        dot_nt(d_own[...], qkv_all[0, :, width:])
        + dot_nt(d_peer[...], qkv_all[1, :, width:])
        + dot_tn(jnp.concatenate([pick, pick], axis=0), jnp.concatenate([high, low], axis=0))
    )
    layer_out[...] = layer_in[...]
    grad_w_up[:, :model] = up_left[...].astype(F32)
    grad_w_up[:, model:] = up_right[...].astype(F32)
    grad_w_down[...] = down[...].astype(F32)
    grad_w_key[...] = key_value[:, :width].astype(F32)
    grad_w_value[...] = key_value[:, width:].astype(F32)
    grad_w_query[...] = query[...].astype(F32)
    grad_w_out[...] = out[...].astype(F32)


def finish(
    d_own, d_peer, extra, picks, qkv_all, layer, sums_ff, sums_rest, vectors, half, sequences
):
    rows, model = d_own.shape
    length = rows // sequences
    width = model // 2
    taken = picks.shape[0] // sequences
    assert half == 2 * model and width % sequences == 0 and sequences % 2 == 0
    part = model // sequences
    shape = jax.ShapeDtypeStruct

    def block(count, columns, start, column=None):
        offset = start // count
        return pl.BlockSpec((count, columns), lambda i: (offset + i, 0))

    turns = sequences // 2
    counts = [model] * 6 + [half, width, width]
    return pl.pallas_call(
        finish_body,
        grid=(sequences,),
        in_specs=[
            rows_spec(length, model),
            rows_spec(length, model),
            rows_spec(taken, model),
            rows_spec(taken, length),
            pl.BlockSpec(qkv_all.shape, lambda i: (0, 0, 0), pipeline_mode=pl.Buffered(1)),
            rows_spec(length, model),
            block(part, model, 0),
            block(part, model, model),
            block(2 * part, model, half),
            block(part, model, 0),
            pl.BlockSpec((part, width), lambda i: (model // part + i % turns, i // turns)),
            block(width // sequences, model, model + width),
            whole_spec(vectors),
        ],
        out_specs=[
            rows_spec(length, model),
            rows_spec(length, model),
            rows_spec(part, half),
            rows_spec(2 * part, model),
            rows_spec(part, width),
            rows_spec(part, width),
            rows_spec(part, width),
            rows_spec(width // sequences, model),
        ]
        + [pl.BlockSpec((count,), lambda i: (0,)) for count in counts],
        out_shape=[
            shape((rows, model), F32),
            shape((rows, model), BF16),
            shape((model, half), F32),
            shape((half, model), F32),
            shape((model, width), F32),
            shape((model, width), F32),
            shape((model, width), F32),
            shape((width, model), F32),
        ]
        + [shape((count,), F32) for count in counts],
        compiler_params=params(),
        cost_estimate=pl.CostEstimate(
            flops=int(rows * model * 4 * 2 * width),
            bytes_accessed=rows * model * 16,
            transcendentals=0,
        ),
        name="finish",
    )(
        d_own,
        d_peer,
        extra,
        picks,
        qkv_all,
        layer,
        sums_ff,
        sums_ff,
        sums_ff,
        sums_rest,
        sums_rest,
        sums_rest,
        vectors,
    )


def dense_body(
    chips,
    levels,
    early,
    tokens,
    attended_own,
    attended_local,
    attended_early,
    attended_late,
    w_out,
    w_up_own,
    w_up_peer,
    w_down_own,
    w_down_peer,
    b_up_peer,
    b_up,
    b_out,
    gain_one,
    shift_one,
    b_down,
    gain_two,
    shift_two,
    reduced,
    grads_rest,
    vectors_in,
    layer_out,
    sums_ff,
    sums_rest,
    vectors,
    total,
    other,
    slots,
    last_pieces,
    held_ff,
    held_rest,
    exchanged,
    gained,
    core_sems,
    ring_sems,
    ff_keep_sems,
    ff_sems,
    ff_mate_sems,
    rest_keep_sems,
    rest_sems,
    rest_mate_sems,
    vector_sems,
):
    step = pl.program_id(0)
    steps = pl.num_programs(0)
    model = tokens.shape[1]
    dp = lax.axis_index("dp")
    ring = Ring(chips, total.shape[0], 2)
    ff_ring = Ring(chips, sums_ff.shape[0] // 2, FF_WAYS)
    reduction = Reduce(ring, grads_rest, total, other, slots, core_sems, ring_sems)
    gather_ff = Gather(
        ff_ring,
        reduced,
        held_ff,
        sums_ff,
        ff_keep_sems,
        ff_sems,
        ff_mate_sems,
    )
    gather_rest = Gather(
        ring,
        last_pieces,
        held_rest,
        sums_rest,
        rest_keep_sems,
        rest_sems,
        rest_mate_sems,
    )

    def exchange(level):
        return remote(
            exchanged.at[level],
            gained.at[level],
            vector_sems.at[0, level],
            vector_sems.at[1, level],
            {"dp": flipped(dp, 2**level)},
        )

    def vector_event(level):
        if level > 0:
            exchange(level - 1).wait()
            exchanged[level] = exchanged[level - 1] + gained[level - 1]
        if level < levels:
            exchange(level).start()
        else:
            vectors[...] = exchanged[level]

    def rest_event(event, way):
        @pl.when(event < chips)
        def _():
            reduction.event(event, (way,))

        @pl.when(event == chips - 1)
        def _():
            last_pieces[way] = total[ring.rows(way, reduction.done_segment(way)), :]
            gather_rest.begin((way,))

        @pl.when(event > chips - 1)
        def _():
            gather_rest.event(event - (chips - 1), (way,))

    def ff_event(way):
        @pl.when((step > 0) & (step < chips))
        def _():
            gather_ff.event(step, (way,))

    def point(index):
        ff_event((1, 0, 3, 2)[index])
        if index < 2:

            @pl.when(step > 0)
            def _():
                rest_event(2 * step - 1, index)

        else:
            rest_event(2 * step, index - 2)

    @pl.when(step == 0)
    def _():
        greet(ring.neighbours() + tuple({"dp": flipped(dp, 2**level)} for level in range(1, levels)))
        reduction.begin()
        gather_ff.begin(range(FF_WAYS))
        exchanged[0] = vectors_in[...]
        vector_event(0)

    point(0)

    for level in range(1, levels + 1):

        @pl.when(step == jnp.minimum(level, steps - 1))
        def _():
            vector_event(level)

    count = tokens.shape[0] // 2
    split = (slice(0, count), slice(count, 2 * count))

    def first_norm(r):
        attended_peer = jnp.where(
            step < LOCAL,
            attended_local[r, :],
            jnp.where(step < LOCAL + early, attended_early[r, :], attended_late[r, :]),
        )
        attended = jnp.concatenate([attended_own[r, :], attended_peer], axis=1)
        normed, _ = norm_parts(tokens[r, :].astype(F32) + dot(attended, w_out[...]) + row(b_out))
        return normed * row(gain_one) + row(shift_one)

    def forward(layer_low, w_up, w_down, bias):
        hidden = dot(layer_low, w_up[...]) + bias
        return dot((hidden * gelu_share(hidden)).astype(BF16), w_down[...])

    layers = [first_norm(r) for r in split]
    lows = [layer.astype(BF16) for layer in layers]
    sums = [layer + row(b_down) for layer in layers]
    sums[0] = sums[0] + forward(lows[0], w_up_own, w_down_own, row(b_up))
    point(1)
    sums[1] = sums[1] + forward(lows[1], w_up_own, w_down_own, row(b_up))

    @pl.when(step == 0)
    def _():
        reduction.join()

    point(2)
    sums[0] = sums[0] + forward(lows[0], w_up_peer, w_down_peer, b_up_peer[...])
    point(3)
    sums[1] = sums[1] + forward(lows[1], w_up_peer, w_down_peer, b_up_peer[...])
    for r, summed in zip(split, sums):
        normed, _ = norm_parts(summed)
        layer_out[r, :] = (normed * row(gain_two) + row(shift_two)).astype(BF16)

    @pl.when(step == steps - 1)
    def _():
        def more_ff(event, carry):
            gather_ff.event(event, range(FF_WAYS))
            return carry

        def more_rest(event, carry):
            rest_event(event, 0)
            rest_event(event, 1)
            return carry

        lax.fori_loop(steps, chips, more_ff, 0)
        lax.fori_loop(2 * steps - 1, 2 * chips - 1, more_rest, 0)
        gather_ff.finish()
        gather_rest.finish()


def dense_rows(
    tokens,
    attended_own,
    attended_local,
    attended_early,
    attended_late,
    w_out,
    w_up_own,
    w_up_peer,
    w_down_own,
    w_down_peer,
    b_up_peer,
    singles,
    reduced,
    grads_rest,
    vectors,
    sequences,
    chips,
):
    rows, model = tokens.shape
    half = w_up_own.shape[1]
    block = rows // sequences
    levels = (2 * chips).bit_length() - 1
    assert 2**levels == 2 * chips
    share = grads_rest.shape[0] // 2
    ff_rows = reduced.shape[0] * reduced.shape[1] * 2 * chips
    piece = (share // (2 * chips), model)
    shape = jax.ShapeDtypeStruct
    anywhere = pl.BlockSpec(memory_space=pl.ANY)
    arrays = (w_out, w_up_own, w_up_peer, w_down_own, w_down_peer, b_up_peer)
    early = attended_early.shape[0] // block
    late = attended_late.shape[0] // block
    dma = pltpu.SemaphoreType.DMA
    return pl.pallas_call(
        functools.partial(dense_body, chips, levels, early),
        grid=(sequences,),
        in_specs=[
            rows_spec(block, model),
            rows_spec(block, model // 2),
            pl.BlockSpec((block, model // 2), lambda i: (jnp.minimum(i, LOCAL - 1), 0)),
            pl.BlockSpec((block, model // 2), lambda i: (jnp.clip(i - LOCAL, 0, early - 1), 0)),
            pl.BlockSpec(
                (block, model // 2), lambda i: (jnp.clip(i - LOCAL - early, 0, late - 1), 0)
            ),
        ]
        + [whole_spec(array) for array in arrays]
        + [vector_spec(array) for array in singles]
        + [
            pl.BlockSpec(reduced.shape, lambda i: (0, 0, 0), pipeline_mode=pl.Buffered(1)),
            anywhere,
            whole_spec(vectors),
        ],
        out_specs=[
            rows_spec(block, model),
            anywhere,
            anywhere,
            pl.BlockSpec(vectors.shape, lambda i: (0, 0)),
        ],
        out_shape=[
            shape((rows, model), BF16),
            shape((ff_rows, model), BF16),
            shape(grads_rest.shape, BF16),
            shape(vectors.shape, F32),
        ],
        scratch_shapes=[
            pltpu.VMEM((share, model), BF16),
            pltpu.VMEM((share, model), BF16),
            pltpu.VMEM((2, chips - 1) + piece, BF16),
            pltpu.VMEM((2,) + piece, BF16),
            pltpu.VMEM((ff_rows, model), BF16),
            pltpu.VMEM(grads_rest.shape, BF16),
            pltpu.VMEM((levels + 1,) + vectors.shape, F32),
            pltpu.VMEM((levels,) + vectors.shape, F32),
            dma((3,)),
            dma((2, 2, chips - 1)),
            dma((2, FF_WAYS, chips)),
            dma((2, FF_WAYS, chips - 1)),
            dma((2, FF_WAYS, chips)),
            dma((2, 2, chips)),
            dma((2, 2, chips - 1)),
            dma((2, 2, chips)),
            dma((2, levels)),
        ],
        compiler_params=pltpu.CompilerParams(
            vmem_limit_bytes=VMEM_BYTES, collective_id=2, has_side_effects=True
        ),
        cost_estimate=pl.CostEstimate(
            flops=int(rows * model * (8 * half + 2 * model)),
            bytes_accessed=rows * model * 6,
            transcendentals=rows * half * 2,
        ),
        name="dense",
    )(
        tokens,
        attended_own,
        attended_local,
        attended_early,
        attended_late,
        *arrays,
        *singles,
        reduced,
        grads_rest,
        vectors,
    )


def on_device(
    chips,
    tokens,
    out_grad,
    positions,
    w_query,
    b_query,
    w_key,
    w_value,
    b_value,
    w_out,
    b_out,
    gain_one,
    shift_one,
    w_up,
    b_up,
    w_down,
    b_down,
    gain_two,
    shift_two,
):
    sequences, count = positions.shape
    half = w_up.shape[1]
    taken = -(-count // 16) * 16
    (
        attended,
        attended_local,
        keys,
        values,
        picked_q,
        picked_tokens,
        picked_grad,
        picks,
        picked_att,
        qkv_all,
        out_all,
        up_peer,
        down_peer,
        b_up_peer,
    ) = attention(
        tokens,
        out_grad,
        positions,
        w_query,
        w_key,
        w_value,
        w_out,
        w_up,
        w_down,
        b_query,
        b_value,
        b_up,
        taken,
    )
    length = tokens.shape[0] // sequences
    early = (sequences - LOCAL) // 3 * length
    late = tokens.shape[0] - LOCAL * length - early
    weights = (out_all, w_up, up_peer, w_down, down_peer, b_up_peer)
    singles = (b_up, b_out, gain_one, shift_one, b_down, gain_two)
    back_one, att_grad, grad_ff, grad_w_out, vectors, attended_early = marked_rows(
        picked_tokens, picked_att, picked_grad, *weights, singles, attended, early, late, chips
    )
    d_own, d_peer, extra, grads_rest, vectors, reduced, attended_late = attention_back(
        tokens,
        keys,
        values,
        picked_q,
        att_grad,
        back_one,
        picked_tokens,
        qkv_all,
        grad_w_out,
        vectors,
        grad_ff,
        attended,
        late,
        sequences,
        chips,
    )
    layer, sums_ff, sums_rest, vectors = dense_rows(
        tokens,
        attended,
        attended_local,
        attended_early,
        attended_late,
        *weights,
        singles + (shift_two,),
        reduced,
        grads_rest,
        vectors,
        sequences,
        chips,
    )
    (
        tokens_grad,
        layer_out,
        grad_w_up,
        grad_w_down,
        grad_w_key,
        grad_w_value,
        grad_w_query,
        grad_w_out,
        grad_b_out,
        grad_gain_one,
        grad_shift_one,
        grad_b_down,
        grad_gain_two,
        grad_shift_two,
        grad_b_up,
        grad_b_query,
        grad_b_value,
    ) = finish(
        d_own, d_peer, extra, picks, qkv_all, layer, sums_ff, sums_rest, vectors, half, sequences
    )
    return (
        layer_out,
        tokens_grad,
        grad_w_query,
        grad_b_query,
        grad_w_key,
        grad_w_value,
        grad_b_value,
        grad_w_out,
        grad_b_out,
        grad_gain_one,
        grad_shift_one,
        grad_w_up,
        grad_b_up,
        grad_w_down,
        grad_b_down,
        grad_gain_two,
        grad_shift_two,
    )


def solution(mesh):
    across = P("dp", None)
    columns, rows, split, copied = P(None, "tensor"), P("tensor", None), P("tensor"), P()
    in_specs = (
        across,
        across,
        across,
        columns,
        split,
        columns,
        columns,
        split,
        rows,
        copied,
        copied,
        copied,
        columns,
        split,
        rows,
        copied,
        copied,
        copied,
    )
    out_specs = (
        across,
        across,
        columns,
        split,
        columns,
        columns,
        split,
        rows,
        copied,
        copied,
        copied,
        columns,
        split,
        rows,
        copied,
        copied,
        copied,
    )
    return jax.shard_map(
        functools.partial(on_device, mesh.shape["dp"] // 2), mesh=mesh, in_specs=in_specs, out_specs=out_specs, check_vma=False
    )
```

```python
import functools
import math

import jax
import jax.numpy as jnp
from jax import lax
from jax.experimental import pallas as pl
from jax.experimental.pallas import tpu as pltpu
from jax.sharding import PartitionSpec as P

HD = 64
NORM_EPSILON = 1e-12
BF16 = jnp.bfloat16
F32 = jnp.float32
EXPONENT = HD**-0.5 * math.log2(math.e)
ROOT_HALF = 0.7071067811865476
DENSITY = 0.3989422804014327
VMEM_BYTES = 58 * 2**20
FF_WAYS = 4
LOCAL = 2


def dot(left, right):
    return jnp.dot(left, right, preferred_element_type=F32)


def dot_nt(left, right):
    return lax.dot_general(left, right, (((1,), (1,)), ((), ())), preferred_element_type=F32)


def dot_tn(left, right):
    return lax.dot_general(left, right, (((0,), (0,)), ((), ())), preferred_element_type=F32)


def norm_parts(summed):
    centred = summed - jnp.mean(summed, axis=-1, keepdims=True)
    inverse = lax.rsqrt(jnp.mean(centred * centred, axis=-1, keepdims=True) + NORM_EPSILON)
    return centred * inverse, inverse


def norm_back(upstream, normed, inverse, gain):
    scaled = upstream * gain
    return inverse * (
        scaled
        - jnp.mean(scaled, axis=-1, keepdims=True)
        - normed * jnp.mean(scaled * normed, axis=-1, keepdims=True)
    )


def row(vector):
    return vector[...].reshape(1, -1)


def row_sum(values):
    return jnp.sum(values, axis=0, keepdims=True)


def rows_spec(rows, width):
    return pl.BlockSpec((rows, width), lambda i: (i, 0))


def vector_spec(array):
    return pl.BlockSpec(array.shape, lambda i: (0,))


def whole_spec(array):
    return pl.BlockSpec(array.shape, lambda i: (0, 0), pipeline_mode=pl.Buffered(1))


def params():
    return pltpu.CompilerParams(vmem_limit_bytes=VMEM_BYTES)


def flipped(index, span):
    return index + span - 2 * span * ((index // span) % 2)


def remote(source, target, send, receive, device):
    return pltpu.make_async_remote_copy(
        src_ref=source,
        dst_ref=target,
        send_sem=send,
        recv_sem=receive,
        device_id=device,
        device_id_type=pl.DeviceIdType.MESH,
    )


def greet(devices):
    barrier = pltpu.get_barrier_semaphore()
    for device in devices:
        pl.semaphore_signal(barrier, inc=1, device_id=device, device_id_type=pl.DeviceIdType.MESH)
    pl.semaphore_wait(barrier, len(devices))


PIECES = 8


class Fetch:
    def __init__(self, source, target, send_sems, recv_sems, first, second):
        self.source, self.target = source, target
        self.send_sems, self.recv_sems = send_sems, recv_sems
        self.dp = lax.axis_index("dp")
        self.hops = ((0, 0), (first, 0), (second, 0), (second, first)) + tuple(
            (1, flips) for flips in (0, first, second, first + second)
        )

    def _copy(self, source, piece, hop):
        count = self.target.shape[0] // PIECES
        rows = pl.ds(pl.multiple_of(piece * count, 16), count)
        if hop:
            device = {"dp": flipped(self.dp, self.hops[hop][0])}
        else:
            device = {"tensor": 1 - lax.axis_index("tensor")}
        return remote(
            source.at[rows], self.target.at[rows], self.send_sems.at[hop], self.recv_sems.at[hop], device
        )

    def _piece(self, flips):
        piece = self.dp % PIECES
        for span in (4, 2, 1):
            if flips & span:
                piece = flipped(piece, span)
        return piece

    def out(self, hop):
        return self._copy(
            self.target if hop else self.source, self._piece(self.hops[hop][1]), hop
        )

    def into(self, hop):
        return self._copy(self.target, self._piece(self.hops[hop][0] | self.hops[hop][1]), hop)

    def move(self, what):
        if what == "x":
            self.out(0).start()
        if what == "z":
            self.into(0).wait_recv()
            for hop in (1, 2, 4):
                self.out(hop).start()
        if what == "y":
            self.into(1).wait_recv()
            for hop in (3, 5):
                self.out(hop).start()
        if what == "c":
            self.into(2).wait_recv()
            self.into(3).wait_recv()
            for hop in (6, 7):
                self.out(hop).start()
        if what == "end":
            for hop in (4, 5, 6, 7):
                self.into(hop).wait_recv()


def attention_body(
    tokens,
    out_grad,
    positions,
    w_query,
    w_key,
    w_value,
    w_out,
    w_up,
    w_down,
    b_query,
    b_value,
    b_up,
    attended,
    attended_local,
    keys,
    values,
    picked_q,
    picked_tokens,
    picked_grad,
    picks,
    picked_att,
    qkv_all,
    out_all,
    up_peer,
    down_peer,
    b_up_peer,
    qkv,
    biases,
    up_biases,
    kept_tokens,
    kept_picks,
    kept_att,
    kept_local,
    places,
    local_sems,
    send_sems,
    recv_sems,
    bias_sems,
    att_sems,
):
    step = pl.program_id(0)
    sequences = pl.num_programs(0) // 2
    sequence = step % sequences
    turn = step // sequences
    length = tokens.shape[0]
    width = keys.shape[1]
    model = tokens.shape[1]
    taken = picks.shape[0]
    dp = lax.axis_index("dp")
    across = {"tensor": 1 - lax.axis_index("tensor")}

    def halves(source, target):
        rows = target.shape[0] // 2
        return [(source.at[pl.ds(i * rows, rows)], target.at[pl.ds(i * rows, rows)]) for i in range(2)]

    pairs = (
        [(w_out, out_all.at[pl.ds(width, width)])]
        + halves(qkv.at[0], qkv.at[1])
        + halves(w_up, up_peer)
        + halves(w_down, down_peer)
    )
    fetches = [
        Fetch(source, target, send_sems.at[i], recv_sems.at[i], *((4, 2), (2, 4))[i % 2])
        for i, (source, target) in enumerate(pairs)
    ]
    bias_copies = [
        remote(source, target, bias_sems.at[0, i], bias_sems.at[1, i], across)
        for i, (source, target) in enumerate(
            (
                (biases.at[0], biases.at[1]),
                (biases.at[2], biases.at[3]),
                (up_biases, b_up_peer),
            )
        )
    ]

    far = pl.ds(LOCAL * taken, (sequences - LOCAL) * taken)
    att_copy = remote(
        kept_att.at[far],
        picked_att.at[far, pl.ds(width, width)],
        att_sems.at[0],
        att_sems.at[1],
        across,
    )

    loads = [
        pltpu.make_async_copy(weight, qkv.at[0, :, pl.ds(i * width, width)], local_sems.at[i])
        for i, weight in enumerate((w_query, w_key, w_value))
    ]
    keep_out = pltpu.make_async_copy(w_out, out_all.at[pl.ds(0, width)], local_sems.at[3])
    keep_qkv = pltpu.make_async_copy(qkv, qkv_all, local_sems.at[4])
    keep_att = pltpu.make_async_copy(kept_att, picked_att.at[:, pl.ds(0, width)], local_sems.at[5])
    keep_local = pltpu.make_async_copy(
        kept_local, picked_att.at[pl.ds(0, LOCAL * taken), pl.ds(width, width)], local_sems.at[6]
    )

    @pl.when(step == 0)
    def _():
        for load in loads:
            load.start()
        keep_out.start()
        places[...] = jnp.full(places.shape, -1, jnp.int32)
        places[:, : positions.shape[1]] = positions[...]
        biases[0] = row(b_query)
        biases[2] = row(b_value)
        up_biases[...] = row(b_up)
        greet((across,) + tuple({"dp": flipped(dp, span)} for span in (1, 2, 4)))
        fetches[0].move("x")
        for load in loads:
            load.wait()
        fetches[1].move("x")
        fetches[2].move("x")
        for copy in bias_copies:
            copy.start()

    moves = {
        1: [(3, "x")],
        2: [(0, "z"), (1, "z")],
        3: [(2, "z"), (4, "x")],
        4: [(3, "z"), (0, "y"), (1, "y"), (5, "x")],
        5: [(4, "z"), (2, "y"), (6, "x")],
        6: [(3, "y"), (0, "c"), (1, "c")],
        7: [(5, "z"), (6, "z"), (4, "y"), (2, "c")],
        8: [(1, "end"), (2, "end")],
        9: [(5, "y"), (6, "y"), (3, "c")],
        10: [(4, "c"), (5, "c")],
        14: [(6, "c")],
    }
    for when, made in moves.items():

        @pl.when(step == when)
        def _():
            for index, what in made:
                fetches[index].move(what)

    @pl.when(step == sequences)
    def _():
        bias_copies[0].wait_recv()
        bias_copies[1].wait_recv()
        keep_qkv.start()
        keep_att.start()
        att_copy.start()

    def attend(query, key, value, outcome):
        pair = 2 * HD
        first = lax.broadcasted_iota(jnp.int32, (length, pair), 1) < HD
        zero = jnp.zeros((length, pair), BF16)
        one = jnp.ones((length, pair), BF16)
        for p in range(width // pair):
            here = slice(p * pair, (p + 1) * pair)
            k, v = key[:, here], value[:, here]
            k_two = jnp.concatenate([jnp.where(first, k, zero), jnp.where(first, zero, k)], axis=0)
            v_two = jnp.concatenate(
                [
                    jnp.concatenate(
                        [jnp.where(first, v, zero), jnp.where(first, one, zero)], axis=1
                    ),
                    jnp.concatenate(
                        [jnp.where(first, zero, v), jnp.where(first, zero, one)], axis=1
                    ),
                ],
                axis=0,
            )
            scores = dot_nt(query[:, here], k_two)
            left, right = scores[:, :length], scores[:, length:]
            left = jnp.exp2((left - jnp.max(left, axis=1, keepdims=True)) * EXPONENT).astype(BF16)
            right = jnp.exp2((right - jnp.max(right, axis=1, keepdims=True)) * EXPONENT).astype(
                BF16
            )
            both = dot(jnp.concatenate([left, right], axis=1), v_two)
            outcome[:, here] = (both[:, :pair] / both[:, pair:]).astype(BF16)

    rows = pl.ds(pl.multiple_of(sequence * taken, 16), taken)

    @pl.when(turn == 0)
    def _():
        tokens_here = tokens[...]
        projected = dot(tokens_here, qkv[0])
        query = (projected[:, :width] + biases[0]).astype(BF16)
        key = projected[:, width : 2 * width].astype(BF16)
        value = (projected[:, 2 * width :] + biases[2]).astype(BF16)
        keys[...] = key
        values[...] = value
        attend(query, key, value, attended)

        spread = jnp.broadcast_to(places[pl.ds(sequence, 1), :], (length, places.shape[1]))
        column = lax.broadcasted_iota(jnp.int32, spread.shape, 1).astype(F32)
        hit = spread == lax.broadcasted_iota(jnp.int32, spread.shape, 0)
        earliest = jnp.min(jnp.where(hit, column, 1e6), axis=1, keepdims=True)
        pick = jnp.where(column == earliest, 1.0, 0.0).T[:taken].astype(BF16)
        picks[...] = pick
        tokens_low = dot(pick, tokens_here).astype(BF16)
        picked_tokens[...] = tokens_low
        picked_grad[...] = dot(pick, out_grad[...]).astype(BF16)
        picked_q[...] = dot(pick, query).astype(BF16)
        kept_tokens[rows, :] = tokens_low
        kept_picks[rows, :] = pick
        kept_att[rows, :] = dot(pick, attended[...]).astype(BF16)

    @pl.when((turn == 1) & (sequence < LOCAL))
    def _():
        projected = dot(tokens[...], qkv[1])
        query = (projected[:, :width] + biases[1]).astype(BF16)
        key = projected[:, width : 2 * width].astype(BF16)
        value = (projected[:, 2 * width :] + biases[3]).astype(BF16)
        keys[...] = key
        values[...] = value
        attend(query, key, value, attended_local)
        pick = kept_picks[rows, :]
        picked_q[...] = dot(pick, query).astype(BF16)
        kept_local[pl.ds(pl.multiple_of(sequence % LOCAL * taken, 16), taken), :] = dot(
            pick, attended_local[...]
        ).astype(BF16)

    @pl.when((turn == 1) & (sequence >= LOCAL))
    def _():
        projected = dot(tokens[...], qkv[1, :, width:])
        keys[...] = projected[:, :width].astype(BF16)
        values[...] = (projected[:, width:] + biases[3]).astype(BF16)
        picked_q[...] = (dot(kept_tokens[rows, :], qkv[1, :, :width]) + biases[1]).astype(BF16)

    @pl.when(step == 2 * sequences - 1)
    def _():
        keep_local.start()
        for index in (0, 3, 4, 5, 6):
            fetches[index].move("end")
        bias_copies[2].wait_recv()
        for fetch in fetches:
            for hop in range(PIECES):
                fetch.out(hop).wait_send()
        for copy in bias_copies:
            copy.wait_send()
        att_copy.wait()
        keep_out.wait()
        keep_qkv.wait()
        keep_att.wait()
        keep_local.wait()


def attention(
    tokens, out_grad, positions, w_query, w_key, w_value, w_out, w_up, w_down, b_query, b_value, b_up, taken
):
    rows, model = tokens.shape
    sequences = positions.shape[0]
    length = rows // sequences
    width = w_query.shape[1]
    shape = jax.ShapeDtypeStruct
    slots = sequences * taken

    def both(count, columns):
        return pl.BlockSpec((count, columns), lambda s: (s % sequences, s // sequences))

    def once(count, columns):
        return pl.BlockSpec((count, columns), lambda s: (jnp.minimum(s, sequences - 1), 0))

    def again(count, columns):
        return pl.BlockSpec((count, columns), lambda s: (s % sequences, 0))

    anywhere = pl.BlockSpec(memory_space=pl.ANY)
    dma = pltpu.SemaphoreType.DMA
    return pl.pallas_call(
        attention_body,
        grid=(2 * sequences,),
        in_specs=[
            again(length, model),
            once(length, model),
            pl.BlockSpec(positions.shape, lambda s: (0, 0)),
        ]
        + [anywhere] * 6
        + [vector_spec(array) for array in (b_query, b_value, b_up)],
        out_specs=[
            once(length, width),
            pl.BlockSpec((length, width), lambda s: (jnp.clip(s - sequences, 0, LOCAL - 1), 0)),
            both(length, width),
            both(length, width),
            both(taken, width),
            once(taken, model),
            once(taken, model),
            once(taken, length),
        ]
        + [anywhere] * 6,
        out_shape=[
            shape((rows, width), BF16),
            shape((LOCAL * length, width), BF16),
            shape((rows, 2 * width), BF16),
            shape((rows, 2 * width), BF16),
            shape((slots, 2 * width), BF16),
            shape((slots, model), BF16),
            shape((slots, model), BF16),
            shape((slots, length), BF16),
            shape((slots, 2 * width), BF16),
            shape((2, model, 3 * width), BF16),
            shape((2 * width, model), BF16),
            shape(w_up.shape, BF16),
            shape(w_down.shape, BF16),
            shape((1, w_up.shape[1]), F32),
        ],
        scratch_shapes=[
            pltpu.VMEM((2, model, 3 * width), BF16),
            pltpu.VMEM((4, 1, width), F32),
            pltpu.VMEM((1, w_up.shape[1]), F32),
            pltpu.VMEM((slots, model), BF16),
            pltpu.VMEM((slots, length), BF16),
            pltpu.VMEM((slots, width), BF16),
            pltpu.VMEM((LOCAL * taken, width), BF16),
            pltpu.VMEM((sequences, -(-positions.shape[1] // 128) * 128), jnp.int32),
            dma((7,)),
            dma((7, PIECES)),
            dma((7, PIECES)),
            dma((2, 3)),
            dma((2,)),
        ],
        compiler_params=pltpu.CompilerParams(
            vmem_limit_bytes=VMEM_BYTES, collective_id=0, has_side_effects=True
        ),
        cost_estimate=pl.CostEstimate(
            flops=int(rows * width * (10 * model + 16 * length)),
            bytes_accessed=rows * model * 12,
            transcendentals=rows * length * width // HD,
        ),
        name="attention",
    )(tokens, out_grad, positions, w_query, w_key, w_value, w_out, w_up, w_down, b_query, b_value, b_up)


def gelu_share(hidden):
    return 0.5 * (1.0 + lax.erf(hidden * ROOT_HALF))


def marked_body(
    late,
    tokens,
    picked_att,
    upstream,
    w_out,
    w_up_own_hbm,
    w_up_peer_hbm,
    w_down_own_hbm,
    w_down_peer_hbm,
    b_up_peer,
    b_up,
    b_out,
    gain_one,
    shift_one,
    b_down,
    gain_two,
    attended,
    back_one_out,
    attended_grad,
    grad_ff_hbm,
    grad_w_out,
    vectors,
    attended_peer,
    w_up,
    w_down,
    grad_ff,
    slope,
    active,
    load_sems,
    store_sems,
    att_sems,
):
    model = tokens.shape[1]
    width = model // 2
    half = w_up.shape[2]
    loads = [
        pltpu.make_async_copy(source, target, load_sems.at[i])
        for i, (source, target) in enumerate(
            (
                (w_up_own_hbm, w_up.at[0]),
                (w_down_own_hbm, w_down.at[0]),
                (w_up_peer_hbm, w_up.at[1]),
                (w_down_peer_hbm, w_down.at[1]),
            )
        )
    ]
    for load in loads:
        load.start()
    across = {"tensor": 1 - lax.axis_index("tensor")}
    share = remote(
        attended.at[pl.ds(attended.shape[0] - attended_peer.shape[0] - late, attended_peer.shape[0])],
        attended_peer,
        att_sems.at[0],
        att_sems.at[1],
        across,
    )
    count = tokens.shape[0] // 2
    split = (slice(0, count), slice(count, 2 * count))
    ones = [
        norm_parts(
            tokens[r, :].astype(F32) + dot(picked_att[r, :], w_out[...]) + row(b_out)
        )
        for r in split
    ]
    layers = [normed * row(gain_one) + row(shift_one) for normed, _ in ones]
    lows = [layer.astype(BF16) for layer in layers]
    sums = [layer + row(b_down) for layer in layers]
    greet((across,))
    share.start()
    for part in range(2):
        loads[2 * part].wait()
        bias = b_up_peer[...] if part else row(b_up)
        for i, r in enumerate(split):
            hidden = dot(lows[i], w_up[part]) + bias
            gate = gelu_share(hidden)
            act = (hidden * gate).astype(BF16)
            slope[part, r, :] = gate + hidden * jnp.exp(-0.5 * hidden * hidden) * DENSITY
            if part == 0:
                active[r, :] = act
            if i == 0:
                loads[2 * part + 1].wait()
            sums[i] = sums[i] + dot(act, w_down[part])
    twos = [norm_parts(summed) for summed in sums]
    ups = [upstream[r, :].astype(F32) for r in split]
    backs = [
        norm_back(up, normed, inverse, row(gain_two)) for up, (normed, inverse) in zip(ups, twos)
    ]
    back_lows = [back.astype(BF16) for back in backs]
    layer_low = jnp.concatenate(lows, axis=0)
    back_low = jnp.concatenate(back_lows, axis=0)
    layer_grads = list(backs)
    stores = [
        pltpu.make_async_copy(
            grad_ff.at[pl.ds(i * half, half)], grad_ff_hbm.at[pl.ds(i * half, half)], store_sems.at[i]
        )
        for i in range(2)
    ]
    grad_ff[half : 2 * half, :] = dot_tn(active[...], back_low).astype(BF16)
    stores[1].start()
    for part in range(2):
        hidden_grads = []
        for i, r in enumerate(split):
            hidden_grad = (dot_nt(back_lows[i], w_down[part]) * slope[part, r, :]).astype(BF16)
            layer_grads[i] = layer_grads[i] + dot_nt(hidden_grad, w_up[part])
            hidden_grads.append(hidden_grad)
        if part == 0:
            hidden_grad = jnp.concatenate(hidden_grads, axis=0)
            grad_b_up = row_sum(hidden_grad.astype(F32))
            for c in range(0, half, model):
                grad_ff[c : c + model, :] = dot_tn(layer_low, hidden_grad[:, c : c + model]).astype(
                    BF16
                )
            stores[0].start()
    back_ones = [
        norm_back(grad, normed, inverse, row(gain_one))
        for grad, (normed, inverse) in zip(layer_grads, ones)
    ]
    back_one_low = jnp.concatenate([back.astype(BF16) for back in back_ones], axis=0)
    for r, back in zip(split, back_ones):
        back_one_out[r, :] = back
    grad_w_out[...] = dot_tn(picked_att[:, :width], back_one_low).astype(BF16)
    attended_grad[...] = dot_nt(back_one_low, w_out[...]).astype(BF16)

    def total(pieces):
        return row_sum(pieces[0]) + row_sum(pieces[1])

    vectors[...] = jnp.concatenate(
        [
            total(back_ones),
            total([grad * normed for grad, (normed, _) in zip(layer_grads, ones)]),
            total(layer_grads),
            total(backs),
            total([up * normed for up, (normed, _) in zip(ups, twos)]),
            total(ups),
        ]
        + [grad_b_up[:, c : c + model] for c in range(0, half, model)],
        axis=0,
    )
    for store in stores:
        store.wait()
    share.wait()


def marked_rows(
    picked_tokens,
    picked_att,
    picked_grad,
    out_all,
    w_up,
    up_peer,
    w_down,
    down_peer,
    b_up_peer,
    vectors,
    attended,
    early,
    late,
    chips,
):
    rows, model = picked_tokens.shape
    width = model // 2
    half = w_up.shape[1]
    shape = jax.ShapeDtypeStruct
    inside = pl.BlockSpec(memory_space=pltpu.VMEM)
    anywhere = pl.BlockSpec(memory_space=pl.ANY)
    dma = pltpu.SemaphoreType.DMA
    return pl.pallas_call(
        functools.partial(marked_body, late),
        in_specs=[inside] * 4 + [anywhere] * 4 + [inside] * (1 + len(vectors)) + [anywhere],
        out_specs=[inside, inside, anywhere, inside, inside, anywhere],
        out_shape=[
            shape((rows, model), F32),
            shape((rows, 2 * width), BF16),
            shape((padded_rows(2 * half, chips, FF_WAYS), model), BF16),
            shape((width, model), BF16),
            shape((6 + half // model, model), F32),
            shape((early, width), BF16),
        ],
        scratch_shapes=[
            pltpu.VMEM((2, model, half), BF16),
            pltpu.VMEM((2, half, model), BF16),
            pltpu.VMEM((2 * half, model), BF16),
            pltpu.VMEM((2, rows, half), F32),
            pltpu.VMEM((rows, half), BF16),
            dma((4,)),
            dma((2,)),
            dma((2,)),
        ],
        compiler_params=pltpu.CompilerParams(
            vmem_limit_bytes=VMEM_BYTES, collective_id=3, has_side_effects=True
        ),
        cost_estimate=pl.CostEstimate(
            flops=int(rows * model * (2 * half * 10 + 2 * width * 5)),
            bytes_accessed=6 * model * half * 2,
            transcendentals=rows * half * 4,
        ),
        name="marked",
    )(
        picked_tokens,
        picked_att,
        picked_grad,
        out_all,
        w_up,
        up_peer,
        w_down,
        down_peer,
        b_up_peer,
        *vectors,
        attended,
    )


class Ring:
    def __init__(self, chips, share, ways):
        self.chips, self.ways, self.count = chips, ways, share // (ways * chips)
        self.share = share
        dp = lax.axis_index("dp")
        self.core, chip = dp % 2, dp // 2
        self.place = self.at(chip)
        self.mate = {"dp": flipped(dp, 1)}
        self.up = {"dp": self.device(self.place + 1)}
        self.down = {"dp": self.device(self.place + chips - 1)}

    def at(self, chip):
        high, low = chip // 2, chip % 2
        return (1 - low) * high + low * (self.chips - 1 - high)

    def device(self, place):
        place = place % self.chips
        back = place // (self.chips // 2)
        chip = (1 - back) * 2 * place + back * (2 * (self.chips - 1 - place) + 1)
        return 2 * chip + self.core

    def neighbours(self):
        return self.up, self.down, self.mate

    def onward(self, way):
        return (self.up, self.down)[way % 2]

    def segment(self, way, step):
        sign = 1 - 2 * (way % 2)
        return (self.place - sign * step + 2 * self.chips) % self.chips

    def rows(self, way, segment):
        return pl.ds(pl.multiple_of((way * self.chips + segment) * self.count, 16), self.count)

    def final_rows(self, way, segment, core):
        start = core * self.share + (way * self.chips + segment) * self.count
        return pl.ds(pl.multiple_of(start, 16), self.count)


class Reduce:
    def __init__(self, ring, source, total, other, slots, core_sems, sems):
        self.ring, self.source, self.total, self.other = ring, source, total, other
        self.slots, self.core_sems, self.sems = slots, core_sems, sems

    def _core(self):
        ring = self.ring
        give = pl.ds(pl.multiple_of((1 - ring.core) * ring.share, 16), ring.share)
        keep = pl.ds(pl.multiple_of(ring.core * ring.share, 16), ring.share)
        return (
            remote(
                self.source.at[give],
                self.other,
                self.core_sems.at[0],
                self.core_sems.at[1],
                ring.mate,
            ),
            pltpu.make_async_copy(self.source.at[keep], self.total, self.core_sems.at[2]),
        )

    def begin(self):
        given, kept = self._core()
        given.start()
        kept.start()

    def join(self):
        given, kept = self._core()
        kept.wait()
        given.wait()
        self.total[...] += self.other[...]

    def _copy(self, way, step):
        ring = self.ring
        return remote(
            self.total.at[ring.rows(way, ring.segment(way, step))],
            self.slots.at[way, step],
            self.sems.at[0, way, step],
            self.sems.at[1, way, step],
            ring.onward(way),
        )

    def event(self, step, ways):
        ring = self.ring

        @pl.when(step > 0)
        def _():
            for way in ways:
                self._copy(way, step - 1).wait()
                here = ring.rows(way, ring.segment(way, step))
                self.total[here, :] += self.slots[way, step - 1]

        @pl.when(step < ring.chips - 1)
        def _():
            for way in ways:
                self._copy(way, step).start()

    def done_segment(self, way):
        return self.ring.segment(way, self.ring.chips - 1)


class Gather:
    def __init__(self, ring, firsts, held, out, store_sems, sems, mate_sems):
        self.ring, self.firsts, self.held, self.out = ring, firsts, held, out
        self.store_sems, self.sems, self.mate_sems = store_sems, sems, mate_sems

    def _rows(self, way, step, core):
        ring, sign = self.ring, 1 - 2 * (way % 2)
        segment = (ring.place + sign - sign * step + 2 * ring.chips) % ring.chips
        return ring.final_rows(way, segment, core)

    def _store(self, way, step, core, which):
        rows = self._rows(way, step, core)
        return pltpu.make_async_copy(
            self.held.at[rows], self.out.at[rows], self.store_sems.at[which, way, step]
        )

    def _own(self, way, step):
        return self._store(way, step, self.ring.core, 0)

    def _mates(self, way, step):
        return self._store(way, step, 1 - self.ring.core, 1)

    def _send(self, way, step):
        here = self.held.at[self._rows(way, step, self.ring.core)]
        return remote(
            here, here, self.sems.at[0, way, step], self.sems.at[1, way, step], self.ring.onward(way)
        )

    def _arrive(self, way, step):
        here = self.held.at[self._rows(way, step + 1, self.ring.core)]
        return remote(
            here, here, self.sems.at[0, way, step], self.sems.at[1, way, step], self.ring.onward(way)
        )

    def _mate(self, way, step, core):
        here = self.held.at[self._rows(way, step, core)]
        return remote(
            here,
            here,
            self.mate_sems.at[0, way, step],
            self.mate_sems.at[1, way, step],
            self.ring.mate,
        )

    def _pass_on(self, step, ways):
        for way in ways:

            @pl.when(step < self.ring.chips - 1)
            def _():
                self._send(way, step).start()

            self._mate(way, step, self.ring.core).start()
            self._own(way, step).start()

    def begin(self, ways):
        for way in ways:
            self.held[self._rows(way, 0, self.ring.core), :] = self.firsts[way]
        self._pass_on(0, ways)

    def event(self, step, ways):
        for way in ways:
            self._arrive(way, step - 1).wait_recv()
        self._pass_on(step, ways)
        for way in ways:
            self._mate(way, step - 1, 1 - self.ring.core).wait_recv()
            self._mates(way, step - 1).start()

    def finish(self):
        last = self.ring.chips - 1
        ways = range(self.ring.ways)
        for way in ways:
            self._mate(way, last, 1 - self.ring.core).wait_recv()
            self._mates(way, last).start()

        def rest(step, carry):
            for way in ways:

                @pl.when(step < last)
                def _():
                    self._send(way, step).wait_send()

                self._mate(way, step, self.ring.core).wait_send()
                self._own(way, step).wait()
                self._mates(way, step).wait()
            return carry

        lax.fori_loop(0, self.ring.chips, rest, 0)


def backward_body(
    chips,
    tokens,
    keys,
    values,
    queries,
    grads,
    back_one,
    picked_tokens,
    qkv_all,
    grad_w_out,
    vectors_in,
    grad_ff,
    attended,
    d_own,
    d_peer,
    extra_out,
    grads_rest,
    vectors,
    reduced,
    attended_peer,
    query_grads,
    sums,
    total,
    other,
    slots,
    core_sems,
    ring_sems,
    att_sems,
):
    step = pl.program_id(0)
    last = pl.num_programs(0) - 1
    model = tokens.shape[1]
    width = keys.shape[1] // 2
    taken = queries.shape[0]
    factor = HD**-0.5
    pair = 2 * HD
    ring = Ring(chips, total.shape[0], FF_WAYS)
    reduction = Reduce(ring, grad_ff, total, other, slots, core_sems, ring_sems)
    across = {"tensor": 1 - lax.axis_index("tensor")}
    shared_rows = attended_peer.shape[0]
    share = remote(
        attended.at[pl.ds(attended.shape[0] - shared_rows, shared_rows)],
        attended_peer,
        att_sems.at[0],
        att_sems.at[1],
        across,
    )

    @pl.when(step == 0)
    def _():
        sums[...] = jnp.zeros_like(sums)
        vectors[...] = jnp.zeros_like(vectors)
        greet(ring.neighbours() + (across,))
        reduction.begin()
        share.start()

    @pl.when(step == 1)
    def _():
        reduction.join()

    @pl.when(step > 0)
    def _():
        reduction.event(step - 1, range(FF_WAYS))

    first = lax.broadcasted_iota(jnp.int32, (taken, pair), 1) < HD
    zero = jnp.zeros((taken, pair), BF16)

    def stacked(block):
        return jnp.concatenate(
            [jnp.where(first, block, zero), jnp.where(first, zero, block)], axis=0
        )

    d_query, d_key, d_value = [], [], []
    for half in range(2):
        starts = [half * width + p * pair for p in range(width // pair)]
        pieces = [
            (
                keys[:, c : c + pair],
                values[:, c : c + pair],
                stacked(queries[:, c : c + pair]),
                stacked(grads[:, c : c + pair]),
            )
            for c in starts
        ]
        scores = [dot_nt(k, q) for k, v, q, g in pieces]
        weights_grads = [dot_nt(v, g) for k, v, q, g in pieces]
        weights_low, scores_grads = [], []
        for score, weights_grad in zip(scores, weights_grads):
            grown = jnp.exp2((score - jnp.max(score, axis=0, keepdims=True)) * EXPONENT)
            weights = grown * (1.0 / jnp.sum(grown, axis=0, keepdims=True))
            inner = jnp.sum(weights * weights_grad, axis=0, keepdims=True)
            weights_low.append(weights.astype(BF16))
            scores_grads.append((weights * (weights_grad - inner)).astype(BF16))
        for weights, scores_grad, (k, v, q, g) in zip(weights_low, scores_grads, pieces):
            d_value.append(dot(weights, g).astype(BF16))
            d_key.append((dot(scores_grad, q) * factor).astype(BF16))
            split = dot_tn(scores_grad, k) * factor
            d_query.append(jnp.where(first, split[:taken], split[taken:]).astype(BF16))
    half = len(d_key) // 2
    own = jnp.concatenate(d_key[:half] + d_value[:half], axis=1)
    d_own[...] = own
    d_peer[...] = jnp.concatenate(d_key[half:] + d_value[half:], axis=1)
    query_own = jnp.concatenate(d_query[:half], axis=1)
    query_peer = jnp.concatenate(d_query[half:], axis=1)
    extra_out[...] = (
        back_one[...]
        + dot_nt(query_own, qkv_all[0, :, :width])
        + dot_nt(query_peer, qkv_all[1, :, :width])
    )
    query_grads[pl.ds(pl.multiple_of(step * taken, taken), taken), :] = query_own
    sums[...] += dot_tn(tokens[...], own)
    vectors[8:9, :width] += row_sum(query_own.astype(F32))
    vectors[8:9, width:] += row_sum(own[:, width:].astype(F32))

    @pl.when(step == last)
    def _():
        grads_rest[:model, :] = sums[...].astype(BF16)
        query_total = dot_tn(picked_tokens[...], query_grads[...]).astype(BF16)
        for c in range(2):
            grads_rest[model : model + width, c * width : (c + 1) * width] = query_total[
                c * width : (c + 1) * width
            ]
        grads_rest[model + width : model + 2 * width, :] = grad_w_out[...]
        vectors[:8, :] = vectors_in[...]

        def rest(event, carry):
            reduction.event(event, range(FF_WAYS))
            return carry

        lax.fori_loop(last, chips, rest, 0)
        for way in range(FF_WAYS):
            reduced[way] = total[ring.rows(way, reduction.done_segment(way)), :]
        share.wait()


def attention_back(
    tokens,
    keys,
    values,
    queries,
    grads,
    back_one,
    picked_tokens,
    qkv_all,
    grad_w_out,
    vectors,
    grad_ff,
    attended,
    late,
    sequences,
    chips,
):
    rows, model = tokens.shape
    length = rows // sequences
    width = keys.shape[1] // 2
    slots = queries.shape[0]
    taken = slots // sequences
    share = grad_ff.shape[0] // 2
    rest_rows = padded_rows(model + 2 * width, chips, 2)
    shape = jax.ShapeDtypeStruct

    def fixed(array_shape):
        return pl.BlockSpec(array_shape, lambda i: (0,) * len(array_shape))

    piece = (FF_WAYS, share // (FF_WAYS * chips), model)
    return pl.pallas_call(
        functools.partial(backward_body, chips),
        grid=(sequences,),
        in_specs=[rows_spec(length, model)]
        + [rows_spec(length, 2 * width)] * 2
        + [rows_spec(taken, 2 * width)] * 2
        + [rows_spec(taken, model)]
        + [
            whole_spec(picked_tokens),
            pl.BlockSpec(qkv_all.shape, lambda i: (0, 0, 0), pipeline_mode=pl.Buffered(1)),
            whole_spec(grad_w_out),
            whole_spec(vectors),
            pl.BlockSpec(memory_space=pl.ANY),
            pl.BlockSpec(memory_space=pl.ANY),
        ],
        out_specs=[
            rows_spec(length, 2 * width),
            rows_spec(length, 2 * width),
            rows_spec(taken, model),
            fixed((rest_rows, model)),
            fixed((16, model)),
            fixed(piece),
            pl.BlockSpec(memory_space=pl.ANY),
        ],
        out_shape=[
            shape((rows, 2 * width), BF16),
            shape((rows, 2 * width), BF16),
            shape((slots, model), F32),
            shape((rest_rows, model), BF16),
            shape((16, model), F32),
            shape(piece, BF16),
            shape((late, width), BF16),
        ],
        scratch_shapes=[
            pltpu.VMEM((slots, width), BF16),
            pltpu.VMEM((model, 2 * width), F32),
            pltpu.VMEM((share, model), BF16),
            pltpu.VMEM((share, model), BF16),
            pltpu.VMEM((FF_WAYS, chips - 1) + piece[1:], BF16),
            pltpu.SemaphoreType.DMA((3,)),
            pltpu.SemaphoreType.DMA((2, FF_WAYS, chips - 1)),
            pltpu.SemaphoreType.DMA((2,)),
        ],
        compiler_params=pltpu.CompilerParams(
            vmem_limit_bytes=VMEM_BYTES, collective_id=1, has_side_effects=True
        ),
        cost_estimate=pl.CostEstimate(
            flops=int(rows * model * 4 * 2 * width),
            bytes_accessed=rows * model * 14,
            transcendentals=0,
        ),
        name="attention_back",
    )(
        tokens,
        keys,
        values,
        queries,
        grads,
        back_one,
        picked_tokens,
        qkv_all,
        grad_w_out,
        vectors,
        grad_ff,
        attended,
    )


def padded_rows(rows, chips, ways):
    unit = 32 * ways * chips
    return -(-rows // unit) * unit


def finish_body(
    d_own,
    d_peer,
    extra,
    picks,
    qkv_all,
    layer_in,
    up_left,
    up_right,
    down,
    key_value,
    query,
    out,
    vectors,
    tokens_grad,
    layer_out,
    grad_w_up,
    grad_w_down,
    grad_w_key,
    grad_w_value,
    grad_w_query,
    grad_w_out,
    grad_b_out,
    grad_gain_one,
    grad_shift_one,
    grad_b_down,
    grad_gain_two,
    grad_shift_two,
    grad_b_up,
    grad_b_query,
    grad_b_value,
):
    @pl.when(pl.program_id(0) == 0)
    def _():
        singles = (
            grad_b_out,
            grad_gain_one,
            grad_shift_one,
            grad_b_down,
            grad_gain_two,
            grad_shift_two,
        )
        for i, single in enumerate(singles):
            single[...] = vectors[i : i + 1, :].reshape(-1)
        grad_b_up[...] = jnp.concatenate([vectors[6:7, :], vectors[7:8, :]], axis=1).reshape(-1)
        grad_b_query[...] = vectors[8:9, : grad_b_query.shape[0]].reshape(-1)
        grad_b_value[...] = vectors[8:9, grad_b_query.shape[0] :].reshape(-1)

    width = grad_w_key.shape[1]
    model = tokens_grad.shape[1]
    length = picks.shape[1]
    taken = picks.shape[0] * length // d_own.shape[0]
    for i in range(d_own.shape[0] // length):
        r, t = slice(i * length, (i + 1) * length), slice(i * taken, (i + 1) * taken)
        wide = extra[t, :]
        high = wide.astype(BF16)
        low = (wide - high.astype(F32)).astype(BF16)
        pick = picks[t, :]
        tokens_grad[r, :] = (
            dot_nt(d_own[r, :], qkv_all[0, :, width:])
            + dot_nt(d_peer[r, :], qkv_all[1, :, width:])
            + dot_tn(jnp.concatenate([pick, pick], axis=0), jnp.concatenate([high, low], axis=0))
        )
    layer_out[...] = layer_in[...]
    grad_w_up[:, :model] = up_left[...].astype(F32)
    grad_w_up[:, model:] = up_right[...].astype(F32)
    grad_w_down[...] = down[...].astype(F32)
    grad_w_key[...] = key_value[:, :width].astype(F32)
    grad_w_value[...] = key_value[:, width:].astype(F32)
    grad_w_query[...] = query[...].astype(F32)
    grad_w_out[...] = out[...].astype(F32)


def finish(
    d_own, d_peer, extra, picks, qkv_all, layer, sums_ff, sums_rest, vectors, half, sequences
):
    rows, model = d_own.shape
    steps = sequences // 2
    length = rows // steps
    width = model // 2
    taken = picks.shape[0] // steps
    assert half == 2 * model and steps % 2 == 0
    part = model // steps
    shape = jax.ShapeDtypeStruct

    def block(count, columns, start, column=None):
        offset = start // count
        return pl.BlockSpec((count, columns), lambda i: (offset + i, 0))

    turns = steps // 2
    counts = [model] * 6 + [half, width, width]
    return pl.pallas_call(
        finish_body,
        grid=(steps,),
        in_specs=[
            rows_spec(length, model),
            rows_spec(length, model),
            rows_spec(taken, model),
            rows_spec(taken, picks.shape[1]),
            pl.BlockSpec(qkv_all.shape, lambda i: (0, 0, 0), pipeline_mode=pl.Buffered(1)),
            rows_spec(length, model),
            block(part, model, 0),
            block(part, model, model),
            block(2 * part, model, half),
            block(part, model, 0),
            pl.BlockSpec((part, width), lambda i: (model // part + i % turns, i // turns)),
            block(width // steps, model, model + width),
            whole_spec(vectors),
        ],
        out_specs=[
            rows_spec(length, model),
            rows_spec(length, model),
            rows_spec(part, half),
            rows_spec(2 * part, model),
            rows_spec(part, width),
            rows_spec(part, width),
            rows_spec(part, width),
            rows_spec(width // steps, model),
        ]
        + [pl.BlockSpec((count,), lambda i: (0,)) for count in counts],
        out_shape=[
            shape((rows, model), F32),
            shape((rows, model), BF16),
            shape((model, half), F32),
            shape((half, model), F32),
            shape((model, width), F32),
            shape((model, width), F32),
            shape((model, width), F32),
            shape((width, model), F32),
        ]
        + [shape((count,), F32) for count in counts],
        compiler_params=params(),
        cost_estimate=pl.CostEstimate(
            flops=int(rows * model * 4 * 2 * width),
            bytes_accessed=rows * model * 16,
            transcendentals=0,
        ),
        name="finish",
    )(
        d_own,
        d_peer,
        extra,
        picks,
        qkv_all,
        layer,
        sums_ff,
        sums_ff,
        sums_ff,
        sums_rest,
        sums_rest,
        sums_rest,
        vectors,
    )


def dense_body(
    chips,
    levels,
    early,
    tokens,
    attended_own,
    attended_local,
    attended_early,
    attended_late,
    w_out,
    w_up_own,
    w_up_peer,
    w_down_own,
    w_down_peer,
    b_up_peer,
    b_up,
    b_out,
    gain_one,
    shift_one,
    b_down,
    gain_two,
    shift_two,
    reduced,
    grads_rest,
    vectors_in,
    layer_out,
    sums_ff,
    sums_rest,
    vectors,
    total,
    other,
    slots,
    last_pieces,
    held_ff,
    held_rest,
    exchanged,
    gained,
    core_sems,
    ring_sems,
    ff_keep_sems,
    ff_sems,
    ff_mate_sems,
    rest_keep_sems,
    rest_sems,
    rest_mate_sems,
    vector_sems,
):
    step = pl.program_id(0)
    steps = pl.num_programs(0)
    model = tokens.shape[1]
    dp = lax.axis_index("dp")
    ring = Ring(chips, total.shape[0], 2)
    ff_ring = Ring(chips, sums_ff.shape[0] // 2, FF_WAYS)
    reduction = Reduce(ring, grads_rest, total, other, slots, core_sems, ring_sems)
    gather_ff = Gather(
        ff_ring,
        reduced,
        held_ff,
        sums_ff,
        ff_keep_sems,
        ff_sems,
        ff_mate_sems,
    )
    gather_rest = Gather(
        ring,
        last_pieces,
        held_rest,
        sums_rest,
        rest_keep_sems,
        rest_sems,
        rest_mate_sems,
    )

    def exchange(level):
        return remote(
            exchanged.at[level],
            gained.at[level],
            vector_sems.at[0, level],
            vector_sems.at[1, level],
            {"dp": flipped(dp, 2**level)},
        )

    def vector_event(level):
        if level > 0:
            exchange(level - 1).wait()
            exchanged[level] = exchanged[level - 1] + gained[level - 1]
        if level < levels:
            exchange(level).start()
        else:
            vectors[...] = exchanged[level]

    def rest_event(event, way):
        @pl.when(event < chips)
        def _():
            reduction.event(event, (way,))

        @pl.when(event == chips - 1)
        def _():
            last_pieces[way] = total[ring.rows(way, reduction.done_segment(way)), :]
            gather_rest.begin((way,))

        @pl.when(event > chips - 1)
        def _():
            gather_rest.event(event - (chips - 1), (way,))

    def point(index):
        def small():
            for way in range(2):
                rest_event(2 * step - 1 + index, way)

        if index == 0:
            pl.when(step > 0)(small)
        else:
            small()

        @pl.when((step > 0) & (step < chips))
        def _():
            gather_ff.event(step, (2 * index, 2 * index + 1))

    @pl.when(step == 0)
    def _():
        greet(ring.neighbours() + tuple({"dp": flipped(dp, 2**level)} for level in range(1, levels)))
        reduction.begin()
        gather_ff.begin(range(FF_WAYS))
        exchanged[0] = vectors_in[...]
        vector_event(0)

    point(0)

    for level in range(1, levels + 1):

        @pl.when(step == jnp.minimum(level, steps - 1))
        def _():
            vector_event(level)

    count = tokens.shape[0] // 2
    split = (slice(0, count), slice(count, 2 * count))

    def first_norm(r):
        attended_peer = jnp.where(
            step < LOCAL,
            attended_local[r, :],
            jnp.where(step < LOCAL + early, attended_early[r, :], attended_late[r, :]),
        )
        attended = jnp.concatenate([attended_own[r, :], attended_peer], axis=1)
        normed, _ = norm_parts(tokens[r, :].astype(F32) + dot(attended, w_out[...]) + row(b_out))
        return normed * row(gain_one) + row(shift_one)

    def forward(layer_low, w_up, w_down, bias):
        hidden = dot(layer_low, w_up[...]) + bias
        return dot((hidden * gelu_share(hidden)).astype(BF16), w_down[...])

    layers = [first_norm(r) for r in split]
    lows = [layer.astype(BF16) for layer in layers]
    sums = [layer + row(b_down) for layer in layers]
    sums[0] = sums[0] + forward(lows[0], w_up_own, w_down_own, row(b_up))
    sums[1] = sums[1] + forward(lows[1], w_up_own, w_down_own, row(b_up))

    @pl.when(step == 0)
    def _():
        reduction.join()

    point(1)
    sums[0] = sums[0] + forward(lows[0], w_up_peer, w_down_peer, b_up_peer[...])
    sums[1] = sums[1] + forward(lows[1], w_up_peer, w_down_peer, b_up_peer[...])
    for r, summed in zip(split, sums):
        normed, _ = norm_parts(summed)
        layer_out[r, :] = (normed * row(gain_two) + row(shift_two)).astype(BF16)

    @pl.when(step == steps - 1)
    def _():
        def more_ff(event, carry):
            gather_ff.event(event, range(FF_WAYS))
            return carry

        def more_rest(event, carry):
            rest_event(event, 0)
            rest_event(event, 1)
            return carry

        lax.fori_loop(steps, chips, more_ff, 0)
        lax.fori_loop(2 * steps - 1, 2 * chips - 1, more_rest, 0)
        gather_ff.finish()
        gather_rest.finish()


def dense_rows(
    tokens,
    attended_own,
    attended_local,
    attended_early,
    attended_late,
    w_out,
    w_up_own,
    w_up_peer,
    w_down_own,
    w_down_peer,
    b_up_peer,
    singles,
    reduced,
    grads_rest,
    vectors,
    sequences,
    chips,
):
    rows, model = tokens.shape
    half = w_up_own.shape[1]
    block = rows // sequences
    levels = (2 * chips).bit_length() - 1
    assert 2**levels == 2 * chips
    share = grads_rest.shape[0] // 2
    ff_rows = reduced.shape[0] * reduced.shape[1] * 2 * chips
    piece = (share // (2 * chips), model)
    shape = jax.ShapeDtypeStruct
    anywhere = pl.BlockSpec(memory_space=pl.ANY)
    arrays = (w_out, w_up_own, w_up_peer, w_down_own, w_down_peer, b_up_peer)
    early = attended_early.shape[0] // block
    late = attended_late.shape[0] // block
    dma = pltpu.SemaphoreType.DMA
    return pl.pallas_call(
        functools.partial(dense_body, chips, levels, early),
        grid=(sequences,),
        in_specs=[
            rows_spec(block, model),
            rows_spec(block, model // 2),
            pl.BlockSpec((block, model // 2), lambda i: (jnp.minimum(i, LOCAL - 1), 0)),
            pl.BlockSpec((block, model // 2), lambda i: (jnp.clip(i - LOCAL, 0, early - 1), 0)),
            pl.BlockSpec(
                (block, model // 2), lambda i: (jnp.clip(i - LOCAL - early, 0, late - 1), 0)
            ),
        ]
        + [whole_spec(array) for array in arrays]
        + [vector_spec(array) for array in singles]
        + [
            pl.BlockSpec(reduced.shape, lambda i: (0, 0, 0), pipeline_mode=pl.Buffered(1)),
            anywhere,
            whole_spec(vectors),
        ],
        out_specs=[
            rows_spec(block, model),
            anywhere,
            anywhere,
            pl.BlockSpec(vectors.shape, lambda i: (0, 0)),
        ],
        out_shape=[
            shape((rows, model), BF16),
            shape((ff_rows, model), BF16),
            shape(grads_rest.shape, BF16),
            shape(vectors.shape, F32),
        ],
        scratch_shapes=[
            pltpu.VMEM((share, model), BF16),
            pltpu.VMEM((share, model), BF16),
            pltpu.VMEM((2, chips - 1) + piece, BF16),
            pltpu.VMEM((2,) + piece, BF16),
            pltpu.VMEM((ff_rows, model), BF16),
            pltpu.VMEM(grads_rest.shape, BF16),
            pltpu.VMEM((levels + 1,) + vectors.shape, F32),
            pltpu.VMEM((levels,) + vectors.shape, F32),
            dma((3,)),
            dma((2, 2, chips - 1)),
            dma((2, FF_WAYS, chips)),
            dma((2, FF_WAYS, chips - 1)),
            dma((2, FF_WAYS, chips)),
            dma((2, 2, chips)),
            dma((2, 2, chips - 1)),
            dma((2, 2, chips)),
            dma((2, levels)),
        ],
        compiler_params=pltpu.CompilerParams(
            vmem_limit_bytes=VMEM_BYTES, collective_id=2, has_side_effects=True
        ),
        cost_estimate=pl.CostEstimate(
            flops=int(rows * model * (8 * half + 2 * model)),
            bytes_accessed=rows * model * 6,
            transcendentals=rows * half * 2,
        ),
        name="dense",
    )(
        tokens,
        attended_own,
        attended_local,
        attended_early,
        attended_late,
        *arrays,
        *singles,
        reduced,
        grads_rest,
        vectors,
    )


def on_device(
    chips,
    tokens,
    out_grad,
    positions,
    w_query,
    b_query,
    w_key,
    w_value,
    b_value,
    w_out,
    b_out,
    gain_one,
    shift_one,
    w_up,
    b_up,
    w_down,
    b_down,
    gain_two,
    shift_two,
):
    sequences, count = positions.shape
    half = w_up.shape[1]
    taken = -(-count // 16) * 16
    (
        attended,
        attended_local,
        keys,
        values,
        picked_q,
        picked_tokens,
        picked_grad,
        picks,
        picked_att,
        qkv_all,
        out_all,
        up_peer,
        down_peer,
        b_up_peer,
    ) = attention(
        tokens,
        out_grad,
        positions,
        w_query,
        w_key,
        w_value,
        w_out,
        w_up,
        w_down,
        b_query,
        b_value,
        b_up,
        taken,
    )
    length = tokens.shape[0] // sequences
    early = (sequences - LOCAL) // 3 * length
    late = tokens.shape[0] - LOCAL * length - early
    weights = (out_all, w_up, up_peer, w_down, down_peer, b_up_peer)
    singles = (b_up, b_out, gain_one, shift_one, b_down, gain_two)
    back_one, att_grad, grad_ff, grad_w_out, vectors, attended_early = marked_rows(
        picked_tokens, picked_att, picked_grad, *weights, singles, attended, early, late, chips
    )
    d_own, d_peer, extra, grads_rest, vectors, reduced, attended_late = attention_back(
        tokens,
        keys,
        values,
        picked_q,
        att_grad,
        back_one,
        picked_tokens,
        qkv_all,
        grad_w_out,
        vectors,
        grad_ff,
        attended,
        late,
        sequences,
        chips,
    )
    layer, sums_ff, sums_rest, vectors = dense_rows(
        tokens,
        attended,
        attended_local,
        attended_early,
        attended_late,
        *weights,
        singles + (shift_two,),
        reduced,
        grads_rest,
        vectors,
        sequences,
        chips,
    )
    (
        tokens_grad,
        layer_out,
        grad_w_up,
        grad_w_down,
        grad_w_key,
        grad_w_value,
        grad_w_query,
        grad_w_out,
        grad_b_out,
        grad_gain_one,
        grad_shift_one,
        grad_b_down,
        grad_gain_two,
        grad_shift_two,
        grad_b_up,
        grad_b_query,
        grad_b_value,
    ) = finish(
        d_own, d_peer, extra, picks, qkv_all, layer, sums_ff, sums_rest, vectors, half, sequences
    )
    return (
        layer_out,
        tokens_grad,
        grad_w_query,
        grad_b_query,
        grad_w_key,
        grad_w_value,
        grad_b_value,
        grad_w_out,
        grad_b_out,
        grad_gain_one,
        grad_shift_one,
        grad_w_up,
        grad_b_up,
        grad_w_down,
        grad_b_down,
        grad_gain_two,
        grad_shift_two,
    )


def solution(mesh):
    across = P("dp", None)
    columns, rows, split, copied = P(None, "tensor"), P("tensor", None), P("tensor"), P()
    in_specs = (
        across,
        across,
        across,
        columns,
        split,
        columns,
        columns,
        split,
        rows,
        copied,
        copied,
        copied,
        columns,
        split,
        rows,
        copied,
        copied,
        copied,
    )
    out_specs = (
        across,
        across,
        columns,
        split,
        columns,
        columns,
        split,
        rows,
        copied,
        copied,
        copied,
        columns,
        split,
        rows,
        copied,
        copied,
        copied,
    )
    return jax.shard_map(
        functools.partial(on_device, mesh.shape["dp"] // 2), mesh=mesh, in_specs=in_specs, out_specs=out_specs, check_vma=False
    )
```

```python
import functools
import math

import jax
import jax.numpy as jnp
from jax import lax
from jax.experimental import pallas as pl
from jax.experimental.pallas import tpu as pltpu
from jax.sharding import PartitionSpec as P

HD = 64
NORM_EPSILON = 1e-12
BF16 = jnp.bfloat16
F32 = jnp.float32
EXPONENT = HD**-0.5 * math.log2(math.e)
ROOT_HALF = 0.7071067811865476
DENSITY = 0.3989422804014327
VMEM_BYTES = 58 * 2**20
FF_WAYS = 4
LOCAL = 2


def dot(left, right):
    return jnp.dot(left, right, preferred_element_type=F32)


def dot_nt(left, right):
    return lax.dot_general(left, right, (((1,), (1,)), ((), ())), preferred_element_type=F32)


def dot_tn(left, right):
    return lax.dot_general(left, right, (((0,), (0,)), ((), ())), preferred_element_type=F32)


def norm_parts(summed):
    centred = summed - jnp.mean(summed, axis=-1, keepdims=True)
    inverse = lax.rsqrt(jnp.mean(centred * centred, axis=-1, keepdims=True) + NORM_EPSILON)
    return centred * inverse, inverse


def norm_back(upstream, normed, inverse, gain):
    scaled = upstream * gain
    return inverse * (
        scaled
        - jnp.mean(scaled, axis=-1, keepdims=True)
        - normed * jnp.mean(scaled * normed, axis=-1, keepdims=True)
    )


def row(vector):
    return vector[...].reshape(1, -1)


def row_sum(values):
    return jnp.sum(values, axis=0, keepdims=True)


def rows_spec(rows, width):
    return pl.BlockSpec((rows, width), lambda i: (i, 0))


def vector_spec(array):
    return pl.BlockSpec(array.shape, lambda i: (0,))


def whole_spec(array):
    return pl.BlockSpec(array.shape, lambda i: (0, 0), pipeline_mode=pl.Buffered(1))


def params():
    return pltpu.CompilerParams(vmem_limit_bytes=VMEM_BYTES)


def flipped(index, span):
    return index + span - 2 * span * ((index // span) % 2)


def remote(source, target, send, receive, device):
    return pltpu.make_async_remote_copy(
        src_ref=source,
        dst_ref=target,
        send_sem=send,
        recv_sem=receive,
        device_id=device,
        device_id_type=pl.DeviceIdType.MESH,
    )


def greet(devices):
    barrier = pltpu.get_barrier_semaphore()
    for device in devices:
        pl.semaphore_signal(barrier, inc=1, device_id=device, device_id_type=pl.DeviceIdType.MESH)
    pl.semaphore_wait(barrier, len(devices))


PIECES = 8


class Fetch:
    def __init__(self, source, target, send_sems, recv_sems, first, second):
        self.source, self.target = source, target
        self.send_sems, self.recv_sems = send_sems, recv_sems
        self.dp = lax.axis_index("dp")
        self.hops = ((0, 0), (first, 0), (second, 0), (second, first)) + tuple(
            (1, flips) for flips in (0, first, second, first + second)
        )

    def _copy(self, source, piece, hop):
        count = self.target.shape[0] // PIECES
        rows = pl.ds(pl.multiple_of(piece * count, 16), count)
        if hop:
            device = {"dp": flipped(self.dp, self.hops[hop][0])}
        else:
            device = {"tensor": 1 - lax.axis_index("tensor")}
        return remote(
            source.at[rows], self.target.at[rows], self.send_sems.at[hop], self.recv_sems.at[hop], device
        )

    def _piece(self, flips):
        piece = self.dp % PIECES
        for span in (4, 2, 1):
            if flips & span:
                piece = flipped(piece, span)
        return piece

    def out(self, hop):
        return self._copy(
            self.target if hop else self.source, self._piece(self.hops[hop][1]), hop
        )

    def into(self, hop):
        return self._copy(self.target, self._piece(self.hops[hop][0] | self.hops[hop][1]), hop)

    def move(self, what):
        if what == "x":
            self.out(0).start()
        if what == "z":
            self.into(0).wait_recv()
            for hop in (1, 2, 4):
                self.out(hop).start()
        if what == "y":
            self.into(1).wait_recv()
            for hop in (3, 5):
                self.out(hop).start()
        if what == "c":
            self.into(2).wait_recv()
            self.into(3).wait_recv()
            for hop in (6, 7):
                self.out(hop).start()
        if what == "end":
            for hop in (4, 5, 6, 7):
                self.into(hop).wait_recv()


def attention_body(
    tokens,
    out_grad,
    positions,
    w_query,
    w_key,
    w_value,
    w_out,
    w_up,
    w_down,
    b_query,
    b_value,
    b_up,
    attended,
    attended_local,
    keys,
    values,
    picked_q,
    picked_tokens,
    picked_grad,
    picks,
    picked_att,
    qkv_all,
    out_all,
    up_peer,
    down_peer,
    b_up_peer,
    qkv,
    biases,
    up_biases,
    kept_tokens,
    kept_picks,
    kept_att,
    kept_local,
    places,
    local_sems,
    send_sems,
    recv_sems,
    bias_sems,
    att_sems,
):
    step = pl.program_id(0)
    sequences = pl.num_programs(0) // 2
    sequence = step % sequences
    turn = step // sequences
    length = tokens.shape[0]
    width = keys.shape[1]
    model = tokens.shape[1]
    taken = picks.shape[0]
    dp = lax.axis_index("dp")
    across = {"tensor": 1 - lax.axis_index("tensor")}

    def halves(source, target):
        rows = target.shape[0] // 2
        return [(source.at[pl.ds(i * rows, rows)], target.at[pl.ds(i * rows, rows)]) for i in range(2)]

    pairs = (
        [(w_out, out_all.at[pl.ds(width, width)])]
        + halves(qkv.at[0], qkv.at[1])
        + halves(w_up, up_peer)
        + halves(w_down, down_peer)
    )
    fetches = [
        Fetch(source, target, send_sems.at[i], recv_sems.at[i], *((4, 2), (2, 4))[i % 2])
        for i, (source, target) in enumerate(pairs)
    ]
    bias_copies = [
        remote(source, target, bias_sems.at[0, i], bias_sems.at[1, i], across)
        for i, (source, target) in enumerate(
            (
                (biases.at[0], biases.at[1]),
                (biases.at[2], biases.at[3]),
                (up_biases, b_up_peer),
            )
        )
    ]

    far = pl.ds(LOCAL * taken, (sequences - LOCAL) * taken)
    att_copy = remote(
        kept_att.at[far],
        picked_att.at[far, pl.ds(width, width)],
        att_sems.at[0],
        att_sems.at[1],
        across,
    )

    loads = [
        pltpu.make_async_copy(weight, qkv.at[0, :, pl.ds(i * width, width)], local_sems.at[i])
        for i, weight in enumerate((w_query, w_key, w_value))
    ]
    keep_out = pltpu.make_async_copy(w_out, out_all.at[pl.ds(0, width)], local_sems.at[3])
    keep_qkv = pltpu.make_async_copy(qkv, qkv_all, local_sems.at[4])
    keep_att = pltpu.make_async_copy(kept_att, picked_att.at[:, pl.ds(0, width)], local_sems.at[5])
    keep_local = pltpu.make_async_copy(
        kept_local, picked_att.at[pl.ds(0, LOCAL * taken), pl.ds(width, width)], local_sems.at[6]
    )

    @pl.when(step == 0)
    def _():
        for load in loads:
            load.start()
        keep_out.start()
        places[...] = jnp.full(places.shape, -1, jnp.int32)
        places[:, : positions.shape[1]] = positions[...]
        biases[0] = row(b_query)
        biases[2] = row(b_value)
        up_biases[...] = row(b_up)
        greet((across,) + tuple({"dp": flipped(dp, span)} for span in (1, 2, 4)))
        fetches[0].move("x")
        for load in loads:
            load.wait()
        fetches[1].move("x")
        fetches[2].move("x")
        for copy in bias_copies:
            copy.start()

    moves = {
        1: [(3, "x")],
        2: [(0, "z"), (1, "z")],
        3: [(2, "z"), (4, "x")],
        4: [(3, "z"), (0, "y"), (1, "y"), (5, "x")],
        5: [(4, "z"), (2, "y"), (6, "x")],
        6: [(3, "y"), (0, "c"), (1, "c")],
        7: [(5, "z"), (6, "z"), (4, "y"), (2, "c")],
        8: [(1, "end"), (2, "end")],
        9: [(5, "y"), (6, "y"), (3, "c")],
        10: [(4, "c"), (5, "c")],
        14: [(6, "c")],
    }
    for when, made in moves.items():

        @pl.when(step == when)
        def _():
            for index, what in made:
                fetches[index].move(what)

    @pl.when(step == sequences)
    def _():
        bias_copies[0].wait_recv()
        bias_copies[1].wait_recv()
        keep_qkv.start()
        keep_att.start()
        att_copy.start()

    def attend(query, key, value, outcome):
        pair = 2 * HD
        first = lax.broadcasted_iota(jnp.int32, (length, pair), 1) < HD
        zero = jnp.zeros((length, pair), BF16)
        one = jnp.ones((length, pair), BF16)
        for p in range(width // pair):
            here = slice(p * pair, (p + 1) * pair)
            k, v = key[:, here], value[:, here]
            k_two = jnp.concatenate([jnp.where(first, k, zero), jnp.where(first, zero, k)], axis=0)
            v_two = jnp.concatenate(
                [
                    jnp.concatenate(
                        [jnp.where(first, v, zero), jnp.where(first, one, zero)], axis=1
                    ),
                    jnp.concatenate(
                        [jnp.where(first, zero, v), jnp.where(first, zero, one)], axis=1
                    ),
                ],
                axis=0,
            )
            scores = dot_nt(query[:, here], k_two)
            left, right = scores[:, :length], scores[:, length:]
            left = jnp.exp2((left - jnp.max(left, axis=1, keepdims=True)) * EXPONENT).astype(BF16)
            right = jnp.exp2((right - jnp.max(right, axis=1, keepdims=True)) * EXPONENT).astype(
                BF16
            )
            both = dot(jnp.concatenate([left, right], axis=1), v_two)
            outcome[:, here] = (both[:, :pair] / both[:, pair:]).astype(BF16)

    rows = pl.ds(pl.multiple_of(sequence * taken, 16), taken)

    @pl.when(turn == 0)
    def _():
        tokens_here = tokens[...]
        projected = dot(tokens_here, qkv[0])
        query = (projected[:, :width] + biases[0]).astype(BF16)
        key = projected[:, width : 2 * width].astype(BF16)
        value = (projected[:, 2 * width :] + biases[2]).astype(BF16)
        keys[...] = key
        values[...] = value
        attend(query, key, value, attended)

        spread = jnp.broadcast_to(places[pl.ds(sequence, 1), :], (length, places.shape[1]))
        column = lax.broadcasted_iota(jnp.int32, spread.shape, 1).astype(F32)
        hit = spread == lax.broadcasted_iota(jnp.int32, spread.shape, 0)
        earliest = jnp.min(jnp.where(hit, column, 1e6), axis=1, keepdims=True)
        pick = jnp.where(column == earliest, 1.0, 0.0).T[:taken].astype(BF16)
        picks[...] = pick
        tokens_low = dot(pick, tokens_here).astype(BF16)
        picked_tokens[...] = tokens_low
        picked_grad[...] = dot(pick, out_grad[...]).astype(BF16)
        picked_q[...] = dot(pick, query).astype(BF16)
        kept_tokens[rows, :] = tokens_low
        kept_picks[rows, :] = pick
        kept_att[rows, :] = dot(pick, attended[...]).astype(BF16)

    @pl.when((turn == 1) & (sequence < LOCAL))
    def _():
        projected = dot(tokens[...], qkv[1])
        query = (projected[:, :width] + biases[1]).astype(BF16)
        key = projected[:, width : 2 * width].astype(BF16)
        value = (projected[:, 2 * width :] + biases[3]).astype(BF16)
        keys[...] = key
        values[...] = value
        attend(query, key, value, attended_local)
        pick = kept_picks[rows, :]
        picked_q[...] = dot(pick, query).astype(BF16)
        kept_local[pl.ds(pl.multiple_of(sequence % LOCAL * taken, 16), taken), :] = dot(
            pick, attended_local[...]
        ).astype(BF16)

    @pl.when((turn == 1) & (sequence >= LOCAL))
    def _():
        projected = dot(tokens[...], qkv[1, :, width:])
        keys[...] = projected[:, :width].astype(BF16)
        values[...] = (projected[:, width:] + biases[3]).astype(BF16)
        picked_q[...] = (dot(kept_tokens[rows, :], qkv[1, :, :width]) + biases[1]).astype(BF16)

    @pl.when(step == 2 * sequences - 1)
    def _():
        keep_local.start()
        for index in (0, 3, 4, 5, 6):
            fetches[index].move("end")
        bias_copies[2].wait_recv()
        for fetch in fetches:
            for hop in range(PIECES):
                fetch.out(hop).wait_send()
        for copy in bias_copies:
            copy.wait_send()
        att_copy.wait()
        keep_out.wait()
        keep_qkv.wait()
        keep_att.wait()
        keep_local.wait()


def attention(
    tokens, out_grad, positions, w_query, w_key, w_value, w_out, w_up, w_down, b_query, b_value, b_up, taken
):
    rows, model = tokens.shape
    sequences = positions.shape[0]
    length = rows // sequences
    width = w_query.shape[1]
    shape = jax.ShapeDtypeStruct
    slots = sequences * taken

    def both(count, columns):
        return pl.BlockSpec((count, columns), lambda s: (s % sequences, s // sequences))

    def once(count, columns):
        return pl.BlockSpec((count, columns), lambda s: (jnp.minimum(s, sequences - 1), 0))

    def again(count, columns):
        return pl.BlockSpec((count, columns), lambda s: (s % sequences, 0))

    anywhere = pl.BlockSpec(memory_space=pl.ANY)
    dma = pltpu.SemaphoreType.DMA
    return pl.pallas_call(
        attention_body,
        grid=(2 * sequences,),
        in_specs=[
            again(length, model),
            once(length, model),
            pl.BlockSpec(positions.shape, lambda s: (0, 0)),
        ]
        + [anywhere] * 6
        + [vector_spec(array) for array in (b_query, b_value, b_up)],
        out_specs=[
            once(length, width),
            pl.BlockSpec((length, width), lambda s: (jnp.clip(s - sequences, 0, LOCAL - 1), 0)),
            both(length, width),
            both(length, width),
            both(taken, width),
            once(taken, model),
            once(taken, model),
            once(taken, length),
        ]
        + [anywhere] * 6,
        out_shape=[
            shape((rows, width), BF16),
            shape((LOCAL * length, width), BF16),
            shape((rows, 2 * width), BF16),
            shape((rows, 2 * width), BF16),
            shape((slots, 2 * width), BF16),
            shape((slots, model), BF16),
            shape((slots, model), BF16),
            shape((slots, length), BF16),
            shape((slots, 2 * width), BF16),
            shape((2, model, 3 * width), BF16),
            shape((2 * width, model), BF16),
            shape(w_up.shape, BF16),
            shape(w_down.shape, BF16),
            shape((1, w_up.shape[1]), F32),
        ],
        scratch_shapes=[
            pltpu.VMEM((2, model, 3 * width), BF16),
            pltpu.VMEM((4, 1, width), F32),
            pltpu.VMEM((1, w_up.shape[1]), F32),
            pltpu.VMEM((slots, model), BF16),
            pltpu.VMEM((slots, length), BF16),
            pltpu.VMEM((slots, width), BF16),
            pltpu.VMEM((LOCAL * taken, width), BF16),
            pltpu.VMEM((sequences, -(-positions.shape[1] // 128) * 128), jnp.int32),
            dma((7,)),
            dma((7, PIECES)),
            dma((7, PIECES)),
            dma((2, 3)),
            dma((2,)),
        ],
        compiler_params=pltpu.CompilerParams(
            vmem_limit_bytes=VMEM_BYTES, collective_id=0, has_side_effects=True
        ),
        cost_estimate=pl.CostEstimate(
            flops=int(rows * width * (10 * model + 16 * length)),
            bytes_accessed=rows * model * 12,
            transcendentals=rows * length * width // HD,
        ),
        name="attention",
    )(tokens, out_grad, positions, w_query, w_key, w_value, w_out, w_up, w_down, b_query, b_value, b_up)


def gelu_share(hidden):
    return 0.5 * (1.0 + lax.erf(hidden * ROOT_HALF))


def marked_body(
    late,
    tokens,
    picked_att,
    upstream,
    w_out,
    w_up_own_hbm,
    w_up_peer_hbm,
    w_down_own_hbm,
    w_down_peer_hbm,
    b_up_peer,
    b_up,
    b_out,
    gain_one,
    shift_one,
    b_down,
    gain_two,
    attended,
    back_one_out,
    attended_grad,
    grad_ff_hbm,
    grad_w_out,
    vectors,
    attended_peer,
    w_up,
    w_down,
    grad_ff,
    slope,
    active,
    load_sems,
    store_sems,
    att_sems,
):
    model = tokens.shape[1]
    width = model // 2
    half = w_up.shape[2]
    loads = [
        pltpu.make_async_copy(source, target, load_sems.at[i])
        for i, (source, target) in enumerate(
            (
                (w_up_own_hbm, w_up.at[0]),
                (w_down_own_hbm, w_down.at[0]),
                (w_up_peer_hbm, w_up.at[1]),
                (w_down_peer_hbm, w_down.at[1]),
            )
        )
    ]
    for load in loads:
        load.start()
    across = {"tensor": 1 - lax.axis_index("tensor")}
    share = remote(
        attended.at[pl.ds(attended.shape[0] - attended_peer.shape[0] - late, attended_peer.shape[0])],
        attended_peer,
        att_sems.at[0],
        att_sems.at[1],
        across,
    )
    count = tokens.shape[0] // 2
    split = (slice(0, count), slice(count, 2 * count))
    ones = [
        norm_parts(
            tokens[r, :].astype(F32) + dot(picked_att[r, :], w_out[...]) + row(b_out)
        )
        for r in split
    ]
    layers = [normed * row(gain_one) + row(shift_one) for normed, _ in ones]
    lows = [layer.astype(BF16) for layer in layers]
    sums = [layer + row(b_down) for layer in layers]
    greet((across,))
    share.start()
    for part in range(2):
        loads[2 * part].wait()
        bias = b_up_peer[...] if part else row(b_up)
        for i, r in enumerate(split):
            hidden = dot(lows[i], w_up[part]) + bias
            gate = gelu_share(hidden)
            act = (hidden * gate).astype(BF16)
            slope[part, r, :] = gate + hidden * jnp.exp(-0.5 * hidden * hidden) * DENSITY
            if part == 0:
                active[r, :] = act
            if i == 0:
                loads[2 * part + 1].wait()
            sums[i] = sums[i] + dot(act, w_down[part])
    twos = [norm_parts(summed) for summed in sums]
    ups = [upstream[r, :].astype(F32) for r in split]
    backs = [
        norm_back(up, normed, inverse, row(gain_two)) for up, (normed, inverse) in zip(ups, twos)
    ]
    back_lows = [back.astype(BF16) for back in backs]
    layer_low = jnp.concatenate(lows, axis=0)
    back_low = jnp.concatenate(back_lows, axis=0)
    layer_grads = list(backs)
    stores = [
        pltpu.make_async_copy(
            grad_ff.at[pl.ds(i * half, half)], grad_ff_hbm.at[pl.ds(i * half, half)], store_sems.at[i]
        )
        for i in range(2)
    ]
    grad_ff[half : 2 * half, :] = dot_tn(active[...], back_low).astype(BF16)
    stores[1].start()
    for part in range(2):
        hidden_grads = []
        for i, r in enumerate(split):
            hidden_grad = (dot_nt(back_lows[i], w_down[part]) * slope[part, r, :]).astype(BF16)
            layer_grads[i] = layer_grads[i] + dot_nt(hidden_grad, w_up[part])
            hidden_grads.append(hidden_grad)
        if part == 0:
            hidden_grad = jnp.concatenate(hidden_grads, axis=0)
            grad_b_up = row_sum(hidden_grad.astype(F32))
            for c in range(0, half, model):
                grad_ff[c : c + model, :] = dot_tn(layer_low, hidden_grad[:, c : c + model]).astype(
                    BF16
                )
            stores[0].start()
    back_ones = [
        norm_back(grad, normed, inverse, row(gain_one))
        for grad, (normed, inverse) in zip(layer_grads, ones)
    ]
    back_one_low = jnp.concatenate([back.astype(BF16) for back in back_ones], axis=0)
    for r, back in zip(split, back_ones):
        back_one_out[r, :] = back
    grad_w_out[...] = dot_tn(picked_att[:, :width], back_one_low).astype(BF16)
    attended_grad[...] = dot_nt(back_one_low, w_out[...]).astype(BF16)

    def total(pieces):
        return row_sum(pieces[0]) + row_sum(pieces[1])

    vectors[...] = jnp.concatenate(
        [
            total(back_ones),
            total([grad * normed for grad, (normed, _) in zip(layer_grads, ones)]),
            total(layer_grads),
            total(backs),
            total([up * normed for up, (normed, _) in zip(ups, twos)]),
            total(ups),
        ]
        + [grad_b_up[:, c : c + model] for c in range(0, half, model)],
        axis=0,
    )
    for store in stores:
        store.wait()
    share.wait()


def marked_rows(
    picked_tokens,
    picked_att,
    picked_grad,
    out_all,
    w_up,
    up_peer,
    w_down,
    down_peer,
    b_up_peer,
    vectors,
    attended,
    early,
    late,
    chips,
):
    rows, model = picked_tokens.shape
    width = model // 2
    half = w_up.shape[1]
    shape = jax.ShapeDtypeStruct
    inside = pl.BlockSpec(memory_space=pltpu.VMEM)
    anywhere = pl.BlockSpec(memory_space=pl.ANY)
    dma = pltpu.SemaphoreType.DMA
    return pl.pallas_call(
        functools.partial(marked_body, late),
        in_specs=[inside] * 4 + [anywhere] * 4 + [inside] * (1 + len(vectors)) + [anywhere],
        out_specs=[inside, inside, anywhere, inside, inside, anywhere],
        out_shape=[
            shape((rows, model), F32),
            shape((rows, 2 * width), BF16),
            shape((padded_rows(2 * half, chips, FF_WAYS), model), BF16),
            shape((width, model), BF16),
            shape((6 + half // model, model), F32),
            shape((early, width), BF16),
        ],
        scratch_shapes=[
            pltpu.VMEM((2, model, half), BF16),
            pltpu.VMEM((2, half, model), BF16),
            pltpu.VMEM((2 * half, model), BF16),
            pltpu.VMEM((2, rows, half), F32),
            pltpu.VMEM((rows, half), BF16),
            dma((4,)),
            dma((2,)),
            dma((2,)),
        ],
        compiler_params=pltpu.CompilerParams(
            vmem_limit_bytes=VMEM_BYTES, collective_id=3, has_side_effects=True
        ),
        cost_estimate=pl.CostEstimate(
            flops=int(rows * model * (2 * half * 10 + 2 * width * 5)),
            bytes_accessed=6 * model * half * 2,
            transcendentals=rows * half * 4,
        ),
        name="marked",
    )(
        picked_tokens,
        picked_att,
        picked_grad,
        out_all,
        w_up,
        up_peer,
        w_down,
        down_peer,
        b_up_peer,
        *vectors,
        attended,
    )


class Ring:
    def __init__(self, chips, share, ways):
        self.chips, self.ways, self.count = chips, ways, share // (ways * chips)
        self.share = share
        dp = lax.axis_index("dp")
        self.core, chip = dp % 2, dp // 2
        self.place = self.at(chip)
        self.mate = {"dp": flipped(dp, 1)}
        self.up = {"dp": self.device(self.place + 1)}
        self.down = {"dp": self.device(self.place + chips - 1)}

    def at(self, chip):
        high, low = chip // 2, chip % 2
        return (1 - low) * high + low * (self.chips - 1 - high)

    def device(self, place):
        place = place % self.chips
        back = place // (self.chips // 2)
        chip = (1 - back) * 2 * place + back * (2 * (self.chips - 1 - place) + 1)
        return 2 * chip + self.core

    def neighbours(self):
        return self.up, self.down, self.mate

    def onward(self, way):
        return (self.up, self.down)[way % 2]

    def segment(self, way, step):
        sign = 1 - 2 * (way % 2)
        return (self.place - sign * step + 2 * self.chips) % self.chips

    def rows(self, way, segment):
        return pl.ds(pl.multiple_of((way * self.chips + segment) * self.count, 16), self.count)

    def final_rows(self, way, segment, core):
        start = core * self.share + (way * self.chips + segment) * self.count
        return pl.ds(pl.multiple_of(start, 16), self.count)


class Reduce:
    def __init__(self, ring, source, total, other, slots, core_sems, sems):
        self.ring, self.source, self.total, self.other = ring, source, total, other
        self.slots, self.core_sems, self.sems = slots, core_sems, sems

    def _core(self):
        ring = self.ring
        give = pl.ds(pl.multiple_of((1 - ring.core) * ring.share, 16), ring.share)
        keep = pl.ds(pl.multiple_of(ring.core * ring.share, 16), ring.share)
        return (
            remote(
                self.source.at[give],
                self.other,
                self.core_sems.at[0],
                self.core_sems.at[1],
                ring.mate,
            ),
            pltpu.make_async_copy(self.source.at[keep], self.total, self.core_sems.at[2]),
        )

    def begin(self):
        given, kept = self._core()
        given.start()
        kept.start()

    def join(self):
        given, kept = self._core()
        kept.wait()
        given.wait()
        self.total[...] += self.other[...]

    def _copy(self, way, step):
        ring = self.ring
        return remote(
            self.total.at[ring.rows(way, ring.segment(way, step))],
            self.slots.at[way, step],
            self.sems.at[0, way, step],
            self.sems.at[1, way, step],
            ring.onward(way),
        )

    def event(self, step, ways):
        ring = self.ring

        @pl.when(step > 0)
        def _():
            for way in ways:
                self._copy(way, step - 1).wait()
                here = ring.rows(way, ring.segment(way, step))
                self.total[here, :] += self.slots[way, step - 1]

        @pl.when(step < ring.chips - 1)
        def _():
            for way in ways:
                self._copy(way, step).start()

    def done_segment(self, way):
        return self.ring.segment(way, self.ring.chips - 1)


class Gather:
    def __init__(self, ring, firsts, held, out, store_sems, sems, mate_sems):
        self.ring, self.firsts, self.held, self.out = ring, firsts, held, out
        self.store_sems, self.sems, self.mate_sems = store_sems, sems, mate_sems

    def _rows(self, way, step, core):
        ring, sign = self.ring, 1 - 2 * (way % 2)
        segment = (ring.place + sign - sign * step + 2 * ring.chips) % ring.chips
        return ring.final_rows(way, segment, core)

    def _store(self, way, step, core, which):
        rows = self._rows(way, step, core)
        return pltpu.make_async_copy(
            self.held.at[rows], self.out.at[rows], self.store_sems.at[which, way, step]
        )

    def _own(self, way, step):
        return self._store(way, step, self.ring.core, 0)

    def _mates(self, way, step):
        return self._store(way, step, 1 - self.ring.core, 1)

    def _send(self, way, step):
        here = self.held.at[self._rows(way, step, self.ring.core)]
        return remote(
            here, here, self.sems.at[0, way, step], self.sems.at[1, way, step], self.ring.onward(way)
        )

    def _arrive(self, way, step):
        here = self.held.at[self._rows(way, step + 1, self.ring.core)]
        return remote(
            here, here, self.sems.at[0, way, step], self.sems.at[1, way, step], self.ring.onward(way)
        )

    def _mate(self, way, step, core):
        here = self.held.at[self._rows(way, step, core)]
        return remote(
            here,
            here,
            self.mate_sems.at[0, way, step],
            self.mate_sems.at[1, way, step],
            self.ring.mate,
        )

    def _pass_on(self, step, ways):
        for way in ways:

            @pl.when(step < self.ring.chips - 1)
            def _():
                self._send(way, step).start()

            self._mate(way, step, self.ring.core).start()
            self._own(way, step).start()

    def begin(self, ways):
        for way in ways:
            self.held[self._rows(way, 0, self.ring.core), :] = self.firsts[way]
        self._pass_on(0, ways)

    def event(self, step, ways):
        for way in ways:
            self._arrive(way, step - 1).wait_recv()
        self._pass_on(step, ways)
        for way in ways:
            self._mate(way, step - 1, 1 - self.ring.core).wait_recv()
            self._mates(way, step - 1).start()

    def finish(self):
        last = self.ring.chips - 1
        ways = range(self.ring.ways)
        for way in ways:
            self._mate(way, last, 1 - self.ring.core).wait_recv()
            self._mates(way, last).start()

        def rest(step, carry):
            for way in ways:

                @pl.when(step < last)
                def _():
                    self._send(way, step).wait_send()

                self._mate(way, step, self.ring.core).wait_send()
                self._own(way, step).wait()
                self._mates(way, step).wait()
            return carry

        lax.fori_loop(0, self.ring.chips, rest, 0)


def backward_body(
    chips,
    tokens,
    keys,
    values,
    queries,
    grads,
    back_one,
    picks,
    picked_tokens,
    qkv_all,
    grad_w_out,
    vectors_in,
    grad_ff,
    attended,
    tokens_low,
    grads_rest,
    vectors,
    reduced,
    attended_peer,
    query_grads,
    sums,
    total,
    other,
    slots,
    core_sems,
    ring_sems,
    att_sems,
):
    step = pl.program_id(0)
    last = pl.num_programs(0) - 1
    model = tokens.shape[1]
    width = keys.shape[1] // 2
    taken = queries.shape[0]
    factor = HD**-0.5
    group, span = 3, 4 * HD
    assert width == 2 * group * HD
    ring = Ring(chips, total.shape[0], FF_WAYS)
    reduction = Reduce(ring, grad_ff, total, other, slots, core_sems, ring_sems)
    across = {"tensor": 1 - lax.axis_index("tensor")}
    shared_rows = attended_peer.shape[0]
    share = remote(
        attended.at[pl.ds(attended.shape[0] - shared_rows, shared_rows)],
        attended_peer,
        att_sems.at[0],
        att_sems.at[1],
        across,
    )

    @pl.when(step == 0)
    def _():
        sums[...] = jnp.zeros_like(sums)
        vectors[...] = jnp.zeros_like(vectors)
        greet(ring.neighbours() + (across,))
        reduction.begin()
        share.start()

    @pl.when(step == 1)
    def _():
        reduction.join()

    @pl.when(step > 0)
    def _():
        reduction.event(step - 1, range(FF_WAYS))

    head = lax.broadcasted_iota(jnp.int32, (taken, span), 1) // HD

    def stacked(block, skip):
        zero = jnp.zeros_like(block)
        return jnp.concatenate(
            [jnp.where(head == j + skip, block, zero) for j in range(group)], axis=0
        )

    def unstacked(block, skip):
        zero = jnp.zeros((taken, span), F32)
        return sum(
            jnp.where(head == j + skip, block[j * taken : (j + 1) * taken], zero)
            for j in range(group)
        )

    def joined(early, late):
        cut = span // 2
        return jnp.concatenate(
            [early[:, :cut], early[:, cut:] + late[:, :cut], late[:, cut:]], axis=1
        ).astype(BF16)

    d_query, d_key, d_value = [], [], []
    for half in range(2):
        starts = (half * width, (half + 1) * width - span)
        pieces = [
            (
                keys[:, c : c + span],
                values[:, c : c + span],
                stacked(queries[:, c : c + span], skip),
                stacked(grads[:, c : c + span], skip),
            )
            for skip, c in enumerate(starts)
        ]
        scores = [dot_nt(k, q) for k, v, q, g in pieces]
        weights_grads = [dot_nt(v, g) for k, v, q, g in pieces]
        weights_low, scores_grads = [], []
        for score, weights_grad in zip(scores, weights_grads):
            grown = jnp.exp2((score - jnp.max(score, axis=0, keepdims=True)) * EXPONENT)
            weights = grown * (1.0 / jnp.sum(grown, axis=0, keepdims=True))
            inner = jnp.sum(weights * weights_grad, axis=0, keepdims=True)
            weights_low.append(weights.astype(BF16))
            scores_grads.append((weights * (weights_grad - inner)).astype(BF16))
        d_value.append(joined(*[dot(w, p[3]) for w, p in zip(weights_low, pieces)]))
        d_key.append(joined(*[dot(w, p[2]) * factor for w, p in zip(scores_grads, pieces)]))
        d_query.append(
            joined(
                *[
                    unstacked(dot_tn(w, p[0]) * factor, skip)
                    for skip, (w, p) in enumerate(zip(scores_grads, pieces))
                ]
            )
        )
    own = jnp.concatenate([d_key[0], d_value[0]], axis=1)
    peer = jnp.concatenate([d_key[1], d_value[1]], axis=1)
    query_own, query_peer = d_query
    extra = (
        back_one[...]
        + dot_nt(query_own, qkv_all[0, :, :width])
        + dot_nt(query_peer, qkv_all[1, :, :width])
    ).astype(BF16)
    tokens_low[...] = (
        dot_nt(own, qkv_all[0, :, width:])
        + dot_nt(peer, qkv_all[1, :, width:])
        + dot_tn(picks[...], extra)
    ).astype(BF16)
    query_grads[pl.ds(pl.multiple_of(step * taken, taken), taken), :] = query_own
    sums[...] += dot_tn(tokens[...], own)
    vectors[8:9, :width] += row_sum(query_own.astype(F32))
    vectors[8:9, width:] += row_sum(own[:, width:].astype(F32))

    @pl.when(step == last)
    def _():
        grads_rest[:model, :] = sums[...].astype(BF16)
        query_total = dot_tn(picked_tokens[...], query_grads[...]).astype(BF16)
        for c in range(2):
            grads_rest[model : model + width, c * width : (c + 1) * width] = query_total[
                c * width : (c + 1) * width
            ]
        grads_rest[model + width : model + 2 * width, :] = grad_w_out[...]
        vectors[:8, :] = vectors_in[...]

        def rest(event, carry):
            reduction.event(event, range(FF_WAYS))
            return carry

        lax.fori_loop(last, chips, rest, 0)
        for way in range(FF_WAYS):
            reduced[way] = total[ring.rows(way, reduction.done_segment(way)), :]
        share.wait()


def attention_back(
    tokens,
    keys,
    values,
    queries,
    grads,
    back_one,
    picks,
    picked_tokens,
    qkv_all,
    grad_w_out,
    vectors,
    grad_ff,
    attended,
    late,
    sequences,
    chips,
):
    rows, model = tokens.shape
    length = rows // sequences
    width = keys.shape[1] // 2
    slots = queries.shape[0]
    taken = slots // sequences
    share = grad_ff.shape[0] // 2
    rest_rows = padded_rows(model + 2 * width, chips, 2)
    shape = jax.ShapeDtypeStruct

    def fixed(array_shape):
        return pl.BlockSpec(array_shape, lambda i: (0,) * len(array_shape))

    piece = (FF_WAYS, share // (FF_WAYS * chips), model)
    return pl.pallas_call(
        functools.partial(backward_body, chips),
        grid=(sequences,),
        in_specs=[rows_spec(length, model)]
        + [rows_spec(length, 2 * width)] * 2
        + [rows_spec(taken, 2 * width)] * 2
        + [rows_spec(taken, model), rows_spec(taken, length)]
        + [
            whole_spec(picked_tokens),
            pl.BlockSpec(qkv_all.shape, lambda i: (0, 0, 0), pipeline_mode=pl.Buffered(1)),
            whole_spec(grad_w_out),
            whole_spec(vectors),
            pl.BlockSpec(memory_space=pl.ANY),
            pl.BlockSpec(memory_space=pl.ANY),
        ],
        out_specs=[
            rows_spec(length, model),
            fixed((rest_rows, model)),
            fixed((16, model)),
            fixed(piece),
            pl.BlockSpec(memory_space=pl.ANY),
        ],
        out_shape=[
            shape((rows, model), BF16),
            shape((rest_rows, model), BF16),
            shape((16, model), F32),
            shape(piece, BF16),
            shape((late, width), BF16),
        ],
        scratch_shapes=[
            pltpu.VMEM((slots, width), BF16),
            pltpu.VMEM((model, 2 * width), F32),
            pltpu.VMEM((share, model), BF16),
            pltpu.VMEM((share, model), BF16),
            pltpu.VMEM((FF_WAYS, chips - 1) + piece[1:], BF16),
            pltpu.SemaphoreType.DMA((3,)),
            pltpu.SemaphoreType.DMA((2, FF_WAYS, chips - 1)),
            pltpu.SemaphoreType.DMA((2,)),
        ],
        compiler_params=pltpu.CompilerParams(
            vmem_limit_bytes=VMEM_BYTES, collective_id=1, has_side_effects=True
        ),
        cost_estimate=pl.CostEstimate(
            flops=int(rows * model * 4 * 2 * width),
            bytes_accessed=rows * model * 14,
            transcendentals=0,
        ),
        name="attention_back",
    )(
        tokens,
        keys,
        values,
        queries,
        grads,
        back_one,
        picks,
        picked_tokens,
        qkv_all,
        grad_w_out,
        vectors,
        grad_ff,
        attended,
    )


def padded_rows(rows, chips, ways):
    unit = 32 * ways * chips
    return -(-rows // unit) * unit


def finish_body(
    tokens_low,
    layer_in,
    up_left,
    up_right,
    down,
    key_value,
    query,
    out,
    vectors,
    tokens_grad,
    layer_out,
    grad_w_up,
    grad_w_down,
    grad_w_key,
    grad_w_value,
    grad_w_query,
    grad_w_out,
    grad_b_out,
    grad_gain_one,
    grad_shift_one,
    grad_b_down,
    grad_gain_two,
    grad_shift_two,
    grad_b_up,
    grad_b_query,
    grad_b_value,
):
    @pl.when(pl.program_id(0) == 0)
    def _():
        singles = (
            grad_b_out,
            grad_gain_one,
            grad_shift_one,
            grad_b_down,
            grad_gain_two,
            grad_shift_two,
        )
        for i, single in enumerate(singles):
            single[...] = vectors[i : i + 1, :].reshape(-1)
        grad_b_up[...] = jnp.concatenate([vectors[6:7, :], vectors[7:8, :]], axis=1).reshape(-1)
        grad_b_query[...] = vectors[8:9, : grad_b_query.shape[0]].reshape(-1)
        grad_b_value[...] = vectors[8:9, grad_b_query.shape[0] :].reshape(-1)

    width = grad_w_key.shape[1]
    model = tokens_grad.shape[1]
    tokens_grad[...] = tokens_low[...].astype(F32)
    layer_out[...] = layer_in[...]
    grad_w_up[:, :model] = up_left[...].astype(F32)
    grad_w_up[:, model:] = up_right[...].astype(F32)
    grad_w_down[...] = down[...].astype(F32)
    grad_w_key[...] = key_value[:, :width].astype(F32)
    grad_w_value[...] = key_value[:, width:].astype(F32)
    grad_w_query[...] = query[...].astype(F32)
    grad_w_out[...] = out[...].astype(F32)


def finish(
    tokens_low, layer, sums_ff, sums_rest, vectors, half, sequences
):
    rows, model = tokens_low.shape
    steps = sequences // 2
    length = rows // steps
    width = model // 2
    assert half == 2 * model and steps % 2 == 0
    part = model // steps
    shape = jax.ShapeDtypeStruct

    def block(count, columns, start, column=None):
        offset = start // count
        return pl.BlockSpec((count, columns), lambda i: (offset + i, 0))

    turns = steps // 2
    counts = [model] * 6 + [half, width, width]
    return pl.pallas_call(
        finish_body,
        grid=(steps,),
        in_specs=[
            rows_spec(length, model),
            rows_spec(length, model),
            block(part, model, 0),
            block(part, model, model),
            block(2 * part, model, half),
            block(part, model, 0),
            pl.BlockSpec((part, width), lambda i: (model // part + i % turns, i // turns)),
            block(width // steps, model, model + width),
            whole_spec(vectors),
        ],
        out_specs=[
            rows_spec(length, model),
            rows_spec(length, model),
            rows_spec(part, half),
            rows_spec(2 * part, model),
            rows_spec(part, width),
            rows_spec(part, width),
            rows_spec(part, width),
            rows_spec(width // steps, model),
        ]
        + [pl.BlockSpec((count,), lambda i: (0,)) for count in counts],
        out_shape=[
            shape((rows, model), F32),
            shape((rows, model), BF16),
            shape((model, half), F32),
            shape((half, model), F32),
            shape((model, width), F32),
            shape((model, width), F32),
            shape((model, width), F32),
            shape((width, model), F32),
        ]
        + [shape((count,), F32) for count in counts],
        compiler_params=params(),
        cost_estimate=pl.CostEstimate(
            flops=int(rows * model * 4 * 2 * width),
            bytes_accessed=rows * model * 16,
            transcendentals=0,
        ),
        name="finish",
    )(
        tokens_low,
        layer,
        sums_ff,
        sums_ff,
        sums_ff,
        sums_rest,
        sums_rest,
        sums_rest,
        vectors,
    )


def dense_body(
    chips,
    levels,
    early,
    tokens,
    attended_own,
    attended_local,
    attended_early,
    attended_late,
    w_out,
    w_up_own,
    w_up_peer,
    w_down_own,
    w_down_peer,
    b_up_peer,
    b_up,
    b_out,
    gain_one,
    shift_one,
    b_down,
    gain_two,
    shift_two,
    reduced,
    grads_rest,
    vectors_in,
    layer_out,
    sums_ff,
    sums_rest,
    vectors,
    total,
    other,
    slots,
    last_pieces,
    held_ff,
    held_rest,
    exchanged,
    gained,
    core_sems,
    ring_sems,
    ff_keep_sems,
    ff_sems,
    ff_mate_sems,
    rest_keep_sems,
    rest_sems,
    rest_mate_sems,
    vector_sems,
):
    step = pl.program_id(0)
    steps = pl.num_programs(0)
    model = tokens.shape[1]
    dp = lax.axis_index("dp")
    ring = Ring(chips, total.shape[0], 2)
    ff_ring = Ring(chips, sums_ff.shape[0] // 2, FF_WAYS)
    reduction = Reduce(ring, grads_rest, total, other, slots, core_sems, ring_sems)
    gather_ff = Gather(
        ff_ring,
        reduced,
        held_ff,
        sums_ff,
        ff_keep_sems,
        ff_sems,
        ff_mate_sems,
    )
    gather_rest = Gather(
        ring,
        last_pieces,
        held_rest,
        sums_rest,
        rest_keep_sems,
        rest_sems,
        rest_mate_sems,
    )

    def exchange(level):
        return remote(
            exchanged.at[level],
            gained.at[level],
            vector_sems.at[0, level],
            vector_sems.at[1, level],
            {"dp": flipped(dp, 2**level)},
        )

    def vector_event(level):
        if level > 0:
            exchange(level - 1).wait()
            exchanged[level] = exchanged[level - 1] + gained[level - 1]
        if level < levels:
            exchange(level).start()
        else:
            vectors[...] = exchanged[level]

    def rest_event(event, way):
        @pl.when(event < chips)
        def _():
            reduction.event(event, (way,))

        @pl.when(event == chips - 1)
        def _():
            last_pieces[way] = total[ring.rows(way, reduction.done_segment(way)), :]
            gather_rest.begin((way,))

        @pl.when(event > chips - 1)
        def _():
            gather_rest.event(event - (chips - 1), (way,))

    def point(index):
        def small():
            for way in range(2):
                rest_event(2 * step - 1 + index, way)

        if index == 0:
            pl.when(step > 0)(small)
        else:
            small()

        @pl.when((step > 0) & (step < chips))
        def _():
            gather_ff.event(step, (2 * index, 2 * index + 1))

    @pl.when(step == 0)
    def _():
        greet(ring.neighbours() + tuple({"dp": flipped(dp, 2**level)} for level in range(1, levels)))
        reduction.begin()
        gather_ff.begin(range(FF_WAYS))
        exchanged[0] = vectors_in[...]
        vector_event(0)

    point(0)

    for level in range(1, levels + 1):

        @pl.when(step == jnp.minimum(level, steps - 1))
        def _():
            vector_event(level)

    count = tokens.shape[0] // 2
    split = (slice(0, count), slice(count, 2 * count))

    def first_norm(r):
        attended_peer = jnp.where(
            step < LOCAL,
            attended_local[r, :],
            jnp.where(step < LOCAL + early, attended_early[r, :], attended_late[r, :]),
        )
        attended = jnp.concatenate([attended_own[r, :], attended_peer], axis=1)
        normed, _ = norm_parts(tokens[r, :].astype(F32) + dot(attended, w_out[...]) + row(b_out))
        return normed * row(gain_one) + row(shift_one)

    def forward(layer_low, w_up, w_down, bias):
        hidden = dot(layer_low, w_up[...]) + bias
        return dot((hidden * gelu_share(hidden)).astype(BF16), w_down[...])

    layers = [first_norm(r) for r in split]
    lows = [layer.astype(BF16) for layer in layers]
    sums = [layer + row(b_down) for layer in layers]
    sums[0] = sums[0] + forward(lows[0], w_up_own, w_down_own, row(b_up))
    sums[1] = sums[1] + forward(lows[1], w_up_own, w_down_own, row(b_up))

    @pl.when(step == 0)
    def _():
        reduction.join()

    point(1)
    sums[0] = sums[0] + forward(lows[0], w_up_peer, w_down_peer, b_up_peer[...])
    sums[1] = sums[1] + forward(lows[1], w_up_peer, w_down_peer, b_up_peer[...])
    for r, summed in zip(split, sums):
        normed, _ = norm_parts(summed)
        layer_out[r, :] = (normed * row(gain_two) + row(shift_two)).astype(BF16)

    @pl.when(step == steps - 1)
    def _():
        def more_ff(event, carry):
            gather_ff.event(event, range(FF_WAYS))
            return carry

        def more_rest(event, carry):
            rest_event(event, 0)
            rest_event(event, 1)
            return carry

        lax.fori_loop(steps, chips, more_ff, 0)
        lax.fori_loop(2 * steps - 1, 2 * chips - 1, more_rest, 0)
        gather_ff.finish()
        gather_rest.finish()


def dense_rows(
    tokens,
    attended_own,
    attended_local,
    attended_early,
    attended_late,
    w_out,
    w_up_own,
    w_up_peer,
    w_down_own,
    w_down_peer,
    b_up_peer,
    singles,
    reduced,
    grads_rest,
    vectors,
    sequences,
    chips,
):
    rows, model = tokens.shape
    half = w_up_own.shape[1]
    block = rows // sequences
    levels = (2 * chips).bit_length() - 1
    assert 2**levels == 2 * chips
    share = grads_rest.shape[0] // 2
    ff_rows = reduced.shape[0] * reduced.shape[1] * 2 * chips
    piece = (share // (2 * chips), model)
    shape = jax.ShapeDtypeStruct
    anywhere = pl.BlockSpec(memory_space=pl.ANY)
    arrays = (w_out, w_up_own, w_up_peer, w_down_own, w_down_peer, b_up_peer)
    early = attended_early.shape[0] // block
    late = attended_late.shape[0] // block
    dma = pltpu.SemaphoreType.DMA
    return pl.pallas_call(
        functools.partial(dense_body, chips, levels, early),
        grid=(sequences,),
        in_specs=[
            rows_spec(block, model),
            rows_spec(block, model // 2),
            pl.BlockSpec((block, model // 2), lambda i: (jnp.minimum(i, LOCAL - 1), 0)),
            pl.BlockSpec((block, model // 2), lambda i: (jnp.clip(i - LOCAL, 0, early - 1), 0)),
            pl.BlockSpec(
                (block, model // 2), lambda i: (jnp.clip(i - LOCAL - early, 0, late - 1), 0)
            ),
        ]
        + [whole_spec(array) for array in arrays]
        + [vector_spec(array) for array in singles]
        + [
            pl.BlockSpec(reduced.shape, lambda i: (0, 0, 0), pipeline_mode=pl.Buffered(1)),
            anywhere,
            whole_spec(vectors),
        ],
        out_specs=[
            rows_spec(block, model),
            anywhere,
            anywhere,
            pl.BlockSpec(vectors.shape, lambda i: (0, 0)),
        ],
        out_shape=[
            shape((rows, model), BF16),
            shape((ff_rows, model), BF16),
            shape(grads_rest.shape, BF16),
            shape(vectors.shape, F32),
        ],
        scratch_shapes=[
            pltpu.VMEM((share, model), BF16),
            pltpu.VMEM((share, model), BF16),
            pltpu.VMEM((2, chips - 1) + piece, BF16),
            pltpu.VMEM((2,) + piece, BF16),
            pltpu.VMEM((ff_rows, model), BF16),
            pltpu.VMEM(grads_rest.shape, BF16),
            pltpu.VMEM((levels + 1,) + vectors.shape, F32),
            pltpu.VMEM((levels,) + vectors.shape, F32),
            dma((3,)),
            dma((2, 2, chips - 1)),
            dma((2, FF_WAYS, chips)),
            dma((2, FF_WAYS, chips - 1)),
            dma((2, FF_WAYS, chips)),
            dma((2, 2, chips)),
            dma((2, 2, chips - 1)),
            dma((2, 2, chips)),
            dma((2, levels)),
        ],
        compiler_params=pltpu.CompilerParams(
            vmem_limit_bytes=VMEM_BYTES, collective_id=2, has_side_effects=True
        ),
        cost_estimate=pl.CostEstimate(
            flops=int(rows * model * (8 * half + 2 * model)),
            bytes_accessed=rows * model * 6,
            transcendentals=rows * half * 2,
        ),
        name="dense",
    )(
        tokens,
        attended_own,
        attended_local,
        attended_early,
        attended_late,
        *arrays,
        *singles,
        reduced,
        grads_rest,
        vectors,
    )


def on_device(
    chips,
    tokens,
    out_grad,
    positions,
    w_query,
    b_query,
    w_key,
    w_value,
    b_value,
    w_out,
    b_out,
    gain_one,
    shift_one,
    w_up,
    b_up,
    w_down,
    b_down,
    gain_two,
    shift_two,
):
    sequences, count = positions.shape
    half = w_up.shape[1]
    taken = -(-count // 16) * 16
    (
        attended,
        attended_local,
        keys,
        values,
        picked_q,
        picked_tokens,
        picked_grad,
        picks,
        picked_att,
        qkv_all,
        out_all,
        up_peer,
        down_peer,
        b_up_peer,
    ) = attention(
        tokens,
        out_grad,
        positions,
        w_query,
        w_key,
        w_value,
        w_out,
        w_up,
        w_down,
        b_query,
        b_value,
        b_up,
        taken,
    )
    length = tokens.shape[0] // sequences
    early = (sequences - LOCAL) // 3 * length
    late = tokens.shape[0] - LOCAL * length - early
    weights = (out_all, w_up, up_peer, w_down, down_peer, b_up_peer)
    singles = (b_up, b_out, gain_one, shift_one, b_down, gain_two)
    back_one, att_grad, grad_ff, grad_w_out, vectors, attended_early = marked_rows(
        picked_tokens, picked_att, picked_grad, *weights, singles, attended, early, late, chips
    )
    tokens_low, grads_rest, vectors, reduced, attended_late = attention_back(
        tokens,
        keys,
        values,
        picked_q,
        att_grad,
        back_one,
        picks,
        picked_tokens,
        qkv_all,
        grad_w_out,
        vectors,
        grad_ff,
        attended,
        late,
        sequences,
        chips,
    )
    layer, sums_ff, sums_rest, vectors = dense_rows(
        tokens,
        attended,
        attended_local,
        attended_early,
        attended_late,
        *weights,
        singles + (shift_two,),
        reduced,
        grads_rest,
        vectors,
        sequences,
        chips,
    )
    (
        tokens_grad,
        layer_out,
        grad_w_up,
        grad_w_down,
        grad_w_key,
        grad_w_value,
        grad_w_query,
        grad_w_out,
        grad_b_out,
        grad_gain_one,
        grad_shift_one,
        grad_b_down,
        grad_gain_two,
        grad_shift_two,
        grad_b_up,
        grad_b_query,
        grad_b_value,
    ) = finish(
        tokens_low, layer, sums_ff, sums_rest, vectors, half, sequences
    )
    return (
        layer_out,
        tokens_grad,
        grad_w_query,
        grad_b_query,
        grad_w_key,
        grad_w_value,
        grad_b_value,
        grad_w_out,
        grad_b_out,
        grad_gain_one,
        grad_shift_one,
        grad_w_up,
        grad_b_up,
        grad_w_down,
        grad_b_down,
        grad_gain_two,
        grad_shift_two,
    )


def solution(mesh):
    across = P("dp", None)
    columns, rows, split, copied = P(None, "tensor"), P("tensor", None), P("tensor"), P()
    in_specs = (
        across,
        across,
        across,
        columns,
        split,
        columns,
        columns,
        split,
        rows,
        copied,
        copied,
        copied,
        columns,
        split,
        rows,
        copied,
        copied,
        copied,
    )
    out_specs = (
        across,
        across,
        columns,
        split,
        columns,
        columns,
        split,
        rows,
        copied,
        copied,
        copied,
        columns,
        split,
        rows,
        copied,
        copied,
        copied,
    )
    return jax.shard_map(
        functools.partial(on_device, mesh.shape["dp"] // 2), mesh=mesh, in_specs=in_specs, out_specs=out_specs, check_vma=False
    )
```

```python
import functools
import math

import jax
import jax.numpy as jnp
from jax import lax
from jax.experimental import pallas as pl
from jax.experimental.pallas import tpu as pltpu
from jax.sharding import PartitionSpec as P

HD = 64
NORM_EPSILON = 1e-12
BF16 = jnp.bfloat16
F32 = jnp.float32
EXPONENT = HD**-0.5 * math.log2(math.e)
ROOT_HALF = 0.7071067811865476
DENSITY = 0.3989422804014327
VMEM_BYTES = 58 * 2**20
FF_WAYS = 4
LOCAL = 2


def dot(left, right):
    return jnp.dot(left, right, preferred_element_type=F32)


def dot_nt(left, right):
    return lax.dot_general(left, right, (((1,), (1,)), ((), ())), preferred_element_type=F32)


def dot_tn(left, right):
    return lax.dot_general(left, right, (((0,), (0,)), ((), ())), preferred_element_type=F32)


def norm_parts(summed):
    centred = summed - jnp.mean(summed, axis=-1, keepdims=True)
    inverse = lax.rsqrt(jnp.mean(centred * centred, axis=-1, keepdims=True) + NORM_EPSILON)
    return centred * inverse, inverse


def norm_back(upstream, normed, inverse, gain):
    scaled = upstream * gain
    return inverse * (
        scaled
        - jnp.mean(scaled, axis=-1, keepdims=True)
        - normed * jnp.mean(scaled * normed, axis=-1, keepdims=True)
    )


def row(vector):
    return vector[...].reshape(1, -1)


def row_sum(values):
    return jnp.sum(values, axis=0, keepdims=True)


def rows_spec(rows, width):
    return pl.BlockSpec((rows, width), lambda i: (i, 0))


def vector_spec(array):
    return pl.BlockSpec(array.shape, lambda i: (0,))


def whole_spec(array):
    return pl.BlockSpec(array.shape, lambda i: (0, 0), pipeline_mode=pl.Buffered(1))


def params():
    return pltpu.CompilerParams(vmem_limit_bytes=VMEM_BYTES)


def flipped(index, span):
    return index + span - 2 * span * ((index // span) % 2)


def remote(source, target, send, receive, device):
    return pltpu.make_async_remote_copy(
        src_ref=source,
        dst_ref=target,
        send_sem=send,
        recv_sem=receive,
        device_id=device,
        device_id_type=pl.DeviceIdType.MESH,
    )


def greet(devices):
    barrier = pltpu.get_barrier_semaphore()
    for device in devices:
        pl.semaphore_signal(barrier, inc=1, device_id=device, device_id_type=pl.DeviceIdType.MESH)
    pl.semaphore_wait(barrier, len(devices))


PIECES = 8


class Fetch:
    def __init__(self, source, target, send_sems, recv_sems, first, second):
        self.source, self.target = source, target
        self.send_sems, self.recv_sems = send_sems, recv_sems
        self.dp = lax.axis_index("dp")
        self.hops = ((0, 0), (first, 0), (second, 0), (second, first)) + tuple(
            (1, flips) for flips in (0, first, second, first + second)
        )

    def _copy(self, source, piece, hop):
        count = self.target.shape[0] // PIECES
        rows = pl.ds(pl.multiple_of(piece * count, 16), count)
        if hop:
            device = {"dp": flipped(self.dp, self.hops[hop][0])}
        else:
            device = {"tensor": 1 - lax.axis_index("tensor")}
        return remote(
            source.at[rows], self.target.at[rows], self.send_sems.at[hop], self.recv_sems.at[hop], device
        )

    def _piece(self, flips):
        piece = self.dp % PIECES
        for span in (4, 2, 1):
            if flips & span:
                piece = flipped(piece, span)
        return piece

    def out(self, hop):
        return self._copy(
            self.target if hop else self.source, self._piece(self.hops[hop][1]), hop
        )

    def into(self, hop):
        return self._copy(self.target, self._piece(self.hops[hop][0] | self.hops[hop][1]), hop)

    def move(self, what):
        if what == "x":
            self.out(0).start()
        if what == "z":
            self.into(0).wait_recv()
            for hop in (1, 2, 4):
                self.out(hop).start()
        if what == "y":
            self.into(1).wait_recv()
            for hop in (3, 5):
                self.out(hop).start()
        if what == "c":
            self.into(2).wait_recv()
            self.into(3).wait_recv()
            for hop in (6, 7):
                self.out(hop).start()
        if what == "end":
            for hop in (4, 5, 6, 7):
                self.into(hop).wait_recv()


def attention_body(
    tokens,
    out_grad,
    positions,
    w_query,
    w_key,
    w_value,
    w_out,
    w_up,
    w_down,
    b_query,
    b_value,
    b_up,
    attended,
    attended_local,
    keys,
    values,
    picked_q,
    picked_tokens,
    picked_grad,
    picks,
    picked_att,
    qkv_all,
    out_all,
    up_peer,
    down_peer,
    b_up_peer,
    qkv,
    biases,
    up_biases,
    kept_tokens,
    kept_picks,
    kept_att,
    kept_local,
    places,
    local_sems,
    send_sems,
    recv_sems,
    bias_sems,
    att_sems,
):
    step = pl.program_id(0)
    sequences = pl.num_programs(0) // 2
    sequence = step % sequences
    turn = step // sequences
    length = tokens.shape[0]
    width = keys.shape[1]
    model = tokens.shape[1]
    taken = picks.shape[0]
    dp = lax.axis_index("dp")
    across = {"tensor": 1 - lax.axis_index("tensor")}

    def halves(source, target):
        rows = target.shape[0] // 2
        return [(source.at[pl.ds(i * rows, rows)], target.at[pl.ds(i * rows, rows)]) for i in range(2)]

    pairs = (
        [(w_out, out_all.at[pl.ds(width, width)])]
        + halves(qkv.at[0], qkv.at[1])
        + halves(w_up, up_peer)
        + halves(w_down, down_peer)
    )
    fetches = [
        Fetch(source, target, send_sems.at[i], recv_sems.at[i], *((4, 2), (2, 4))[i % 2])
        for i, (source, target) in enumerate(pairs)
    ]
    bias_copies = [
        remote(source, target, bias_sems.at[0, i], bias_sems.at[1, i], across)
        for i, (source, target) in enumerate(
            (
                (biases.at[0], biases.at[1]),
                (biases.at[2], biases.at[3]),
                (up_biases, b_up_peer),
            )
        )
    ]

    far = pl.ds(LOCAL * taken, (sequences - LOCAL) * taken)
    att_copy = remote(
        kept_att.at[far],
        picked_att.at[far, pl.ds(width, width)],
        att_sems.at[0],
        att_sems.at[1],
        across,
    )

    loads = [
        pltpu.make_async_copy(weight, qkv.at[0, :, pl.ds(i * width, width)], local_sems.at[i])
        for i, weight in enumerate((w_query, w_key, w_value))
    ]
    keep_out = pltpu.make_async_copy(w_out, out_all.at[pl.ds(0, width)], local_sems.at[3])
    keep_qkv = pltpu.make_async_copy(qkv, qkv_all, local_sems.at[4])
    keep_att = pltpu.make_async_copy(kept_att, picked_att.at[:, pl.ds(0, width)], local_sems.at[5])
    keep_local = pltpu.make_async_copy(
        kept_local, picked_att.at[pl.ds(0, LOCAL * taken), pl.ds(width, width)], local_sems.at[6]
    )

    @pl.when(step == 0)
    def _():
        for load in loads:
            load.start()
        keep_out.start()
        places[...] = jnp.full(places.shape, -1, jnp.int32)
        places[:, : positions.shape[1]] = positions[...]
        biases[0] = row(b_query)
        biases[2] = row(b_value)
        up_biases[...] = row(b_up)
        greet((across,) + tuple({"dp": flipped(dp, span)} for span in (1, 2, 4)))
        fetches[0].move("x")
        for load in loads:
            load.wait()
        fetches[1].move("x")
        fetches[2].move("x")
        for copy in bias_copies:
            copy.start()

    moves = {
        1: [(3, "x")],
        2: [(0, "z"), (1, "z")],
        3: [(2, "z"), (4, "x")],
        4: [(3, "z"), (0, "y"), (1, "y"), (5, "x")],
        5: [(4, "z"), (2, "y"), (6, "x")],
        6: [(3, "y"), (0, "c"), (1, "c")],
        7: [(5, "z"), (6, "z"), (4, "y"), (2, "c")],
        8: [(1, "end"), (2, "end")],
        9: [(5, "y"), (6, "y"), (3, "c")],
        10: [(4, "c"), (5, "c")],
        14: [(6, "c")],
    }
    for when, made in moves.items():

        @pl.when(step == when)
        def _():
            for index, what in made:
                fetches[index].move(what)

    @pl.when(step == sequences)
    def _():
        bias_copies[0].wait_recv()
        bias_copies[1].wait_recv()
        keep_qkv.start()
        keep_att.start()
        att_copy.start()

    def attend(query, key, value, outcome):
        pair = 2 * HD
        first = lax.broadcasted_iota(jnp.int32, (length, pair), 1) < HD
        zero = jnp.zeros((length, pair), BF16)
        one = jnp.ones((length, pair), BF16)
        for p in range(width // pair):
            here = slice(p * pair, (p + 1) * pair)
            k, v = key[:, here], value[:, here]
            k_two = jnp.concatenate([jnp.where(first, k, zero), jnp.where(first, zero, k)], axis=0)
            v_two = jnp.concatenate(
                [
                    jnp.concatenate(
                        [jnp.where(first, v, zero), jnp.where(first, one, zero)], axis=1
                    ),
                    jnp.concatenate(
                        [jnp.where(first, zero, v), jnp.where(first, zero, one)], axis=1
                    ),
                ],
                axis=0,
            )
            scores = dot_nt(query[:, here], k_two)
            left, right = scores[:, :length], scores[:, length:]
            left = jnp.exp2((left - jnp.max(left, axis=1, keepdims=True)) * EXPONENT).astype(BF16)
            right = jnp.exp2((right - jnp.max(right, axis=1, keepdims=True)) * EXPONENT).astype(
                BF16
            )
            both = dot(jnp.concatenate([left, right], axis=1), v_two)
            outcome[:, here] = (both[:, :pair] / both[:, pair:]).astype(BF16)

    rows = pl.ds(pl.multiple_of(sequence * taken, 16), taken)

    @pl.when(turn == 0)
    def _():
        tokens_here = tokens[...]
        projected = dot(tokens_here, qkv[0])
        query = (projected[:, :width] + biases[0]).astype(BF16)
        key = projected[:, width : 2 * width].astype(BF16)
        value = (projected[:, 2 * width :] + biases[2]).astype(BF16)
        keys[...] = key
        values[...] = value
        attend(query, key, value, attended)

        spread = jnp.broadcast_to(places[pl.ds(sequence, 1), :], (length, places.shape[1]))
        column = lax.broadcasted_iota(jnp.int32, spread.shape, 1).astype(F32)
        hit = spread == lax.broadcasted_iota(jnp.int32, spread.shape, 0)
        earliest = jnp.min(jnp.where(hit, column, 1e6), axis=1, keepdims=True)
        pick = jnp.where(column == earliest, 1.0, 0.0).T[:taken].astype(BF16)
        picks[...] = pick
        tokens_low = dot(pick, tokens_here).astype(BF16)
        picked_tokens[...] = tokens_low
        picked_grad[...] = dot(pick, out_grad[...]).astype(BF16)
        picked_q[...] = dot(pick, query).astype(BF16)
        kept_tokens[rows, :] = tokens_low
        kept_picks[rows, :] = pick
        kept_att[rows, :] = dot(pick, attended[...]).astype(BF16)

    @pl.when((turn == 1) & (sequence < LOCAL))
    def _():
        projected = dot(tokens[...], qkv[1])
        query = (projected[:, :width] + biases[1]).astype(BF16)
        key = projected[:, width : 2 * width].astype(BF16)
        value = (projected[:, 2 * width :] + biases[3]).astype(BF16)
        keys[...] = key
        values[...] = value
        attend(query, key, value, attended_local)
        pick = kept_picks[rows, :]
        picked_q[...] = dot(pick, query).astype(BF16)
        kept_local[pl.ds(pl.multiple_of(sequence % LOCAL * taken, 16), taken), :] = dot(
            pick, attended_local[...]
        ).astype(BF16)

    @pl.when((turn == 1) & (sequence >= LOCAL))
    def _():
        projected = dot(tokens[...], qkv[1, :, width:])
        keys[...] = projected[:, :width].astype(BF16)
        values[...] = (projected[:, width:] + biases[3]).astype(BF16)
        picked_q[...] = (dot(kept_tokens[rows, :], qkv[1, :, :width]) + biases[1]).astype(BF16)

    @pl.when(step == 2 * sequences - 1)
    def _():
        keep_local.start()
        for index in (0, 3, 4, 5, 6):
            fetches[index].move("end")
        bias_copies[2].wait_recv()
        for fetch in fetches:
            for hop in range(PIECES):
                fetch.out(hop).wait_send()
        for copy in bias_copies:
            copy.wait_send()
        att_copy.wait()
        keep_out.wait()
        keep_qkv.wait()
        keep_att.wait()
        keep_local.wait()


def attention(
    tokens, out_grad, positions, w_query, w_key, w_value, w_out, w_up, w_down, b_query, b_value, b_up, taken
):
    rows, model = tokens.shape
    sequences = positions.shape[0]
    length = rows // sequences
    width = w_query.shape[1]
    shape = jax.ShapeDtypeStruct
    slots = sequences * taken

    def both(count, columns):
        return pl.BlockSpec((count, columns), lambda s: (s % sequences, s // sequences))

    def once(count, columns):
        return pl.BlockSpec((count, columns), lambda s: (jnp.minimum(s, sequences - 1), 0))

    def again(count, columns):
        return pl.BlockSpec((count, columns), lambda s: (s % sequences, 0))

    anywhere = pl.BlockSpec(memory_space=pl.ANY)
    dma = pltpu.SemaphoreType.DMA
    return pl.pallas_call(
        attention_body,
        grid=(2 * sequences,),
        in_specs=[
            again(length, model),
            once(length, model),
            pl.BlockSpec(positions.shape, lambda s: (0, 0)),
        ]
        + [anywhere] * 6
        + [vector_spec(array) for array in (b_query, b_value, b_up)],
        out_specs=[
            once(length, width),
            pl.BlockSpec((length, width), lambda s: (jnp.clip(s - sequences, 0, LOCAL - 1), 0)),
            both(length, width),
            both(length, width),
            both(taken, width),
            once(taken, model),
            once(taken, model),
            once(taken, length),
        ]
        + [anywhere] * 6,
        out_shape=[
            shape((rows, width), BF16),
            shape((LOCAL * length, width), BF16),
            shape((rows, 2 * width), BF16),
            shape((rows, 2 * width), BF16),
            shape((slots, 2 * width), BF16),
            shape((slots, model), BF16),
            shape((slots, model), BF16),
            shape((slots, length), BF16),
            shape((slots, 2 * width), BF16),
            shape((2, model, 3 * width), BF16),
            shape((2 * width, model), BF16),
            shape(w_up.shape, BF16),
            shape(w_down.shape, BF16),
            shape((1, w_up.shape[1]), F32),
        ],
        scratch_shapes=[
            pltpu.VMEM((2, model, 3 * width), BF16),
            pltpu.VMEM((4, 1, width), F32),
            pltpu.VMEM((1, w_up.shape[1]), F32),
            pltpu.VMEM((slots, model), BF16),
            pltpu.VMEM((slots, length), BF16),
            pltpu.VMEM((slots, width), BF16),
            pltpu.VMEM((LOCAL * taken, width), BF16),
            pltpu.VMEM((sequences, -(-positions.shape[1] // 128) * 128), jnp.int32),
            dma((7,)),
            dma((7, PIECES)),
            dma((7, PIECES)),
            dma((2, 3)),
            dma((2,)),
        ],
        compiler_params=pltpu.CompilerParams(
            vmem_limit_bytes=VMEM_BYTES, collective_id=0, has_side_effects=True
        ),
        cost_estimate=pl.CostEstimate(
            flops=int(rows * width * (10 * model + 16 * length)),
            bytes_accessed=rows * model * 12,
            transcendentals=rows * length * width // HD,
        ),
        name="attention",
    )(tokens, out_grad, positions, w_query, w_key, w_value, w_out, w_up, w_down, b_query, b_value, b_up)


def gelu_share(hidden):
    return 0.5 * (1.0 + lax.erf(hidden * ROOT_HALF))


def marked_body(
    late,
    tokens,
    picked_att,
    upstream,
    w_out,
    w_up_own_hbm,
    w_up_peer_hbm,
    w_down_own_hbm,
    w_down_peer_hbm,
    b_up_peer,
    b_up,
    b_out,
    gain_one,
    shift_one,
    b_down,
    gain_two,
    attended,
    back_one_out,
    attended_grad,
    grad_ff_hbm,
    grad_w_out,
    vectors,
    attended_peer,
    w_up,
    w_down,
    grad_ff,
    slope,
    active,
    load_sems,
    store_sems,
    att_sems,
):
    model = tokens.shape[1]
    width = model // 2
    half = w_up.shape[2]
    loads = [
        pltpu.make_async_copy(source, target, load_sems.at[i])
        for i, (source, target) in enumerate(
            (
                (w_up_own_hbm, w_up.at[0]),
                (w_down_own_hbm, w_down.at[0]),
                (w_up_peer_hbm, w_up.at[1]),
                (w_down_peer_hbm, w_down.at[1]),
            )
        )
    ]
    for load in loads:
        load.start()
    across = {"tensor": 1 - lax.axis_index("tensor")}
    share = remote(
        attended.at[pl.ds(attended.shape[0] - attended_peer.shape[0] - late, attended_peer.shape[0])],
        attended_peer,
        att_sems.at[0],
        att_sems.at[1],
        across,
    )
    count = tokens.shape[0] // 2
    split = (slice(0, count), slice(count, 2 * count))
    ones = [
        norm_parts(
            tokens[r, :].astype(F32) + dot(picked_att[r, :], w_out[...]) + row(b_out)
        )
        for r in split
    ]
    layers = [normed * row(gain_one) + row(shift_one) for normed, _ in ones]
    lows = [layer.astype(BF16) for layer in layers]
    sums = [layer + row(b_down) for layer in layers]
    greet((across,))
    share.start()
    for part in range(2):
        loads[2 * part].wait()
        bias = b_up_peer[...] if part else row(b_up)
        for i, r in enumerate(split):
            hidden = dot(lows[i], w_up[part]) + bias
            gate = gelu_share(hidden)
            act = (hidden * gate).astype(BF16)
            slope[part, r, :] = gate + hidden * jnp.exp(-0.5 * hidden * hidden) * DENSITY
            if part == 0:
                active[r, :] = act
            if i == 0:
                loads[2 * part + 1].wait()
            sums[i] = sums[i] + dot(act, w_down[part])
    twos = [norm_parts(summed) for summed in sums]
    ups = [upstream[r, :].astype(F32) for r in split]
    backs = [
        norm_back(up, normed, inverse, row(gain_two)) for up, (normed, inverse) in zip(ups, twos)
    ]
    back_lows = [back.astype(BF16) for back in backs]
    layer_low = jnp.concatenate(lows, axis=0)
    back_low = jnp.concatenate(back_lows, axis=0)
    layer_grads = list(backs)
    stores = [
        pltpu.make_async_copy(
            grad_ff.at[pl.ds(i * half, half)], grad_ff_hbm.at[pl.ds(i * half, half)], store_sems.at[i]
        )
        for i in range(2)
    ]
    grad_ff[half : 2 * half, :] = dot_tn(active[...], back_low).astype(BF16)
    stores[1].start()
    for part in range(2):
        hidden_grads = []
        for i, r in enumerate(split):
            hidden_grad = (dot_nt(back_lows[i], w_down[part]) * slope[part, r, :]).astype(BF16)
            layer_grads[i] = layer_grads[i] + dot_nt(hidden_grad, w_up[part])
            hidden_grads.append(hidden_grad)
        if part == 0:
            hidden_grad = jnp.concatenate(hidden_grads, axis=0)
            grad_b_up = row_sum(hidden_grad.astype(F32))
            for c in range(0, half, model):
                grad_ff[c : c + model, :] = dot_tn(layer_low, hidden_grad[:, c : c + model]).astype(
                    BF16
                )
            stores[0].start()
    back_ones = [
        norm_back(grad, normed, inverse, row(gain_one))
        for grad, (normed, inverse) in zip(layer_grads, ones)
    ]
    back_one_low = jnp.concatenate([back.astype(BF16) for back in back_ones], axis=0)
    for r, back in zip(split, back_ones):
        back_one_out[r, :] = back
    grad_w_out[...] = dot_tn(picked_att[:, :width], back_one_low).astype(BF16)
    attended_grad[...] = dot_nt(back_one_low, w_out[...]).astype(BF16)

    def total(pieces):
        return row_sum(pieces[0]) + row_sum(pieces[1])

    vectors[...] = jnp.concatenate(
        [
            total(back_ones),
            total([grad * normed for grad, (normed, _) in zip(layer_grads, ones)]),
            total(layer_grads),
            total(backs),
            total([up * normed for up, (normed, _) in zip(ups, twos)]),
            total(ups),
        ]
        + [grad_b_up[:, c : c + model] for c in range(0, half, model)],
        axis=0,
    )
    for store in stores:
        store.wait()
    share.wait()


def marked_rows(
    picked_tokens,
    picked_att,
    picked_grad,
    out_all,
    w_up,
    up_peer,
    w_down,
    down_peer,
    b_up_peer,
    vectors,
    attended,
    early,
    late,
    chips,
):
    rows, model = picked_tokens.shape
    width = model // 2
    half = w_up.shape[1]
    shape = jax.ShapeDtypeStruct
    inside = pl.BlockSpec(memory_space=pltpu.VMEM)
    anywhere = pl.BlockSpec(memory_space=pl.ANY)
    dma = pltpu.SemaphoreType.DMA
    return pl.pallas_call(
        functools.partial(marked_body, late),
        in_specs=[inside] * 4 + [anywhere] * 4 + [inside] * (1 + len(vectors)) + [anywhere],
        out_specs=[inside, inside, anywhere, inside, inside, anywhere],
        out_shape=[
            shape((rows, model), F32),
            shape((rows, 2 * width), BF16),
            shape((padded_rows(2 * half, chips, FF_WAYS), model), BF16),
            shape((width, model), BF16),
            shape((6 + half // model, model), F32),
            shape((early, width), BF16),
        ],
        scratch_shapes=[
            pltpu.VMEM((2, model, half), BF16),
            pltpu.VMEM((2, half, model), BF16),
            pltpu.VMEM((2 * half, model), BF16),
            pltpu.VMEM((2, rows, half), F32),
            pltpu.VMEM((rows, half), BF16),
            dma((4,)),
            dma((2,)),
            dma((2,)),
        ],
        compiler_params=pltpu.CompilerParams(
            vmem_limit_bytes=VMEM_BYTES, collective_id=3, has_side_effects=True
        ),
        cost_estimate=pl.CostEstimate(
            flops=int(rows * model * (2 * half * 10 + 2 * width * 5)),
            bytes_accessed=6 * model * half * 2,
            transcendentals=rows * half * 4,
        ),
        name="marked",
    )(
        picked_tokens,
        picked_att,
        picked_grad,
        out_all,
        w_up,
        up_peer,
        w_down,
        down_peer,
        b_up_peer,
        *vectors,
        attended,
    )


class Ring:
    def __init__(self, chips, share, ways):
        self.chips, self.ways, self.count = chips, ways, share // (ways * chips)
        self.share = share
        dp = lax.axis_index("dp")
        self.core, chip = dp % 2, dp // 2
        self.place = self.at(chip)
        self.mate = {"dp": flipped(dp, 1)}
        self.up = {"dp": self.device(self.place + 1)}
        self.down = {"dp": self.device(self.place + chips - 1)}

    def at(self, chip):
        high, low = chip // 2, chip % 2
        return (1 - low) * high + low * (self.chips - 1 - high)

    def device(self, place):
        place = place % self.chips
        back = place // (self.chips // 2)
        chip = (1 - back) * 2 * place + back * (2 * (self.chips - 1 - place) + 1)
        return 2 * chip + self.core

    def neighbours(self):
        return self.up, self.down, self.mate

    def onward(self, way):
        return (self.up, self.down)[way % 2]

    def segment(self, way, step):
        sign = 1 - 2 * (way % 2)
        return (self.place - sign * step + 2 * self.chips) % self.chips

    def rows(self, way, segment):
        return pl.ds(pl.multiple_of((way * self.chips + segment) * self.count, 16), self.count)

    def final_rows(self, way, segment, core):
        start = core * self.share + (way * self.chips + segment) * self.count
        return pl.ds(pl.multiple_of(start, 16), self.count)


class Reduce:
    def __init__(self, ring, source, total, other, slots, core_sems, sems):
        self.ring, self.source, self.total, self.other = ring, source, total, other
        self.slots, self.core_sems, self.sems = slots, core_sems, sems

    def _core(self):
        ring = self.ring
        give = pl.ds(pl.multiple_of((1 - ring.core) * ring.share, 16), ring.share)
        keep = pl.ds(pl.multiple_of(ring.core * ring.share, 16), ring.share)
        return (
            remote(
                self.source.at[give],
                self.other,
                self.core_sems.at[0],
                self.core_sems.at[1],
                ring.mate,
            ),
            pltpu.make_async_copy(self.source.at[keep], self.total, self.core_sems.at[2]),
        )

    def begin(self):
        given, kept = self._core()
        given.start()
        kept.start()

    def join(self):
        given, kept = self._core()
        kept.wait()
        given.wait()
        self.total[...] += self.other[...]

    def _copy(self, way, step):
        ring = self.ring
        return remote(
            self.total.at[ring.rows(way, ring.segment(way, step))],
            self.slots.at[way, step],
            self.sems.at[0, way, step],
            self.sems.at[1, way, step],
            ring.onward(way),
        )

    def event(self, step, ways):
        ring = self.ring

        @pl.when(step > 0)
        def _():
            for way in ways:
                self._copy(way, step - 1).wait()
                here = ring.rows(way, ring.segment(way, step))
                self.total[here, :] += self.slots[way, step - 1]

        @pl.when(step < ring.chips - 1)
        def _():
            for way in ways:
                self._copy(way, step).start()

    def done_segment(self, way):
        return self.ring.segment(way, self.ring.chips - 1)


class Gather:
    def __init__(self, ring, firsts, held, out, store_sems, sems, mate_sems):
        self.ring, self.firsts, self.held, self.out = ring, firsts, held, out
        self.store_sems, self.sems, self.mate_sems = store_sems, sems, mate_sems

    def _rows(self, way, step, core):
        ring, sign = self.ring, 1 - 2 * (way % 2)
        segment = (ring.place + sign - sign * step + 2 * ring.chips) % ring.chips
        return ring.final_rows(way, segment, core)

    def _store(self, way, step, core, which):
        rows = self._rows(way, step, core)
        return pltpu.make_async_copy(
            self.held.at[rows], self.out.at[rows], self.store_sems.at[which, way, step]
        )

    def _own(self, way, step):
        return self._store(way, step, self.ring.core, 0)

    def _mates(self, way, step):
        return self._store(way, step, 1 - self.ring.core, 1)

    def _send(self, way, step):
        here = self.held.at[self._rows(way, step, self.ring.core)]
        return remote(
            here, here, self.sems.at[0, way, step], self.sems.at[1, way, step], self.ring.onward(way)
        )

    def _arrive(self, way, step):
        here = self.held.at[self._rows(way, step + 1, self.ring.core)]
        return remote(
            here, here, self.sems.at[0, way, step], self.sems.at[1, way, step], self.ring.onward(way)
        )

    def _mate(self, way, step, core):
        here = self.held.at[self._rows(way, step, core)]
        return remote(
            here,
            here,
            self.mate_sems.at[0, way, step],
            self.mate_sems.at[1, way, step],
            self.ring.mate,
        )

    def _pass_on(self, step, ways):
        for way in ways:

            @pl.when(step < self.ring.chips - 1)
            def _():
                self._send(way, step).start()

            self._mate(way, step, self.ring.core).start()
            self._own(way, step).start()

    def begin(self, ways):
        for way in ways:
            self.held[self._rows(way, 0, self.ring.core), :] = self.firsts[way]
        self._pass_on(0, ways)

    def event(self, step, ways):
        for way in ways:
            self._arrive(way, step - 1).wait_recv()
        self._pass_on(step, ways)
        for way in ways:
            self._mate(way, step - 1, 1 - self.ring.core).wait_recv()
            self._mates(way, step - 1).start()

    def finish(self):
        last = self.ring.chips - 1
        ways = range(self.ring.ways)
        for way in ways:
            self._mate(way, last, 1 - self.ring.core).wait_recv()
            self._mates(way, last).start()

        def rest(step, carry):
            for way in ways:

                @pl.when(step < last)
                def _():
                    self._send(way, step).wait_send()

                self._mate(way, step, self.ring.core).wait_send()
                self._own(way, step).wait()
                self._mates(way, step).wait()
            return carry

        lax.fori_loop(0, self.ring.chips, rest, 0)


def backward_body(
    chips,
    tokens,
    keys,
    values,
    queries,
    grads,
    back_one,
    picks,
    picked_tokens,
    qkv_all,
    grad_w_out,
    vectors_in,
    grad_ff,
    attended,
    tokens_low,
    grads_rest,
    vectors,
    reduced,
    attended_peer,
    query_grads,
    sums,
    total,
    other,
    slots,
    core_sems,
    ring_sems,
    att_sems,
):
    step = pl.program_id(0)
    last = pl.num_programs(0) - 1
    model = tokens.shape[1]
    width = keys.shape[1] // 2
    taken = queries.shape[0]
    factor = HD**-0.5
    group, span = 3, 4 * HD
    assert width == 2 * group * HD
    ring = Ring(chips, total.shape[0], FF_WAYS)
    reduction = Reduce(ring, grad_ff, total, other, slots, core_sems, ring_sems)
    across = {"tensor": 1 - lax.axis_index("tensor")}
    shared_rows = attended_peer.shape[0]
    share = remote(
        attended.at[pl.ds(attended.shape[0] - shared_rows, shared_rows)],
        attended_peer,
        att_sems.at[0],
        att_sems.at[1],
        across,
    )

    @pl.when(step == 0)
    def _():
        sums[...] = jnp.zeros_like(sums)
        vectors[...] = jnp.zeros_like(vectors)
        greet(ring.neighbours() + (across,))
        reduction.begin()
        share.start()

    @pl.when(step == 1)
    def _():
        reduction.join()

    @pl.when(step > 0)
    def _():
        reduction.event(step - 1, range(FF_WAYS))

    head = lax.broadcasted_iota(jnp.int32, (taken, span), 1) // HD

    def stacked(block, skip):
        zero = jnp.zeros_like(block)
        return jnp.concatenate(
            [jnp.where(head == j + skip, block, zero) for j in range(group)], axis=0
        )

    def unstacked(block, skip):
        zero = jnp.zeros((taken, span), F32)
        return sum(
            jnp.where(head == j + skip, block[j * taken : (j + 1) * taken], zero)
            for j in range(group)
        )

    def joined(early, late):
        cut = span // 2
        return jnp.concatenate(
            [early[:, :cut], early[:, cut:] + late[:, :cut], late[:, cut:]], axis=1
        ).astype(BF16)

    d_query, d_key, d_value = [], [], []
    for half in range(2):
        starts = (half * width, (half + 1) * width - span)
        pieces = [
            (
                keys[:, c : c + span],
                values[:, c : c + span],
                stacked(queries[:, c : c + span], skip),
                stacked(grads[:, c : c + span], skip),
            )
            for skip, c in enumerate(starts)
        ]
        scores = [dot_nt(k, q) for k, v, q, g in pieces]
        weights_grads = [dot_nt(v, g) for k, v, q, g in pieces]
        weights_low, scores_grads = [], []
        for score, weights_grad in zip(scores, weights_grads):
            grown = jnp.exp2((score - jnp.max(score, axis=0, keepdims=True)) * EXPONENT)
            weights = grown * (1.0 / jnp.sum(grown, axis=0, keepdims=True))
            inner = jnp.sum(weights * weights_grad, axis=0, keepdims=True)
            weights_low.append(weights.astype(BF16))
            scores_grads.append((weights * (weights_grad - inner)).astype(BF16))
        d_value.append(joined(*[dot(w, p[3]) for w, p in zip(weights_low, pieces)]))
        d_key.append(joined(*[dot(w, p[2]) * factor for w, p in zip(scores_grads, pieces)]))
        d_query.append(
            joined(
                *[
                    unstacked(dot_tn(w, p[0]) * factor, skip)
                    for skip, (w, p) in enumerate(zip(scores_grads, pieces))
                ]
            )
        )
    own = jnp.concatenate([d_key[0], d_value[0]], axis=1)
    peer = jnp.concatenate([d_key[1], d_value[1]], axis=1)
    query_own, query_peer = d_query
    extra = (
        back_one[...]
        + dot_nt(query_own, qkv_all[0, :, :width])
        + dot_nt(query_peer, qkv_all[1, :, :width])
    ).astype(BF16)
    tokens_low[...] = (
        dot_nt(own, qkv_all[0, :, width:])
        + dot_nt(peer, qkv_all[1, :, width:])
        + dot_tn(picks[...], extra)
    ).astype(BF16)
    query_grads[pl.ds(pl.multiple_of(step * taken, taken), taken), :] = query_own
    sums[...] += dot_tn(tokens[...], own)
    vectors[8:9, :width] += row_sum(query_own.astype(F32))
    vectors[8:9, width:] += row_sum(own[:, width:].astype(F32))

    @pl.when(step == last)
    def _():
        grads_rest[:model, :] = sums[...].astype(BF16)
        query_total = dot_tn(picked_tokens[...], query_grads[...]).astype(BF16)
        for c in range(2):
            grads_rest[model : model + width, c * width : (c + 1) * width] = query_total[
                c * width : (c + 1) * width
            ]
        grads_rest[model + width : model + 2 * width, :] = grad_w_out[...]
        vectors[:8, :] = vectors_in[...]

        def rest(event, carry):
            reduction.event(event, range(FF_WAYS))
            return carry

        lax.fori_loop(last, chips, rest, 0)
        for way in range(FF_WAYS):
            reduced[way] = total[ring.rows(way, reduction.done_segment(way)), :]
        share.wait()


def attention_back(
    tokens,
    keys,
    values,
    queries,
    grads,
    back_one,
    picks,
    picked_tokens,
    qkv_all,
    grad_w_out,
    vectors,
    grad_ff,
    attended,
    late,
    sequences,
    chips,
):
    rows, model = tokens.shape
    length = rows // sequences
    width = keys.shape[1] // 2
    slots = queries.shape[0]
    taken = slots // sequences
    share = grad_ff.shape[0] // 2
    rest_rows = padded_rows(model + 2 * width, chips, 2)
    shape = jax.ShapeDtypeStruct

    def fixed(array_shape):
        return pl.BlockSpec(array_shape, lambda i: (0,) * len(array_shape))

    piece = (FF_WAYS, share // (FF_WAYS * chips), model)
    return pl.pallas_call(
        functools.partial(backward_body, chips),
        grid=(sequences,),
        in_specs=[rows_spec(length, model)]
        + [rows_spec(length, 2 * width)] * 2
        + [rows_spec(taken, 2 * width)] * 2
        + [rows_spec(taken, model), rows_spec(taken, length)]
        + [
            whole_spec(picked_tokens),
            pl.BlockSpec(qkv_all.shape, lambda i: (0, 0, 0), pipeline_mode=pl.Buffered(1)),
            whole_spec(grad_w_out),
            whole_spec(vectors),
            pl.BlockSpec(memory_space=pl.ANY),
            pl.BlockSpec(memory_space=pl.ANY),
        ],
        out_specs=[
            rows_spec(length, model),
            fixed((rest_rows, model)),
            fixed((16, model)),
            fixed(piece),
            pl.BlockSpec(memory_space=pl.ANY),
        ],
        out_shape=[
            shape((rows, model), BF16),
            shape((rest_rows, model), BF16),
            shape((16, model), F32),
            shape(piece, BF16),
            shape((late, width), BF16),
        ],
        scratch_shapes=[
            pltpu.VMEM((slots, width), BF16),
            pltpu.VMEM((model, 2 * width), F32),
            pltpu.VMEM((share, model), BF16),
            pltpu.VMEM((share, model), BF16),
            pltpu.VMEM((FF_WAYS, chips - 1) + piece[1:], BF16),
            pltpu.SemaphoreType.DMA((3,)),
            pltpu.SemaphoreType.DMA((2, FF_WAYS, chips - 1)),
            pltpu.SemaphoreType.DMA((2,)),
        ],
        compiler_params=pltpu.CompilerParams(
            vmem_limit_bytes=VMEM_BYTES, collective_id=1, has_side_effects=True
        ),
        cost_estimate=pl.CostEstimate(
            flops=int(rows * model * 4 * 2 * width),
            bytes_accessed=rows * model * 14,
            transcendentals=0,
        ),
        name="attention_back",
    )(
        tokens,
        keys,
        values,
        queries,
        grads,
        back_one,
        picks,
        picked_tokens,
        qkv_all,
        grad_w_out,
        vectors,
        grad_ff,
        attended,
    )


def padded_rows(rows, chips, ways):
    unit = 32 * ways * chips
    return -(-rows // unit) * unit


def finish_body(
    tokens_low,
    layer_in,
    up_left,
    up_right,
    down,
    key_value,
    query,
    out,
    vectors,
    tokens_grad,
    layer_out,
    grad_w_up,
    grad_w_down,
    grad_w_key,
    grad_w_value,
    grad_w_query,
    grad_w_out,
    grad_b_out,
    grad_gain_one,
    grad_shift_one,
    grad_b_down,
    grad_gain_two,
    grad_shift_two,
    grad_b_up,
    grad_b_query,
    grad_b_value,
):
    @pl.when(pl.program_id(0) == 0)
    def _():
        singles = (
            grad_b_out,
            grad_gain_one,
            grad_shift_one,
            grad_b_down,
            grad_gain_two,
            grad_shift_two,
        )
        for i, single in enumerate(singles):
            single[...] = vectors[i : i + 1, :].reshape(-1)
        grad_b_up[...] = jnp.concatenate([vectors[6:7, :], vectors[7:8, :]], axis=1).reshape(-1)
        grad_b_query[...] = vectors[8:9, : grad_b_query.shape[0]].reshape(-1)
        grad_b_value[...] = vectors[8:9, grad_b_query.shape[0] :].reshape(-1)

    width = grad_w_key.shape[1]
    model = tokens_grad.shape[1]
    tokens_grad[...] = tokens_low[...].astype(F32)
    layer_out[...] = layer_in[...]
    grad_w_up[:, :model] = up_left[...].astype(F32)
    grad_w_up[:, model:] = up_right[...].astype(F32)
    grad_w_down[...] = down[...].astype(F32)
    grad_w_key[...] = key_value[:, :width].astype(F32)
    grad_w_value[...] = key_value[:, width:].astype(F32)
    grad_w_query[...] = query[...].astype(F32)
    grad_w_out[...] = out[...].astype(F32)


def finish(
    tokens_low, layer, sums_ff, sums_rest, vectors, half, sequences
):
    rows, model = tokens_low.shape
    steps = sequences // 4
    length = rows // steps
    width = model // 2
    assert half == 2 * model and steps % 2 == 0
    part = model // steps
    shape = jax.ShapeDtypeStruct

    def block(count, columns, start, column=None):
        offset = start // count
        return pl.BlockSpec((count, columns), lambda i: (offset + i, 0))

    turns = steps // 2
    counts = [model] * 6 + [half, width, width]
    return pl.pallas_call(
        finish_body,
        grid=(steps,),
        in_specs=[
            rows_spec(length, model),
            rows_spec(length, model),
            block(part, model, 0),
            block(part, model, model),
            block(2 * part, model, half),
            block(part, model, 0),
            pl.BlockSpec((part, width), lambda i: (model // part + i % turns, i // turns)),
            block(width // steps, model, model + width),
            whole_spec(vectors),
        ],
        out_specs=[
            rows_spec(length, model),
            rows_spec(length, model),
            rows_spec(part, half),
            rows_spec(2 * part, model),
            rows_spec(part, width),
            rows_spec(part, width),
            rows_spec(part, width),
            rows_spec(width // steps, model),
        ]
        + [pl.BlockSpec((count,), lambda i: (0,)) for count in counts],
        out_shape=[
            shape((rows, model), F32),
            shape((rows, model), BF16),
            shape((model, half), F32),
            shape((half, model), F32),
            shape((model, width), F32),
            shape((model, width), F32),
            shape((model, width), F32),
            shape((width, model), F32),
        ]
        + [shape((count,), F32) for count in counts],
        compiler_params=params(),
        cost_estimate=pl.CostEstimate(
            flops=int(rows * model * 4 * 2 * width),
            bytes_accessed=rows * model * 16,
            transcendentals=0,
        ),
        name="finish",
    )(
        tokens_low,
        layer,
        sums_ff,
        sums_ff,
        sums_ff,
        sums_rest,
        sums_rest,
        sums_rest,
        vectors,
    )


def dense_body(
    chips,
    levels,
    early,
    tokens,
    attended_own,
    attended_local,
    attended_early,
    attended_late,
    w_out,
    w_up_own,
    w_up_peer,
    w_down_own,
    w_down_peer,
    b_up_peer,
    b_up,
    b_out,
    gain_one,
    shift_one,
    b_down,
    gain_two,
    shift_two,
    reduced,
    grads_rest,
    vectors_in,
    layer_out,
    sums_ff,
    sums_rest,
    vectors,
    total,
    other,
    slots,
    last_pieces,
    held_ff,
    held_rest,
    exchanged,
    gained,
    core_sems,
    ring_sems,
    ff_keep_sems,
    ff_sems,
    ff_mate_sems,
    rest_keep_sems,
    rest_sems,
    rest_mate_sems,
    vector_sems,
):
    step = pl.program_id(0)
    steps = pl.num_programs(0)
    model = tokens.shape[1]
    dp = lax.axis_index("dp")
    ring = Ring(chips, total.shape[0], 2)
    ff_ring = Ring(chips, sums_ff.shape[0] // 2, FF_WAYS)
    reduction = Reduce(ring, grads_rest, total, other, slots, core_sems, ring_sems)
    gather_ff = Gather(
        ff_ring,
        reduced,
        held_ff,
        sums_ff,
        ff_keep_sems,
        ff_sems,
        ff_mate_sems,
    )
    gather_rest = Gather(
        ring,
        last_pieces,
        held_rest,
        sums_rest,
        rest_keep_sems,
        rest_sems,
        rest_mate_sems,
    )

    def exchange(level):
        return remote(
            exchanged.at[level],
            gained.at[level],
            vector_sems.at[0, level],
            vector_sems.at[1, level],
            {"dp": flipped(dp, 2**level)},
        )

    def vector_event(level):
        if level > 0:
            exchange(level - 1).wait()
            exchanged[level] = exchanged[level - 1] + gained[level - 1]
        if level < levels:
            exchange(level).start()
        else:
            vectors[...] = exchanged[level]

    def rest_event(event, way):
        @pl.when(event < chips)
        def _():
            reduction.event(event, (way,))

        @pl.when(event == chips - 1)
        def _():
            last_pieces[way] = total[ring.rows(way, reduction.done_segment(way)), :]
            gather_rest.begin((way,))

        @pl.when(event > chips - 1)
        def _():
            gather_rest.event(event - (chips - 1), (way,))

    def point(index):
        def small():
            for way in range(2):
                rest_event(2 * step - 1 + index, way)

        if index == 0:
            pl.when(step > 0)(small)
        else:
            small()

        @pl.when((step > 0) & (step < chips))
        def _():
            gather_ff.event(step, (2 * index, 2 * index + 1))

    @pl.when(step == 0)
    def _():
        greet(ring.neighbours() + tuple({"dp": flipped(dp, 2**level)} for level in range(1, levels)))
        reduction.begin()
        gather_ff.begin(range(FF_WAYS))
        exchanged[0] = vectors_in[...]
        vector_event(0)

    point(0)

    for level in range(1, levels + 1):

        @pl.when(step == jnp.minimum(level, steps - 1))
        def _():
            vector_event(level)

    count = tokens.shape[0] // 2
    split = (slice(0, count), slice(count, 2 * count))

    def first_norm(r):
        attended_peer = jnp.where(
            step < LOCAL,
            attended_local[r, :],
            jnp.where(step < LOCAL + early, attended_early[r, :], attended_late[r, :]),
        )
        attended = jnp.concatenate([attended_own[r, :], attended_peer], axis=1)
        normed, _ = norm_parts(tokens[r, :].astype(F32) + dot(attended, w_out[...]) + row(b_out))
        return normed * row(gain_one) + row(shift_one)

    def forward(layer_low, w_up, w_down, bias):
        hidden = dot(layer_low, w_up[...]) + bias
        return dot((hidden * gelu_share(hidden)).astype(BF16), w_down[...])

    layers = [first_norm(r) for r in split]
    lows = [layer.astype(BF16) for layer in layers]
    sums = [layer + row(b_down) for layer in layers]
    sums[0] = sums[0] + forward(lows[0], w_up_own, w_down_own, row(b_up))
    sums[1] = sums[1] + forward(lows[1], w_up_own, w_down_own, row(b_up))

    @pl.when(step == 0)
    def _():
        reduction.join()

    point(1)
    sums[0] = sums[0] + forward(lows[0], w_up_peer, w_down_peer, b_up_peer[...])
    sums[1] = sums[1] + forward(lows[1], w_up_peer, w_down_peer, b_up_peer[...])
    for r, summed in zip(split, sums):
        normed, _ = norm_parts(summed)
        layer_out[r, :] = (normed * row(gain_two) + row(shift_two)).astype(BF16)

    @pl.when(step == steps - 1)
    def _():
        def more_ff(event, carry):
            gather_ff.event(event, range(FF_WAYS))
            return carry

        def more_rest(event, carry):
            rest_event(event, 0)
            rest_event(event, 1)
            return carry

        lax.fori_loop(steps, chips, more_ff, 0)
        lax.fori_loop(2 * steps - 1, 2 * chips - 1, more_rest, 0)
        gather_ff.finish()
        gather_rest.finish()


def dense_rows(
    tokens,
    attended_own,
    attended_local,
    attended_early,
    attended_late,
    w_out,
    w_up_own,
    w_up_peer,
    w_down_own,
    w_down_peer,
    b_up_peer,
    singles,
    reduced,
    grads_rest,
    vectors,
    sequences,
    chips,
):
    rows, model = tokens.shape
    half = w_up_own.shape[1]
    block = rows // sequences
    levels = (2 * chips).bit_length() - 1
    assert 2**levels == 2 * chips
    share = grads_rest.shape[0] // 2
    ff_rows = reduced.shape[0] * reduced.shape[1] * 2 * chips
    piece = (share // (2 * chips), model)
    shape = jax.ShapeDtypeStruct
    anywhere = pl.BlockSpec(memory_space=pl.ANY)
    arrays = (w_out, w_up_own, w_up_peer, w_down_own, w_down_peer, b_up_peer)
    early = attended_early.shape[0] // block
    late = attended_late.shape[0] // block
    dma = pltpu.SemaphoreType.DMA
    return pl.pallas_call(
        functools.partial(dense_body, chips, levels, early),
        grid=(sequences,),
        in_specs=[
            rows_spec(block, model),
            rows_spec(block, model // 2),
            pl.BlockSpec((block, model // 2), lambda i: (jnp.minimum(i, LOCAL - 1), 0)),
            pl.BlockSpec((block, model // 2), lambda i: (jnp.clip(i - LOCAL, 0, early - 1), 0)),
            pl.BlockSpec(
                (block, model // 2), lambda i: (jnp.clip(i - LOCAL - early, 0, late - 1), 0)
            ),
        ]
        + [whole_spec(array) for array in arrays]
        + [vector_spec(array) for array in singles]
        + [
            pl.BlockSpec(reduced.shape, lambda i: (0, 0, 0), pipeline_mode=pl.Buffered(1)),
            anywhere,
            whole_spec(vectors),
        ],
        out_specs=[
            rows_spec(block, model),
            anywhere,
            anywhere,
            pl.BlockSpec(vectors.shape, lambda i: (0, 0)),
        ],
        out_shape=[
            shape((rows, model), BF16),
            shape((ff_rows, model), BF16),
            shape(grads_rest.shape, BF16),
            shape(vectors.shape, F32),
        ],
        scratch_shapes=[
            pltpu.VMEM((share, model), BF16),
            pltpu.VMEM((share, model), BF16),
            pltpu.VMEM((2, chips - 1) + piece, BF16),
            pltpu.VMEM((2,) + piece, BF16),
            pltpu.VMEM((ff_rows, model), BF16),
            pltpu.VMEM(grads_rest.shape, BF16),
            pltpu.VMEM((levels + 1,) + vectors.shape, F32),
            pltpu.VMEM((levels,) + vectors.shape, F32),
            dma((3,)),
            dma((2, 2, chips - 1)),
            dma((2, FF_WAYS, chips)),
            dma((2, FF_WAYS, chips - 1)),
            dma((2, FF_WAYS, chips)),
            dma((2, 2, chips)),
            dma((2, 2, chips - 1)),
            dma((2, 2, chips)),
            dma((2, levels)),
        ],
        compiler_params=pltpu.CompilerParams(
            vmem_limit_bytes=VMEM_BYTES, collective_id=2, has_side_effects=True
        ),
        cost_estimate=pl.CostEstimate(
            flops=int(rows * model * (8 * half + 2 * model)),
            bytes_accessed=rows * model * 6,
            transcendentals=rows * half * 2,
        ),
        name="dense",
    )(
        tokens,
        attended_own,
        attended_local,
        attended_early,
        attended_late,
        *arrays,
        *singles,
        reduced,
        grads_rest,
        vectors,
    )


def on_device(
    chips,
    tokens,
    out_grad,
    positions,
    w_query,
    b_query,
    w_key,
    w_value,
    b_value,
    w_out,
    b_out,
    gain_one,
    shift_one,
    w_up,
    b_up,
    w_down,
    b_down,
    gain_two,
    shift_two,
):
    sequences, count = positions.shape
    half = w_up.shape[1]
    taken = -(-count // 16) * 16
    (
        attended,
        attended_local,
        keys,
        values,
        picked_q,
        picked_tokens,
        picked_grad,
        picks,
        picked_att,
        qkv_all,
        out_all,
        up_peer,
        down_peer,
        b_up_peer,
    ) = attention(
        tokens,
        out_grad,
        positions,
        w_query,
        w_key,
        w_value,
        w_out,
        w_up,
        w_down,
        b_query,
        b_value,
        b_up,
        taken,
    )
    length = tokens.shape[0] // sequences
    early = (sequences - LOCAL) // 3 * length
    late = tokens.shape[0] - LOCAL * length - early
    weights = (out_all, w_up, up_peer, w_down, down_peer, b_up_peer)
    singles = (b_up, b_out, gain_one, shift_one, b_down, gain_two)
    back_one, att_grad, grad_ff, grad_w_out, vectors, attended_early = marked_rows(
        picked_tokens, picked_att, picked_grad, *weights, singles, attended, early, late, chips
    )
    tokens_low, grads_rest, vectors, reduced, attended_late = attention_back(
        tokens,
        keys,
        values,
        picked_q,
        att_grad,
        back_one,
        picks,
        picked_tokens,
        qkv_all,
        grad_w_out,
        vectors,
        grad_ff,
        attended,
        late,
        sequences,
        chips,
    )
    layer, sums_ff, sums_rest, vectors = dense_rows(
        tokens,
        attended,
        attended_local,
        attended_early,
        attended_late,
        *weights,
        singles + (shift_two,),
        reduced,
        grads_rest,
        vectors,
        sequences,
        chips,
    )
    (
        tokens_grad,
        layer_out,
        grad_w_up,
        grad_w_down,
        grad_w_key,
        grad_w_value,
        grad_w_query,
        grad_w_out,
        grad_b_out,
        grad_gain_one,
        grad_shift_one,
        grad_b_down,
        grad_gain_two,
        grad_shift_two,
        grad_b_up,
        grad_b_query,
        grad_b_value,
    ) = finish(
        tokens_low, layer, sums_ff, sums_rest, vectors, half, sequences
    )
    return (
        layer_out,
        tokens_grad,
        grad_w_query,
        grad_b_query,
        grad_w_key,
        grad_w_value,
        grad_b_value,
        grad_w_out,
        grad_b_out,
        grad_gain_one,
        grad_shift_one,
        grad_w_up,
        grad_b_up,
        grad_w_down,
        grad_b_down,
        grad_gain_two,
        grad_shift_two,
    )


def solution(mesh):
    across = P("dp", None)
    columns, rows, split, copied = P(None, "tensor"), P("tensor", None), P("tensor"), P()
    in_specs = (
        across,
        across,
        across,
        columns,
        split,
        columns,
        columns,
        split,
        rows,
        copied,
        copied,
        copied,
        columns,
        split,
        rows,
        copied,
        copied,
        copied,
    )
    out_specs = (
        across,
        across,
        columns,
        split,
        columns,
        columns,
        split,
        rows,
        copied,
        copied,
        copied,
        columns,
        split,
        rows,
        copied,
        copied,
        copied,
    )
    return jax.shard_map(
        functools.partial(on_device, mesh.shape["dp"] // 2), mesh=mesh, in_specs=in_specs, out_specs=out_specs, check_vma=False
    )
```
